128 devices in a mesh: dp: 16 (over z, x), pipe: 2 (over core), tensor: 4 (over y).
Axes of the slice: x: 4, y: 4, z: 4, core: 2. Of those that a mesh axis runs over, the one named last changes fastest.
Arguments:
- patches: bfloat16 [4096, 192], P(('dp', 'pipe')), may hold values from -6 to 6
- item_lengths: int32 [32, 3], P('dp'), may hold values from 1 to 96, 128 in all within a row
- cotangent: bfloat16 [4096, 1024], P(('dp', 'pipe')), may hold values from -6 to 6
- patch_weight: bfloat16 [48, 4, 1024], replicated, may hold values from -3 to 3
- var_embed: bfloat16 [48, 1024], replicated, may hold values from -6 to 6
- agg_query: bfloat16 [1024], replicated, may hold values from -6 to 6
- agg_wq: bfloat16 [1024, 1024], P(None, 'tensor'), may hold values from -0.1875 to 0.1875
- agg_wk: bfloat16 [1024, 1024], P(None, 'tensor'), may hold values from -0.1875 to 0.1875
- agg_wv: bfloat16 [1024, 1024], P(None, 'tensor'), may hold values from -0.1875 to 0.1875
- agg_wo: bfloat16 [1024, 1024], P('tensor'), may hold values from -0.75 to 0.75
- agg_bias: bfloat16 [1024], P('tensor'), may hold values from -3 to 3
- pos_table: bfloat16 [96, 1024], P(None, 'tensor'), may hold values from -3 to 3
- first_gain: bfloat16 [1024], replicated, may hold values from 0.5 to 1.5
- first_shift: bfloat16 [1024], replicated, may hold values from -2 to 2
- attn_qkv: bfloat16 [1024, 3, 1024], P(None, None, 'tensor'), may hold values from -0.1875 to 0.1875
- attn_out: bfloat16 [1024, 1024], P('tensor'), may hold values from -0.75 to 0.75
- attn_bias: bfloat16 [1024], replicated, may hold values from -2 to 2
- second_gain: bfloat16 [1024], replicated, may hold values from 0.5 to 1.5
- second_shift: bfloat16 [1024], replicated, may hold values from -2 to 2
- mlp_up: bfloat16 [1024, 4096], P(None, 'tensor'), may hold values from -0.1875 to 0.1875
- up_bias: bfloat16 [4096], P('tensor'), may hold values from -3 to 3
- mlp_down: bfloat16 [4096, 1024], P('tensor'), may hold values from -0.09375 to 0.09375
- down_bias: bfloat16 [1024], replicated, may hold values from -2 to 2
Outputs:
- block_out: bfloat16 [4096, 1024], P(('dp', 'pipe'), 'tensor')
- patch_grad: float32 [4096, 192], P(('dp', 'pipe'), 'tensor')
- grad_patch_weight: float32 [48, 4, 1024], P(None, None, 'tensor')
- grad_var_embed: float32 [48, 1024], P(None, 'tensor')
- grad_agg_query: float32 [1024], P('tensor')
- grad_agg_wq: float32 [1024, 1024], P(None, 'tensor')
- grad_agg_wk: float32 [1024, 1024], P(None, 'tensor')
- grad_agg_wv: float32 [1024, 1024], P(None, 'tensor')
- grad_agg_wo: float32 [1024, 1024], P('tensor')
- grad_agg_bias: float32 [1024], P('tensor')
- grad_pos_table: float32 [96, 1024], P(None, 'tensor')
- grad_first_gain: float32 [1024], P('tensor')
- grad_first_shift: float32 [1024], P('tensor')
- grad_attn_qkv: float32 [1024, 3, 1024], P(None, None, 'tensor')
- grad_attn_out: float32 [1024, 1024], P('tensor')
- grad_attn_bias: float32 [1024], P('tensor')
- grad_second_gain: float32 [1024], P('tensor')
- grad_second_shift: float32 [1024], P('tensor')
- grad_mlp_up: float32 [1024, 4096], P(None, 'tensor')
- grad_up_bias: float32 [4096], P('tensor')
- grad_mlp_down: float32 [4096, 1024], P('tensor')
- grad_down_bias: float32 [1024], P('tensor')
The draws below stay inside these ranges and needn't reach their ends.
Inputs may be any that keep to these rules, and one draw needn't show every extreme that they name: `item_lengths`: each row holds the lengths of the 3 items of one micro-batch; a row sums to 128, and its longest item has 96 patches.
All inputs are finite; a program needn't handle non-finite values.
Results may differ from the reference program's by a relative error of at most 0.024.
Values may be sent and summed in bfloat16 or wider, within the bound.
A program may use at most 384 MiB of HBM per device.

```python
import math
from functools import partial
import jax
import jax.numpy as jnp
import numpy as np
from jax import lax

D = 1024
HEADS = 16
HEAD_DIM = 64
FF = 4096
VARS = 48
PATCH = 4
TOK_MB = 128
MICRO = 2
ITEMS = 3
LONGEST = 96
VP = 192
TOKENS = 4096
N_DP = 16


def level_of(own_key, shape, pieces, smallest, largest):
    def one(axis_at, parts):
        draws = jax.random.uniform(jax.random.fold_in(jax.random.fold_in(own_key, 6), axis_at), (parts,), jnp.float32, smallest / len(pieces), largest / len(pieces))
        return jnp.repeat(jnp.exp(draws), shape[axis_at] // parts).reshape((-1,) + (1,) * (len(shape) - axis_at - 1))

    factor_of = one(*pieces[0])
    for cut in pieces[1:]:
        factor_of = factor_of * one(*cut)
    return factor_of


def profile(amount, total, reach, lean):
    portions = [(1 << 20) // math.isqrt(grade ** lean) + 1 for grade in range(2, amount + 1)]
    rest, counts = total - reach - (amount - 1), [1] * (amount - 1)
    while rest > 0:
        candidates = [i for i in range(amount - 1) if counts[i] < reach]
        mass, left = sum([portions[i] for i in candidates]), rest
        for i in candidates:
            addition = min(reach - counts[i], max(1, left * portions[i] // mass), rest)
            counts[i] = counts[i] + addition
            rest = rest - addition
    return np.array([reach] + counts)


def uneven_parts(own_key, count, total, limit, slope):
    if count == 2:
        one = jax.random.randint(own_key, (), max(1, total - limit), min(limit, total - 1) + 1)
        return jnp.stack([one, total - one])
    sizes = jnp.asarray(profile(count, total, limit, slope), jnp.int32)
    couples = (count - 1) // 2
    donor, sink = sizes[1:1 + 2 * couples:2], sizes[2:2 + 2 * couples:2]
    slack = jnp.minimum(donor - 1, limit - sink)
    moved = jax.random.randint(jax.random.fold_in(own_key, 1), (couples,), 0, 1 << 20) % (slack + 1)
    sizes = sizes.at[1:1 + 2 * couples:2].set(donor - moved).at[2:2 + 2 * couples:2].set(sink + moved)
    return sizes[jax.random.permutation(jax.random.fold_in(own_key, 2), count)]


def normal_values(key, dims, scale, reach, pieces=(), held_as=jnp.bfloat16):
    level = level_of(key, dims, pieces, -0.22, 0.18) if pieces else 1.0
    result = jax.random.normal(key, dims, jnp.float32) * scale * level
    return jnp.minimum(jnp.maximum(result, -reach), reach).astype(held_as)


def setup_inputs(seed: int = 0) -> dict:
    key_of = jax.random.split(jax.random.key(seed), 24)
    patches = normal_values(key_of[0], (TOKENS, VP), 1.0, 6.0, ((0, 32),))
    item_lengths = jax.vmap(lambda own: uneven_parts(own, ITEMS, TOK_MB, LONGEST, 2))(jax.random.split(key_of[1], (N_DP * MICRO))).reshape((N_DP * MICRO, ITEMS)).astype(jnp.int32)
    cotangent = normal_values(key_of[2], (TOKENS, D), 1.0, 6.0, ((0, 32),))
    patch_weight = normal_values(key_of[3], (VARS, PATCH, D), PATCH ** -0.5, 3.0)
    var_embed = normal_values(key_of[4], (VARS, D), 1.0, 6.0)
    agg_query = normal_values(key_of[5], (D,), 1.0, 6.0)
    agg_wq = normal_values(key_of[6], (D, D), D ** -0.5, 0.1875, ((1, 4),))
    agg_wk = normal_values(key_of[7], (D, D), D ** -0.5, 0.1875, ((1, 4),))
    agg_wv = normal_values(key_of[8], (D, D), D ** -0.5, 0.1875, ((1, 4),))
    agg_wo = normal_values(key_of[9], (D, D), (D // 16) ** -0.5, 0.75, ((0, 4),))
    agg_bias = normal_values(key_of[10], (D,), 0.5, 3.0, ((0, 4),))
    pos_table = normal_values(key_of[11], (LONGEST, D), 0.5, 3.0, ((1, 4),))
    first_gain = jnp.clip(1.0 + 0.1 * jax.random.normal(key_of[12], (D,), jnp.float32), 0.5, 1.5).astype(jnp.bfloat16)
    first_shift = normal_values(key_of[13], (D,), 0.3, 2.0)
    attn_qkv = normal_values(key_of[14], (D, 3, D), D ** -0.5, 0.1875, ((2, 4),))
    attn_out = normal_values(key_of[15], (D, D), (D // 16) ** -0.5, 0.75, ((0, 4),))
    attn_bias = normal_values(key_of[16], (D,), 0.3, 2.0)
    second_gain = jnp.clip(1.0 + 0.1 * jax.random.normal(key_of[17], (D,), jnp.float32), 0.5, 1.5).astype(jnp.bfloat16)
    second_shift = normal_values(key_of[18], (D,), 0.3, 2.0)
    mlp_up = normal_values(key_of[19], (D, FF), D ** -0.5, 0.1875, ((1, 4),))
    up_bias = normal_values(key_of[20], (FF,), 0.5, 3.0, ((0, 4),))
    mlp_down = normal_values(key_of[21], (FF, D), FF ** -0.5, 0.09375, ((0, 4),))
    down_bias = normal_values(key_of[22], (D,), 0.3, 2.0)
    return {"patches": patches, "item_lengths": item_lengths, "cotangent": cotangent, "patch_weight": patch_weight, "var_embed": var_embed, "agg_query": agg_query, "agg_wq": agg_wq, "agg_wk": agg_wk, "agg_wv": agg_wv, "agg_wo": agg_wo, "agg_bias": agg_bias, "pos_table": pos_table, "first_gain": first_gain, "first_shift": first_shift, "attn_qkv": attn_qkv, "attn_out": attn_out, "attn_bias": attn_bias, "second_gain": second_gain, "second_shift": second_shift, "mlp_up": mlp_up, "up_bias": up_bias, "mlp_down": mlp_down, "down_bias": down_bias}


@jax.custom_vjp
def low(v):
    return lax.optimization_barrier(v.astype(jnp.bfloat16)).astype(jnp.float32)

@jax.custom_vjp
def low_back(v):
    return v

def low_keep(v):
    return (low(v), None)

def low_pass(kept, grad):
    return (grad,)

def back_keep(v):
    return (v, None)

def back_low(kept, grad):
    return (low(grad),)
low.defvjp(low_keep, low_pass)
low_back.defvjp(back_keep, back_low)
highest = lax.Precision.HIGHEST
norm_eps = 1e-05

def both_round(value):
    return low_back(low(value))

def layer_norm(inputs, gain_vec, shift_vec):
    centred = inputs - lax.optimization_barrier(jnp.mean(inputs, axis=-1, keepdims=True))
    variance = lax.optimization_barrier(jnp.mean(centred * centred, axis=-1, keepdims=True))
    return centred * lax.rsqrt(variance + norm_eps) * gain_vec + shift_vec

def locate(lengths_row, row_count):
    item_ends = jnp.cumsum(lengths_row).astype(jnp.int32)
    row_index = jnp.arange(row_count, dtype=jnp.int32)
    passed = (row_index[:, None] >= item_ends[None, :]).astype(jnp.int32)
    segment = lax.optimization_barrier(jnp.sum(passed, axis=1)).astype(jnp.int32)
    offset = lax.optimization_barrier(jnp.sum(passed * lengths_row[None, :], axis=1)).astype(jnp.int32)
    return (segment, row_index - offset)

def micro_batch(params, patch_rows, segment, position):
    patch_weight, var_embed, agg_query, agg_wq, agg_wk, agg_wv, agg_wo, agg_bias, pos_table, first_gain, first_shift, attn_qkv, attn_out, attn_bias, second_gain, second_shift, mlp_up, up_bias, mlp_down, down_bias = params
    row_count = patch_rows.shape[0]
    score_scale = HEAD_DIM ** (-0.5)
    patch_view = patch_rows.reshape(row_count, VARS, PATCH)
    embedded = low(jnp.einsum('tvp,vpd->tvd', patch_view, patch_weight, precision=highest) + var_embed[None])
    query_vec = low(jnp.dot(agg_query, agg_wq, precision=highest)).reshape(HEADS, HEAD_DIM)
    key_rows = both_round(jnp.einsum('tvd,de->tve', embedded, agg_wk, precision=highest)).reshape(row_count, VARS, HEADS, HEAD_DIM)
    value_rows = both_round(jnp.einsum('tvd,de->tve', embedded, agg_wv, precision=highest)).reshape(row_count, VARS, HEADS, HEAD_DIM)
    var_scores = jnp.einsum('tvhc,hc->tvh', key_rows, query_vec, precision=highest) * score_scale
    var_weights = jax.nn.softmax(var_scores, axis=1)
    mixed_heads = low(jnp.einsum('tvh,tvhc->thc', var_weights, value_rows, precision=highest).reshape(row_count, D))
    onehot = (position[:, None] == jnp.arange(LONGEST, dtype=jnp.int32)[None, :]).astype(jnp.float32)
    stream = both_round(jnp.dot(mixed_heads, agg_wo, precision=highest) + agg_bias + jnp.dot(onehot, pos_table, precision=highest))
    normed = low(layer_norm(stream, first_gain, first_shift))
    projected = jnp.einsum('td,dke->tke', normed, attn_qkv, precision=highest)
    queries = both_round(projected[:, 0]).reshape(row_count, HEADS, HEAD_DIM)
    key_heads = both_round(projected[:, 1]).reshape(row_count, HEADS, HEAD_DIM)
    value_heads = both_round(projected[:, 2]).reshape(row_count, HEADS, HEAD_DIM)
    raw_scores = low_back(jnp.einsum('qhc,khc->hqk', queries, key_heads, precision=highest) * score_scale)
    same_item = (segment[:, None] == segment[None, :])[None]
    probs = low(jax.nn.softmax(jnp.where(same_item, raw_scores, -1e+30), axis=-1))
    attended = both_round(jnp.einsum('hqk,khc->qhc', probs, value_heads, precision=highest).reshape(row_count, D))
    residual = low_back(stream + jnp.dot(attended, attn_out, precision=highest) + attn_bias)
    normed_two = low(layer_norm(residual, second_gain, second_shift))
    pre_act = low_back(jnp.dot(normed_two, mlp_up, precision=highest) + up_bias)
    active = low(jax.nn.gelu(pre_act, approximate=False))
    return residual + jnp.dot(active, mlp_down, precision=highest) + down_bias

def reference(patches, item_lengths, cotangent, patch_weight, var_embed, agg_query, agg_wq, agg_wk, agg_wv, agg_wo, agg_bias, pos_table, first_gain, first_shift, attn_qkv, attn_out, attn_bias, second_gain, second_shift, mlp_up, up_bias, mlp_down, down_bias):
    params = (patch_weight.astype(jnp.float32), var_embed.astype(jnp.float32), agg_query.astype(jnp.float32), agg_wq.astype(jnp.float32), agg_wk.astype(jnp.float32), agg_wv.astype(jnp.float32), agg_wo.astype(jnp.float32), agg_bias.astype(jnp.float32), pos_table.astype(jnp.float32), first_gain.astype(jnp.float32), first_shift.astype(jnp.float32), attn_qkv.astype(jnp.float32), attn_out.astype(jnp.float32), attn_bias.astype(jnp.float32), second_gain.astype(jnp.float32), second_shift.astype(jnp.float32), mlp_up.astype(jnp.float32), up_bias.astype(jnp.float32), mlp_down.astype(jnp.float32), down_bias.astype(jnp.float32))
    blocks = N_DP * MICRO
    segments, positions = jax.vmap(partial(locate, row_count=TOK_MB))(item_lengths)

    def forward(patch_all, weights):
        patch_blocks = patch_all.reshape(blocks, TOK_MB, VARS * PATCH)

        def one_block(inputs):
            return micro_batch(weights, inputs[0], inputs[1], inputs[2])
        outputs = lax.map(jax.checkpoint(one_block), (patch_blocks, segments, positions))
        return outputs.reshape(blocks * TOK_MB, D)
    outputs, pullback = jax.vjp(forward, patches.astype(jnp.float32), params)
    grad_patches, grad_params = pullback(cotangent.astype(jnp.float32))
    return (outputs.astype(jnp.bfloat16), grad_patches, grad_params[0], grad_params[1], grad_params[2], grad_params[3], grad_params[4], grad_params[5], grad_params[6], grad_params[7], grad_params[8], grad_params[9], grad_params[10], grad_params[11], grad_params[12], grad_params[13], grad_params[14], grad_params[15], grad_params[16], grad_params[17], grad_params[18], grad_params[19])
```

```python
import jax
import jax.numpy as jnp
from jax import lax
from jax.sharding import PartitionSpec as P

D = 1024
HEADS = 16
HEAD_DIM = 64
VARS = 48
PATCH = 4
LONGEST = 96
TERMS = PATCH + 1

norm_eps = 1e-05
root_half = 0.7071067811865476
inv_root_tau = 0.3989422804014327
highest = lax.Precision.HIGHEST
score_scale = HEAD_DIM ** (-0.5)
f32 = jnp.float32
bf16 = jnp.bfloat16


def dot(left, right, dims, precision=None):
    return lax.dot_general(left, right, (dims, ((), ())), precision=precision, preferred_element_type=f32)


def mm(a, b, **kw):
    return dot(a, b, ((1,), (0,)), **kw)


def mm_nt(a, b, **kw):
    return dot(a, b, ((1,), (1,)), **kw)


def mm_tn(a, b, **kw):
    return dot(a, b, ((0,), (0,)), **kw)


def locate(lengths_row, row_count):
    item_ends = jnp.cumsum(lengths_row)
    row_index = jnp.arange(row_count, dtype=jnp.int32)
    passed = (row_index[:, None] >= item_ends[None, :]).astype(jnp.int32)
    segment = jnp.sum(passed, axis=1)
    offset = jnp.sum(passed * lengths_row[None, :], axis=1)
    return (segment, row_index - offset)


def norm_parts(x):
    centred = x - jnp.mean(x, axis=-1, keepdims=True)
    inverse = lax.rsqrt(jnp.mean(centred * centred, axis=-1, keepdims=True) + norm_eps)
    return centred * inverse, inverse


def norm_back(grad, xhat, inverse, gain):
    scaled = grad * gain
    return inverse * (
        scaled
        - jnp.mean(scaled, axis=-1, keepdims=True)
        - xhat * jnp.mean(scaled * xhat, axis=-1, keepdims=True)
    )


def shards(
    patches, item_lengths, cotangent, patch_weight, var_embed, agg_query, agg_wq, agg_wk, agg_wv,
    agg_wo, agg_bias, pos_table, first_gain, first_shift, attn_qkv, attn_out, attn_bias,
    second_gain, second_shift, mlp_up, up_bias, mlp_down, down_bias,
):
    rows = patches.shape[0]
    cols = agg_wq.shape[1]
    heads = cols // HEAD_DIM
    own = lax.axis_index("tensor")
    pipe = lax.axis_index("pipe")
    own_start = own * cols
    lengths = lax.dynamic_index_in_dim(item_lengths, pipe, 0, keepdims=False)
    segment, position = locate(lengths, rows)
    wide = lambda v: v.astype(f32)

    def psum_y(v):
        return wide(lax.psum(v.astype(bf16), "tensor"))

    terms = jnp.concatenate([patch_weight, var_embed[:, None, :]], axis=1).reshape(VARS * TERMS, D)
    spread = jnp.concatenate(
        [patches.reshape(rows, VARS, PATCH), jnp.ones((rows, VARS, 1), bf16)], axis=2
    )
    values = wide(spread)
    query = mm(agg_query[None, :], agg_wq).astype(bf16).reshape(heads, HEAD_DIM)
    block = jnp.where(
        (jnp.arange(cols) // HEAD_DIM)[None, :] == jnp.arange(heads)[:, None],
        query.reshape(1, cols), 0.0,
    ).astype(bf16)
    key_dir = mm_nt(block, agg_wk) * score_scale
    key_terms = mm_nt(key_dir, wide(terms), precision=highest).reshape(heads, VARS, TERMS)
    value_terms = mm(terms, agg_wv).astype(bf16).reshape(VARS * TERMS, heads, HEAD_DIM)
    scores = jnp.einsum("tvp,hvp->htv", values, key_terms, precision=highest)
    raised = jnp.exp(scores - jnp.max(scores, axis=-1, keepdims=True))
    weights = raised / jnp.sum(raised, axis=-1, keepdims=True)
    shares = (weights[..., None] * values[None]).astype(bf16).reshape(heads, rows, VARS * TERMS)
    mixed = jnp.einsum("htk,khc->thc", shares, value_terms, preferred_element_type=f32)
    mixed = mixed.reshape(rows, cols).astype(bf16)
    onehot = (position[:, None] == jnp.arange(LONGEST, dtype=jnp.int32)[None, :]).astype(bf16)
    extra = wide(agg_bias)[None, :] + mm(onehot, pos_table)
    placed = jnp.where((jnp.arange(D // cols) == own)[None, :, None], extra[:, None, :], 0.0)
    stream = psum_y(mm(mixed, agg_wo) + placed.reshape(rows, D))

    xhat_one, inverse_one = norm_parts(stream)
    normed = (xhat_one * wide(first_gain) + wide(first_shift)).astype(bf16)
    projected = jnp.einsum("td,dke->kte", normed, attn_qkv, preferred_element_type=f32).astype(bf16)
    q, k, v = [projected[j].reshape(rows, heads, HEAD_DIM) for j in range(3)]
    raw = jnp.einsum("qhc,khc->hqk", q, k, preferred_element_type=f32) * score_scale
    raw = jnp.where((segment[:, None] == segment[None, :])[None], raw, -1e30)
    raised = jnp.exp(raw - jnp.max(raw, axis=-1, keepdims=True))
    probs = raised / jnp.sum(raised, axis=-1, keepdims=True)
    probs_low = probs.astype(bf16)
    attended = jnp.einsum("hqk,khc->qhc", probs_low, v, preferred_element_type=f32)
    attended = attended.reshape(rows, cols).astype(bf16)
    resid = stream + psum_y(mm(attended, attn_out)) + wide(attn_bias)
    xhat_two, inverse_two = norm_parts(resid)
    normed_two = (xhat_two * wide(second_gain) + wide(second_shift)).astype(bf16)
    pre = mm(normed_two, mlp_up) + wide(up_bias)
    half_cdf = 0.5 * (1.0 + lax.erf(pre * root_half))
    active = (pre * half_cdf).astype(bf16)
    slope = half_cdf + pre * jnp.exp(-0.5 * pre * pre) * inv_root_tau

    def own_cols(a):
        return lax.dynamic_slice_in_dim(a, own_start, cols, a.ndim - 1)

    mlp_sum = wide(
        lax.psum_scatter(mm(active, mlp_down).astype(bf16), "tensor", scatter_dimension=1, tiled=True)
    )
    block_out = (own_cols(resid) + mlp_sum + wide(own_cols(down_bias))).astype(bf16)

    dy = wide(cotangent)
    g_down = mm_tn(active, cotangent)
    g_down_bias = jnp.sum(own_cols(dy), axis=0)
    g_pre_wide = mm_nt(cotangent, mlp_down) * slope
    g_pre = g_pre_wide.astype(bf16)
    g_up = mm_tn(normed_two, g_pre)
    g_up_bias = jnp.sum(wide(g_pre), axis=0)
    e_two = psum_y(mm_nt(g_pre, mlp_up))
    g_resid = (dy + norm_back(e_two, xhat_two, inverse_two, wide(second_gain))).astype(bf16)
    g_gain_two = jnp.sum(own_cols(e_two * xhat_two), axis=0)
    g_shift_two = jnp.sum(own_cols(e_two), axis=0)
    g_attn_bias = jnp.sum(wide(own_cols(g_resid)), axis=0)
    g_out = mm_tn(attended, g_resid)
    g_att = mm_nt(g_resid, attn_out).astype(bf16).reshape(rows, heads, HEAD_DIM)
    g_probs = jnp.einsum("qhc,khc->hqk", g_att, v, preferred_element_type=f32)
    g_v = jnp.einsum("hqk,qhc->khc", probs_low, g_att, preferred_element_type=f32)
    g_scores = (probs * (g_probs - jnp.sum(probs * g_probs, axis=-1, keepdims=True))).astype(bf16)
    g_q = jnp.einsum("hqk,khc->qhc", g_scores, k, preferred_element_type=f32) * score_scale
    g_k = jnp.einsum("hqk,qhc->khc", g_scores, q, preferred_element_type=f32) * score_scale
    g_qkv = jnp.stack([a.reshape(rows, cols).astype(bf16) for a in (g_q, g_k, g_v)], axis=1)
    g_attn_qkv = jnp.einsum("td,tke->dke", normed, g_qkv, preferred_element_type=f32)
    e_one = psum_y(jnp.einsum("tke,dke->td", g_qkv, attn_qkv, preferred_element_type=f32))
    g_stream = (wide(g_resid) + norm_back(e_one, xhat_one, inverse_one, wide(first_gain))).astype(bf16)
    g_gain_one = jnp.sum(own_cols(e_one * xhat_one), axis=0)
    g_shift_one = jnp.sum(own_cols(e_one), axis=0)

    g_wo = mm_tn(mixed, g_stream)
    g_own = own_cols(g_stream)
    g_agg_bias = jnp.sum(wide(g_own), axis=0)
    g_pos = mm_tn(onehot, g_own)
    g_mixed = mm_nt(g_stream, agg_wo).reshape(rows, heads, HEAD_DIM)
    g_mixed_low = g_mixed.astype(bf16)
    by_term = jnp.einsum("thc,khc->htk", g_mixed_low, value_terms, preferred_element_type=f32)
    by_term = by_term.reshape(heads, rows, VARS, TERMS)
    g_weights = jnp.sum(by_term * values[None], axis=-1)
    g_sc = weights * (g_weights - jnp.sum(weights * g_weights, axis=-1, keepdims=True))
    g_values = g_sc[..., None] * key_terms[:, None] + weights[..., None] * by_term
    g_patch = jnp.sum(g_values[..., :PATCH], axis=0).reshape(rows, VARS * PATCH)
    patch_out = wide(
        lax.psum_scatter(g_patch.astype(bf16), "tensor", scatter_dimension=1, tiled=True)
    )
    t_sum = jnp.einsum("htk,thc->khc", shares, g_mixed_low, preferred_element_type=f32)
    t_sum = t_sum.reshape(VARS * TERMS, cols)
    s_sum = jnp.sum(g_sc[..., None] * values[None], axis=1).reshape(heads, VARS * TERMS)

    parts = [
        t_sum, s_sum, g_wo, g_agg_bias, g_pos, g_gain_one, g_shift_one, g_attn_qkv, g_out,
        g_attn_bias, g_gain_two, g_shift_two, g_up, g_up_bias, g_down, g_down_bias,
    ]
    parts = [wide(p) for p in lax.psum([p.astype(bf16) for p in parts], ("dp", "pipe"))]
    (
        t_sum, s_sum, g_wo, g_agg_bias, g_pos, g_gain_one, g_shift_one, g_attn_qkv, g_out,
        g_attn_bias, g_gain_two, g_shift_two, g_up, g_up_bias, g_down, g_down_bias,
    ) = parts
    t_low = t_sum.astype(bf16)
    g_terms = mm_nt(t_low, agg_wv) + mm_tn(s_sum, key_dir, precision=highest)
    g_terms = wide(lax.psum_scatter(g_terms.astype(bf16), "tensor", scatter_dimension=1, tiled=True))
    g_terms = g_terms.reshape(VARS, TERMS, cols)
    g_wv = mm_tn(terms, t_low)
    along = mm(s_sum, wide(terms), precision=highest) * score_scale
    g_wk = (along.T[:, :, None] * wide(query)[None]).reshape(D, cols)
    g_query = jnp.einsum(
        "hd,dhc->hc", along, wide(agg_wk).reshape(D, heads, HEAD_DIM), precision=highest
    ).reshape(cols)
    g_wq = wide(agg_query)[:, None] * g_query[None, :]
    g_agg_query = jnp.dot(wide(agg_wq), g_query, precision=highest)
    g_agg_query = lax.psum_scatter(g_agg_query, "tensor", scatter_dimension=0, tiled=True)
    return (
        block_out, patch_out, g_terms[:, :PATCH], g_terms[:, PATCH], g_agg_query, g_wq, g_wk, g_wv,
        g_wo, g_agg_bias, g_pos, g_gain_one, g_shift_one, g_attn_qkv, g_out, g_attn_bias,
        g_gain_two, g_shift_two, g_up, g_up_bias, g_down, g_down_bias,
    )


def solution(mesh):
    rows = P(("dp", "pipe"), None)
    cols = P(None, "tensor")
    split = P("tensor", None)
    part = P("tensor")
    both = P(("dp", "pipe"), "tensor")
    last = P(None, None, "tensor")
    return jax.shard_map(
        shards,
        mesh=mesh,
        in_specs=(
            rows, P("dp", None), rows, P(), P(), P(), cols, cols, cols, split, part, cols, P(), P(),
            last, split, P(), P(), P(), cols, part, split, P(),
        ),
        out_specs=(
            both, both, last, cols, part, cols, cols, cols, split, part, cols, part, part, last,
            split, part, part, part, cols, part, split, part,
        ),
        check_vma=False,
    )
```

```python
import jax
import jax.numpy as jnp
from jax import lax
from jax.experimental import pallas as pl
from jax.experimental.pallas import tpu as pltpu
from jax.sharding import PartitionSpec as P

D = 1024
HEAD_DIM = 64
VARS = 48
PATCH = 4
LONGEST = 96
RING = 4
ROWS = 128
OWN = ROWS // RING
COLS = D // RING
HEADS = COLS // HEAD_DIM
HALF = 64
TERMS = 6 * HALF

AT_DOWN = 0
AT_UP = 4096
AT_OUT = 8192
AT_QKV = 9216
AT_WO = 12288
AT_T = 13312
AT_POS = AT_T + TERMS
AT_SMALL = AT_POS + 128
SMALL = 32
PAY = 14336

norm_eps = 1e-05
root_half = 0.7071067811865476
inv_root_tau = 0.3989422804014327
score_scale = HEAD_DIM ** (-0.5)
highest = lax.Precision.HIGHEST
f32 = jnp.float32
bf16 = jnp.bfloat16
MESH = pl.DeviceIdType.MESH


def wide(v):
    return v.astype(f32)


def dot(left, right, dims, precision=None):
    return lax.dot_general(left, right, (dims, ((), ())), precision=precision, preferred_element_type=f32)


def mm(a, b, **kw):
    return dot(a, b, ((1,), (0,)), **kw)


def mm_nt(a, b, **kw):
    return dot(a, b, ((1,), (1,)), **kw)


def mm_tn(a, b, **kw):
    return dot(a, b, ((0,), (0,)), **kw)


def iota(shape, axis):
    return lax.broadcasted_iota(jnp.int32, shape, axis)


def norm_parts(x):
    centred = x - jnp.mean(x, axis=-1, keepdims=True)
    inverse = lax.rsqrt(jnp.mean(centred * centred, axis=-1, keepdims=True) + norm_eps)
    return centred * inverse, inverse


def norm_back(grad, xhat, inverse, gain):
    scaled = grad * gain
    return inverse * (
        scaled
        - jnp.mean(scaled, axis=-1, keepdims=True)
        - xhat * jnp.mean(scaled * xhat, axis=-1, keepdims=True)
    )


def col_sum(a):
    return jnp.sum(a, axis=0, keepdims=True)


WEIGHTS = ("wq", "wk", "wv", "wo", "pos", "wqkv", "wout", "wup", "wdown", "dy")


def chain(
    lengths, patches, pw, ve, vecs,
    hq, hk, hv, ho, hpos, hqkv, hout, hup, hdown, hdy,
    out_block, out_patch, pay,
    wq, wk, wv, wo, pos, wqkv, wout, wup, wdown, dy,
    terms, shares, vterms, kterms, soft, x3, onehot,
    part, rs_in, stream, normed, resid, normed2, g_resid, g_stream,
    mixed, qkv, probs, attended, active, slope, g_pre, masked,
    got_block, put_block, got_patch, put_patch, got_gain, put_gain, small,
    load_sem, rs_send, rs_recv, ag_send, ag_recv, end_send, end_recv,
):
    y = lax.axis_index("tensor")
    pipe = lax.axis_index("pipe")
    own_rows = pl.ds(pl.multiple_of(y * OWN, OWN), OWN)
    own_cols = pl.ds(pl.multiple_of(y * COLS, COLS), COLS)
    loads = {
        name: pltpu.make_async_copy(src, dst, load_sem.at[i])
        for i, (name, src, dst) in enumerate(zip(
            WEIGHTS,
            (hq, hk, hv, ho, hpos, hqkv, hout, hup, hdown, hdy),
            (wq, wk, wv, wo, pos.at[pl.ds(0, LONGEST)], wqkv, wout, wup, wdown, dy),
        ))
    }
    for name in WEIGHTS:
        loads[name].start()

    barrier = pltpu.get_barrier_semaphore()
    for j in (1, 2, 3):
        pl.semaphore_signal(
            barrier, inc=1, device_id={"tensor": lax.rem(y + j, RING)}, device_id_type=MESH
        )
    pl.semaphore_wait(barrier, 3)

    def remote(src, dst, send, recv, j):
        return pltpu.make_async_remote_copy(
            src_ref=src, dst_ref=dst, send_sem=send, recv_sem=recv,
            device_id={"tensor": lax.rem(y + j, RING)}, device_id_type=MESH,
        )

    def rows_of(j):
        return pl.ds(pl.multiple_of(lax.rem(y + j, RING) * OWN, OWN), OWN)

    def scatter(phase):
        copies = [
            remote(part.at[phase, rows_of(j)], rs_in.at[phase, j - 1],
                   rs_send.at[phase, j - 1], rs_recv.at[phase, j - 1], j)
            for j in (2, 1, 3)
        ]
        for c in copies:
            c.start()
        return copies

    def scattered(phase, copies):
        total = wide(part[phase, own_rows, :])
        for c in copies:
            c.wait_recv()
        for j in range(3):
            total = total + wide(rs_in[phase, j])
        return total

    def gather(phase, full):
        copies = [
            remote(full.at[own_rows], full.at[own_rows],
                   ag_send.at[phase, j - 1], ag_recv.at[phase, j - 1], j)
            for j in (2, 1, 3)
        ]
        for c in copies:
            c.start()
        return copies

    def arrived(copies):
        for c in copies:
            c.wait_recv()

    started = []
    vec = wide(vecs[...])

    first, second = lengths[pipe, 0], lengths[pipe, 1]
    both = first + second

    def segment_of(r):
        return (r >= first).astype(jnp.int32) + (r >= both).astype(jnp.int32)

    same_item = segment_of(iota((ROWS, ROWS), 0)) == segment_of(iota((ROWS, ROWS), 1))
    row = iota((ROWS, 128), 0)
    place = row - jnp.where(row >= first, first, 0) - jnp.where(row >= both, second, 0)
    onehot[...] = jnp.where(place == iota((ROWS, 128), 1), 1.0, 0.0).astype(bf16)
    pos[LONGEST:, :] = jnp.zeros((128 - LONGEST, COLS), bf16)

    r, c = iota((4 * HALF, VARS * PATCH), 0), iota((4 * HALF, VARS * PATCH), 1)
    pick = jnp.where((c == PATCH * (r % HALF) + r // HALF) & (r % HALF < VARS), 1.0, 0.0).astype(bf16)
    terms[: 4 * HALF, :] = mm(pick, pw[...]).astype(bf16)
    terms[4 * HALF : 4 * HALF + VARS, :] = ve[...]
    terms[4 * HALF + VARS :, :] = jnp.zeros((TERMS - 4 * HALF - VARS, D), bf16)
    x3[:, : 4 * HALF] = mm_nt(patches[...], pick)
    lane = iota((ROWS, 128), 1)
    x3[:, 4 * HALF :] = jnp.where(lane < VARS, 1.0, 0.0)

    loads["wq"].wait()
    query = mm(vecs[...], wq[...])[0:1, :].astype(bf16)
    head_of = iota((8, COLS), 1) // HEAD_DIM
    block = jnp.where(
        head_of == iota((8, COLS), 0) % HEADS, jnp.broadcast_to(wide(query), (8, COLS)), 0.0
    ).astype(bf16)
    loads["wk"].wait()
    key_dir = mm_nt(block, wk[...]) * score_scale
    high = key_dir.astype(bf16)
    split = jnp.where(iota((8, D), 0) < HEADS, wide(high), key_dir - wide(high)).astype(bf16)
    key_parts = mm_nt(split, terms[...])
    kterms[...] = key_parts + pltpu.roll(key_parts, HEADS, 0)
    loads["wv"].wait()
    vterms[...] = mm(terms[...], wv[...]).astype(bf16)

    def fold(v):
        folded = v[:, :128] + v[:, 128:256] + v[:, 256:]
        return folded + pltpu.roll(folded, HALF, 1)

    def thrice(v):
        return jnp.concatenate([v, v, v], axis=1)

    for h in range(HEADS):
        scores = fold(x3[...] * kterms[h : h + 1, :])
        scores = jnp.where(lane % HALF < VARS, scores, -1e30)
        raised = jnp.exp(scores - jnp.max(scores, axis=-1, keepdims=True))
        weights = raised / (0.5 * jnp.sum(raised, axis=-1, keepdims=True))
        soft[h] = weights
        shares[h * ROWS : (h + 1) * ROWS, :] = (x3[...] * thrice(weights)).astype(bf16)

    col_head = iota((ROWS, COLS), 1) // HEAD_DIM

    def pick_heads(stacked):
        total = jnp.zeros((ROWS, COLS), f32)
        for h in range(HEADS):
            total = jnp.where(col_head == h, stacked[h * ROWS : (h + 1) * ROWS, :], total)
        return total

    def spread_heads(value):
        for h in range(HEADS):
            masked[h * ROWS : (h + 1) * ROWS, :] = jnp.where(col_head == h, value, 0.0).astype(bf16)

    mixed[...] = pick_heads(mm(shares[...], vterms[...])).astype(bf16)
    loads["wo"].wait()
    loads["pos"].wait()
    for j in range(RING):
        cols = slice(j * COLS, (j + 1) * COLS)
        part[0, :, cols] = mm(mixed[...], wo[:, cols]).astype(bf16)
    extra = mm(mixed[...], wo[:, own_cols]) + mm(onehot[...], pos[...]) + vec[8:9, :COLS]
    part[0, :, own_cols] = extra.astype(bf16)
    sent = scatter(0)
    started += sent
    stream_own = wide(scattered(0, sent).astype(bf16))
    xhat1, inv1 = norm_parts(stream_own)
    normed[own_rows, :] = (xhat1 * vec[1:2, :] + vec[2:3, :]).astype(bf16)
    stream[...] = stream_own
    sent = gather(0, normed)
    started += sent
    loads["wqkv"].wait()
    arrived(sent)

    for j in range(3):
        qkv[j] = mm(normed[...], wqkv[:, j * COLS : (j + 1) * COLS]).astype(bf16)
    spread_heads(qkv[0])
    raw = mm_nt(masked[...], qkv[1]) * score_scale
    for h in range(HEADS):
        rows = slice(h * ROWS, (h + 1) * ROWS)
        score = jnp.where(same_item, raw[rows, :], -1e30)
        raised = jnp.exp(score - jnp.max(score, axis=-1, keepdims=True))
        probs[rows, :] = raised / jnp.sum(raised, axis=-1, keepdims=True)
    attended[...] = pick_heads(mm(probs[...].astype(bf16), qkv[2])).astype(bf16)
    loads["wout"].wait()
    for j in range(RING):
        cols = slice(j * COLS, (j + 1) * COLS)
        part[1, :, cols] = mm(attended[...], wout[:, cols]).astype(bf16)
    sent = scatter(1)
    started += sent
    resid_own = stream[...] + scattered(1, sent) + vec[3:4, :]
    xhat2, inv2 = norm_parts(resid_own)
    normed2[own_rows, :] = (xhat2 * vec[4:5, :] + vec[5:6, :]).astype(bf16)
    resid[...] = resid_own
    sent = gather(1, normed2)
    started += sent
    loads["wup"].wait()
    loads["wdown"].wait()
    loads["dy"].wait()
    arrived(sent)

    for j in range(RING):
        cols = slice(j * COLS, (j + 1) * COLS)
        pre = mm(normed2[...], wup[:, cols]) + vec[7:8, cols]
        half_cdf = 0.5 * (1.0 + lax.erf(pre * root_half))
        active[:, cols] = (pre * half_cdf).astype(bf16)
        slope = half_cdf + pre * jnp.exp(-0.5 * pre * pre) * inv_root_tau
        grad = (mm_nt(dy[...], wdown[cols, :]) * slope).astype(bf16)
        g_pre[:, cols] = grad
        small[8 + j : 9 + j, :] = col_sum(wide(grad))
    for j in range(RING):
        rows = slice(j * COLS, (j + 1) * COLS)
        part[3, :, rows] = mm_nt(g_pre[...], wup[rows, :]).astype(bf16)
    sent3 = scatter(3)
    for j in range(RING):
        cols = slice(j * COLS, (j + 1) * COLS)
        part[2, :, cols] = mm(active[...], wdown[:, cols]).astype(bf16)
    sent2 = scatter(2)
    for j in range(RING):
        cols = slice(j * COLS, (j + 1) * COLS)
        pay[AT_DOWN + j * D : AT_DOWN + (j + 1) * D, :] = mm_tn(active[...], dy[:, cols]).astype(bf16)
        pay[AT_UP + j * D : AT_UP + (j + 1) * D, :] = mm_tn(normed2[...], g_pre[:, cols]).astype(bf16)
    started += sent3 + sent2
    e2 = scattered(3, sent3)
    g_resid_own = (wide(dy[own_rows, :]) + norm_back(e2, xhat2, inv2, vec[4:5, :])).astype(bf16)
    g_resid[own_rows, :] = g_resid_own
    sent = gather(2, g_resid)
    started += sent
    result = resid[...] + scattered(2, sent2) + vec[6:7, :]
    gain2, shift2 = col_sum(e2 * xhat2), col_sum(e2)
    for j in range(RING):
        put_block[j] = result[:, j * COLS : (j + 1) * COLS].astype(bf16)
    block_sent = [
        remote(put_block.at[lax.rem(y + j, RING)], got_block.at[own_rows],
               end_send.at[0, j - 1], end_recv.at[0, j - 1], j)
        for j in (2, 1, 3)
    ]
    for copy in block_sent:
        copy.start()
    got_block[own_rows, :] = put_block[y]
    arrived(sent)

    spread_heads(mm_nt(g_resid[...], wout[...]).astype(bf16))
    g_probs = mm_nt(masked[...], qkv[2])
    g_v = mm_tn(probs[...].astype(bf16), masked[...]).astype(bf16)
    p = probs[...]
    g_scores = (p * (g_probs - jnp.sum(p * g_probs, axis=-1, keepdims=True))).astype(bf16)
    g_q = (pick_heads(mm(g_scores, qkv[1])) * score_scale).astype(bf16)
    spread_heads(qkv[0])
    g_k = (mm_tn(g_scores, masked[...]) * score_scale).astype(bf16)
    for j in range(RING):
        rows = slice(j * COLS, (j + 1) * COLS)
        total = mm_nt(g_q, wqkv[rows, :COLS]) + mm_nt(g_k, wqkv[rows, COLS : 2 * COLS])
        part[4, :, rows] = (total + mm_nt(g_v, wqkv[rows, 2 * COLS :])).astype(bf16)
    sent = scatter(4)
    started += sent
    for j, g in enumerate((g_q, g_k, g_v)):
        pay[AT_QKV + j * D : AT_QKV + (j + 1) * D, :] = mm_tn(normed[...], g).astype(bf16)
    for j in range(RING):
        cols = slice(j * COLS, (j + 1) * COLS)
        pay[AT_OUT + j * COLS : AT_OUT + (j + 1) * COLS, :] = mm_tn(
            attended[...], g_resid[:, cols]
        ).astype(bf16)
    e1 = scattered(4, sent)
    g_stream_own = (
        wide(g_resid[own_rows, :]) + norm_back(e1, xhat1, inv1, vec[1:2, :])
    ).astype(bf16)
    g_stream[own_rows, :] = g_stream_own
    sent = gather(3, g_stream)
    started += sent
    gain1, shift1 = col_sum(e1 * xhat1), col_sum(e1)
    for j in range(RING):
        cols = slice(j * COLS, (j + 1) * COLS)
        for i, v in enumerate((gain1, shift1, gain2, shift2)):
            put_gain[j, i : i + 1, :] = v[:, cols]
        put_gain[j, 4:8, :] = jnp.zeros((4, COLS), f32)
    gain_sent = [
        remote(put_gain.at[lax.rem(y + j, RING)], got_gain.at[j - 1],
               end_send.at[1, j - 1], end_recv.at[1, j - 1], j)
        for j in (2, 1, 3)
    ]
    for copy in gain_sent:
        copy.start()
    arrived(sent)

    spread_heads(mm_nt(g_stream[...], wo[...]).astype(bf16))
    by_term = mm_nt(masked[...], vterms[...])
    grad_patch = jnp.zeros((ROWS, 4 * HALF), f32)
    for h in range(HEADS):
        mine = by_term[h * ROWS : (h + 1) * ROWS, :]
        weights = soft[h]
        g_weights = fold(x3[...] * mine)
        g_sc = weights * (
            g_weights - 0.5 * jnp.sum(weights * g_weights, axis=-1, keepdims=True)
        )
        g_sc2 = jnp.concatenate([g_sc, g_sc], axis=1)
        w2 = jnp.concatenate([weights, weights], axis=1)
        grad_patch = grad_patch + g_sc2 * kterms[h : h + 1, : 4 * HALF] + w2 * mine[:, : 4 * HALF]
        sums = col_sum(x3[...] * thrice(g_sc))
        small[12 + 2 * h : 13 + 2 * h, :] = sums[:, :COLS]
        small[13 + 2 * h : 14 + 2 * h, :128] = sums[:, COLS:]
        small[13 + 2 * h : 14 + 2 * h, 128:] = jnp.zeros((1, 128), f32)
    low_patch = grad_patch.astype(bf16)
    r, c = iota((4 * HALF, 128), 0), iota((4 * HALF, 128), 1)
    width = VARS * PATCH // RING
    for j in range(RING):
        col = c + width * j
        pick_own = jnp.where(
            (col == PATCH * (r % HALF) + r // HALF) & (r % HALF < VARS) & (c < width), 1.0, 0.0
        ).astype(bf16)
        put_patch[j] = mm(low_patch, pick_own).astype(bf16)
    patch_sent = [
        remote(put_patch.at[lax.rem(y + j, RING)], got_patch.at[j - 1],
               end_send.at[2, j - 1], end_recv.at[2, j - 1], j)
        for j in (2, 1, 3)
    ]
    for copy in patch_sent:
        copy.start()
    pay[AT_T : AT_T + TERMS, :] = mm_tn(shares[...], masked[...]).astype(bf16)
    for j in range(RING):
        cols = slice(j * COLS, (j + 1) * COLS)
        pay[AT_WO + j * COLS : AT_WO + (j + 1) * COLS, :] = mm_tn(
            mixed[...], g_stream[:, cols]
        ).astype(bf16)
    g_own = g_stream[:, own_cols]
    pay[AT_POS : AT_POS + 128, :] = mm_tn(onehot[...], g_own).astype(bf16)
    small[0:1, :] = col_sum(wide(g_own))
    small[5:6, :] = col_sum(wide(g_resid[:, own_cols]))
    small[6:7, :] = col_sum(wide(dy[:, own_cols]))
    arrived(gain_sent)
    small[1:5, :] = (put_gain[y] + got_gain[0] + got_gain[1] + got_gain[2])[0:4, :]
    small[7:8, :] = jnp.zeros((1, COLS), f32)
    small[20:32, :] = jnp.zeros((12, COLS), f32)
    pay[AT_SMALL : AT_SMALL + SMALL, :] = small[...].astype(bf16)
    pay[AT_SMALL + SMALL :, :] = jnp.zeros((PAY - AT_SMALL - SMALL, COLS), bf16)
    arrived(patch_sent)
    out_patch[...] = (
        wide(put_patch[y]) + wide(got_patch[0]) + wide(got_patch[1]) + wide(got_patch[2])
    )
    arrived(block_sent)
    out_block[...] = got_block[...]
    for copy in started + block_sent + gain_sent + patch_sent:
        copy.wait_send()


def run_chain(lengths, patches, pw, ve, vecs, *weights):
    vmem = pl.BlockSpec(memory_space=pltpu.VMEM)
    hbm = pl.BlockSpec(memory_space=pl.ANY)
    V = pltpu.VMEM
    low = lambda *s: V(s, bf16)
    full = lambda *s: V(s, f32)
    scratch = [low(*w.shape) if w.shape[0] != LONGEST else low(128, COLS) for w in weights]
    scratch += [
        low(TERMS, D), low(HEADS * ROWS, TERMS), low(TERMS, COLS), full(8, TERMS),
        full(HEADS, ROWS, 128), full(ROWS, TERMS), low(ROWS, 128),
        low(5, ROWS, D), low(5, 3, OWN, D), full(OWN, D), low(ROWS, D), full(OWN, D),
        low(ROWS, D), low(ROWS, D), low(ROWS, D),
        low(ROWS, COLS), low(3, ROWS, COLS), full(HEADS * ROWS, ROWS), low(ROWS, COLS),
        low(ROWS, D), full(8, 128), low(ROWS, D), low(HEADS * ROWS, COLS),
        low(ROWS, COLS), low(RING, OWN, COLS), low(3, ROWS, 128), low(RING, ROWS, 128),
        full(3, 8, COLS), full(RING, 8, COLS), full(SMALL, COLS),
    ]
    dma = pltpu.SemaphoreType.DMA
    scratch += [dma((len(weights),)), dma((5, 3)), dma((5, 3)), dma((4, 3)), dma((4, 3)), dma((3, 3)), dma((3, 3))]
    return pl.pallas_call(
        chain,
        out_shape=(
            jax.ShapeDtypeStruct((ROWS, COLS), bf16),
            jax.ShapeDtypeStruct((ROWS, 128), f32),
            jax.ShapeDtypeStruct((PAY, COLS), bf16),
        ),
        in_specs=[pl.BlockSpec(memory_space=pltpu.SMEM)] + [vmem] * 4 + [hbm] * len(weights),
        out_specs=(vmem, vmem, vmem),
        scratch_shapes=scratch,
        compiler_params=pltpu.CompilerParams(
            collective_id=0, has_side_effects=True, vmem_limit_bytes=60 * 1024 * 1024
        ),
    )(lengths, patches, pw, ve, vecs, *weights)


def shards(
    patches, item_lengths, cotangent, patch_weight, var_embed, agg_query, agg_wq, agg_wk, agg_wv,
    agg_wo, agg_bias, pos_table, first_gain, first_shift, attn_qkv, attn_out, attn_bias,
    second_gain, second_shift, mlp_up, up_bias, mlp_down, down_bias,
):
    flat_pw = patch_weight.reshape(VARS * PATCH, D)
    vecs = jnp.stack([
        agg_query, first_gain, first_shift, attn_bias, second_gain, second_shift, down_bias, up_bias,
        jnp.pad(agg_bias, (0, D - COLS)),
    ] + [jnp.zeros((D,), bf16)] * 7)
    block_out, patch_out, pay = run_chain(
        item_lengths, patches, flat_pw, var_embed, vecs,
        agg_wq, agg_wk, agg_wv, agg_wo, pos_table, attn_qkv.reshape(D, 3 * COLS), attn_out,
        mlp_up, mlp_down, cotangent,
    )
    pay = lax.psum(pay, ("dp", "pipe"))

    def stacked(at, blocks, rows):
        return wide(pay[at : at + blocks * rows]).reshape(blocks, rows, COLS)

    def columns(at, rows):
        return stacked(at, RING, rows).transpose(1, 0, 2).reshape(rows, D)

    g_down, g_up = columns(AT_DOWN, D), columns(AT_UP, D)
    g_out, g_wo = columns(AT_OUT, COLS), columns(AT_WO, COLS)
    g_qkv = stacked(AT_QKV, 3, D).transpose(1, 0, 2)
    t_low = pay[AT_T : AT_T + TERMS]
    g_pos = wide(pay[AT_POS : AT_POS + LONGEST])
    small = wide(pay[AT_SMALL : AT_SMALL + SMALL])
    s_sum = small[12:20].reshape(HEADS, 2 * COLS)[:, :TERMS]
    terms = jnp.zeros((6, HALF, D), bf16)
    terms = terms.at[:PATCH, :VARS].set(patch_weight.transpose(1, 0, 2))
    terms = terms.at[PATCH, :VARS].set(var_embed).reshape(TERMS, D)
    query = mm(agg_query[None, :], agg_wq).astype(bf16)
    block = jnp.where(
        (jnp.arange(COLS) // HEAD_DIM)[None, :] == jnp.arange(HEADS)[:, None], wide(query), 0.0
    )
    key_dir = mm_nt(block.astype(bf16), agg_wk) * score_scale
    g_terms = mm_nt(t_low, agg_wv) + mm_tn(s_sum, key_dir, precision=highest)
    g_terms = wide(lax.psum_scatter(g_terms.astype(bf16), "tensor", scatter_dimension=1, tiled=True))
    g_terms = g_terms.reshape(6, HALF, COLS)
    g_wv = mm_tn(terms, t_low)
    along = mm(s_sum, wide(terms), precision=highest) * score_scale
    g_wk = mm_tn(along, block, precision=highest)
    g_query = jnp.sum(
        jnp.where(block != 0, mm(along, wide(agg_wk), precision=highest), 0.0), axis=0
    )
    g_query = jnp.sum(
        jnp.where(
            (jnp.arange(COLS) // HEAD_DIM)[None, :] == jnp.arange(HEADS)[:, None],
            mm(along, wide(agg_wk), precision=highest), 0.0,
        ), axis=0,
    )
    g_wq = wide(agg_query)[:, None] * g_query[None, :]
    g_agg_query = jnp.dot(wide(agg_wq), g_query, precision=highest)
    g_agg_query = lax.psum_scatter(g_agg_query, "tensor", scatter_dimension=0, tiled=True)
    return (
        block_out, patch_out[:, : VARS * PATCH // RING],
        g_terms[:PATCH, :VARS].transpose(1, 0, 2), g_terms[PATCH, :VARS],
        g_agg_query, g_wq, g_wk, g_wv, g_wo, small[0], g_pos, small[1], small[2], g_qkv, g_out,
        small[5], small[3], small[4], g_up, small[8:12].reshape(D), g_down, small[6],
    )


def solution(mesh):
    rows = P(("dp", "pipe"), None)
    cols = P(None, "tensor")
    split = P("tensor", None)
    part = P("tensor")
    both = P(("dp", "pipe"), "tensor")
    last = P(None, None, "tensor")
    return jax.shard_map(
        shards,
        mesh=mesh,
        in_specs=(
            rows, P("dp", None), rows, P(), P(), P(), cols, cols, cols, split, part, cols, P(), P(),
            last, split, P(), P(), P(), cols, part, split, P(),
        ),
        out_specs=(
            both, both, last, cols, part, cols, cols, cols, split, part, cols, part, part, last,
            split, part, part, part, cols, part, split, part,
        ),
        check_vma=False,
    )
```

```python
import jax
import jax.numpy as jnp
from jax import lax
from jax.experimental import pallas as pl
from jax.experimental.pallas import tpu as pltpu
from jax.sharding import PartitionSpec as P

D = 1024
HEAD_DIM = 64
VARS = 48
PATCH = 4
LONGEST = 96
RING = 4
ROWS = 128
OWN = ROWS // RING
COLS = D // RING
HEADS = COLS // HEAD_DIM
HALF = 64
TERMS = 6 * HALF

AT_DOWN = 0
AT_UP = 4096
AT_OUT = 8192
AT_QKV = 9216
AT_REST = 12288
PAY = 14336
AT_TERMS = PAY
ALL = PAY + 512
SEGMENTS = ((AT_DOWN, 4096), (AT_UP, 4096), (AT_OUT, 4096), (AT_REST, 2048))
HALF_REST = 1024
AT_POS = AT_REST + HALF_REST + 128
SMALL = 32

norm_eps = 1e-05
root_half = 0.7071067811865476
inv_root_tau = 0.3989422804014327
score_scale = HEAD_DIM ** (-0.5)
highest = lax.Precision.HIGHEST
f32 = jnp.float32
bf16 = jnp.bfloat16
MESH = pl.DeviceIdType.MESH


def wide(v):
    return v.astype(f32)


def dot(left, right, dims, precision=None):
    return lax.dot_general(left, right, (dims, ((), ())), precision=precision, preferred_element_type=f32)


def mm(a, b, **kw):
    return dot(a, b, ((1,), (0,)), **kw)


def mm_nt(a, b, **kw):
    return dot(a, b, ((1,), (1,)), **kw)


def mm_tn(a, b, **kw):
    return dot(a, b, ((0,), (0,)), **kw)


def iota(shape, axis):
    return lax.broadcasted_iota(jnp.int32, shape, axis)


def norm_parts(x):
    centred = x - jnp.mean(x, axis=-1, keepdims=True)
    inverse = lax.rsqrt(jnp.mean(centred * centred, axis=-1, keepdims=True) + norm_eps)
    return centred * inverse, inverse


def norm_back(grad, xhat, inverse, gain):
    scaled = grad * gain
    return inverse * (
        scaled
        - jnp.mean(scaled, axis=-1, keepdims=True)
        - xhat * jnp.mean(scaled * xhat, axis=-1, keepdims=True)
    )


def col_sum(a):
    return jnp.sum(a, axis=0, keepdims=True)


WEIGHTS = ("wq", "wk", "wv", "wo", "pos", "wqkv", "wout", "wup", "wdown", "dy")


def as_row(ref):
    value = wide(ref[...])
    return jnp.concatenate([value[i : i + 1, :] for i in range(value.shape[0])], axis=1)


def in_two(value):
    high = wide(value.astype(bf16))
    return jnp.concatenate([high, value - high], axis=0).astype(bf16)


def chain(
    lengths, patches, pw, ve, aq_in, gain1_in, shift1_in, abias_in, gain2_in, shift2_in, dbias_in,
    ubias_in, aggbias_in,
    hq, hk, hv, ho, hpos, hqkv, hout, hup, hdown, hdy,
    out_block, out_patch, out_all, out_terms, out_small, out_query,
    wq, wk, wv, wo, pos, wqkv, wout, wup, wdown, dy,
    pwf, terms, shares, vterms, kterms, kdir, soft, x3, onehot,
    part, rs_in, stream, normed, resid, normed2, g_resid, g_stream,
    mixed, qkv, probs, attended, active, g_pre, masked,
    got_block, put_block, got_patch, put_patch, got_gain, put_gain, small, score_sum,
    got_aq, put_aq, got_terms, put_terms, rd_out, rd_in,
    pay, tot, sum_in,
    load_sem, rs_send, rs_recv, ag_send, ag_recv, end_send, end_recv,
    sum_send, sum_recv, extra_send, extra_recv, rd_send, rd_recv, save_sem,
):
    y = lax.axis_index("tensor")
    pipe = lax.axis_index("pipe")
    dp = lax.axis_index("dp")
    x, z = lax.rem(dp, 4), dp // 4
    own_rows = pl.ds(pl.multiple_of(y * OWN, OWN), OWN)
    own_cols = pl.ds(pl.multiple_of(y * COLS, COLS), COLS)
    dims = {
        "core": (pipe, {"pipe": 1 - pipe}),
        "xa": (lax.rem((x + 1) // 2, 2), {"dp": dp + 1 - 2 * lax.rem(x, 2)}),
        "xb": (x // 2, {"dp": 4 * z + 3 - x}),
        "za": (lax.rem((z + 1) // 2, 2), {"dp": dp + 4 - 8 * lax.rem(z, 2)}),
        "zb": (z // 2, {"dp": 4 * (3 - z) + x}),
    }
    ring = ("xa", "za", "xb", "zb")
    orders = [ring[k:] + ring[:k] for k in range(4)]
    loads = {
        name: pltpu.make_async_copy(src, dst, load_sem.at[i])
        for i, (name, src, dst) in enumerate(zip(
            WEIGHTS,
            (hq, hk, hv, ho, hpos, hqkv, hout, hup, hdown, hdy),
            (wq, wk, wv, wo, pos.at[pl.ds(0, LONGEST)], wqkv, wout, wup, wdown, dy),
        ))
    }
    for name in WEIGHTS:
        loads[name].start()

    barrier = pltpu.get_barrier_semaphore()
    for j in (1, 2, 3):
        pl.semaphore_signal(
            barrier, inc=1, device_id={"tensor": lax.rem(y + j, RING)}, device_id_type=MESH
        )
    for _, partner in dims.values():
        pl.semaphore_signal(barrier, inc=1, device_id=partner, device_id_type=MESH)
    pl.semaphore_wait(barrier, 8)

    started = []

    def to_partner(src, dst, send, recv, dim):
        return pltpu.make_async_remote_copy(
            src_ref=src, dst_ref=dst, send_sem=send, recv_sem=recv,
            device_id=dims[dim][1], device_id_type=MESH,
        )

    def rows_at(start, length):
        return pl.ds(pl.multiple_of(start, 16), length)

    def region(base, length, order, steps):
        for dim in order[:steps]:
            length //= 2
            base = base + dims[dim][0] * length
        return base, length

    def part_of(seg, k, steps):
        at, count = SEGMENTS[seg]
        return region(at + pipe * (count // 2) + k * (count // 8), count // 8, orders[k], steps)

    in_at = {}
    place_in = 0
    for seg, (_, count) in enumerate(SEGMENTS):
        in_at[seg, "core"] = place_in
        place_in += count // 2
        for s in range(4):
            for k in range(4):
                in_at[seg, s, k] = place_in
                place_in += count // 16 >> s

    def core_halving(seg):
        at, count = SEGMENTS[seg]
        half = count // 2
        return to_partner(
            pay.at[rows_at(at + (1 - pipe) * half, half)], sum_in.at[pl.ds(in_at[seg, "core"], half)],
            sum_send.at[seg, 0], sum_recv.at[seg, 0], "core",
        )

    def halving(seg, s, k):
        base, length = part_of(seg, k, s)
        dim = orders[k][s]
        length //= 2
        at = 1 + 4 * s + k
        return to_partner(
            pay.at[rows_at(base + (1 - dims[dim][0]) * length, length)],
            sum_in.at[pl.ds(in_at[seg, s, k], length)], sum_send.at[seg, at], sum_recv.at[seg, at], dim,
        )

    def doubling(seg, t, k):
        rows = rows_at(*part_of(seg, k, t + 1))
        at = 17 + 4 * t + k
        return to_partner(
            tot.at[rows], tot.at[rows], sum_send.at[seg, at], sum_recv.at[seg, at], orders[k][t]
        )

    def core_doubling(seg):
        at, count = SEGMENTS[seg]
        rows = rows_at(at + pipe * (count // 2), count // 2)
        return to_partner(tot.at[rows], tot.at[rows], sum_send.at[seg, 33], sum_recv.at[seg, 33], "core")

    def save(at, count, i):
        return pltpu.make_async_copy(tot.at[pl.ds(at, count)], out_all.at[pl.ds(at, count)], save_sem.at[i])

    def launch(copy):
        copy.start()
        started.append(copy)

    def advance(seg, stage):
        at, count = SEGMENTS[seg]
        if stage == 0:
            launch(core_halving(seg))
        elif stage == 1:
            core_halving(seg).wait_recv()
            quarter = count // 8
            for k in range(4):
                rows = rows_at(at + pipe * (count // 2) + k * quarter, quarter)
                came = pl.ds(in_at[seg, "core"] + k * quarter, quarter)
                pay[rows, :] = pay[rows, :] + sum_in[came, :]
                launch(halving(seg, 0, k))
        elif stage <= 5:
            s = stage - 2
            for k in range(4):
                halving(seg, s, k).wait_recv()
                base, length = part_of(seg, k, s + 1)
                rows = rows_at(base, length)
                total = pay[rows, :] + sum_in[pl.ds(in_at[seg, s, k], length), :]
                if s < 3:
                    pay[rows, :] = total
                    launch(halving(seg, s + 1, k))
                else:
                    tot[rows, :] = total
                    launch(doubling(seg, 3, k))
        elif stage <= 9:
            t = 9 - stage
            for k in range(4):
                doubling(seg, t, k).wait_recv()
                if t:
                    launch(doubling(seg, t - 1, k))
            if t == 0:
                launch(core_doubling(seg))
        else:
            core_doubling(seg).wait_recv()
            save(at, count, seg).start()

    def remote(src, dst, send, recv, j):
        return pltpu.make_async_remote_copy(
            src_ref=src, dst_ref=dst, send_sem=send, recv_sem=recv,
            device_id={"tensor": lax.rem(y + j, RING)}, device_id_type=MESH,
        )

    def rows_of(j):
        return pl.ds(pl.multiple_of(lax.rem(y + j, RING) * OWN, OWN), OWN)

    def scatter(phase):
        copies = [
            remote(part.at[phase, rows_of(j)], rs_in.at[phase, j - 1],
                   rs_send.at[phase, j - 1], rs_recv.at[phase, j - 1], j)
            for j in (2, 1, 3)
        ]
        for c in copies:
            c.start()
        return copies

    def scattered(phase, copies):
        total = wide(part[phase, own_rows, :])
        for c in copies:
            c.wait_recv()
        for j in range(3):
            total = total + wide(rs_in[phase, j])
        return total

    def gather(phase, full):
        copies = [
            remote(full.at[own_rows], full.at[own_rows],
                   ag_send.at[phase, j - 1], ag_recv.at[phase, j - 1], j)
            for j in (2, 1, 3)
        ]
        for c in copies:
            c.start()
        return copies

    def arrived(copies):
        for c in copies:
            c.wait_recv()

    aq_row, gain1_row, shift1_row = as_row(aq_in), as_row(gain1_in), as_row(shift1_in)
    abias_row, gain2_row, shift2_row = as_row(abias_in), as_row(gain2_in), as_row(shift2_in)
    dbias_row, ubias_row, aggbias_row = as_row(dbias_in), as_row(ubias_in), as_row(aggbias_in)
    for c in range(2):
        pay[AT_REST + c * HALF_REST : AT_REST + c * HALF_REST + 512, :] = jnp.zeros((512, COLS), bf16)

    first, second = lengths[pipe, 0], lengths[pipe, 1]
    both = first + second

    def segment_of(r):
        return (r >= first).astype(jnp.int32) + (r >= both).astype(jnp.int32)

    same_item = segment_of(iota((ROWS, ROWS), 0)) == segment_of(iota((ROWS, ROWS), 1))
    row = iota((ROWS, 128), 0)
    place = row - jnp.where(row >= first, first, 0) - jnp.where(row >= both, second, 0)
    onehot[...] = jnp.where(place == iota((ROWS, 128), 1), 1.0, 0.0).astype(bf16)
    pos[LONGEST:, :] = jnp.zeros((128 - LONGEST, COLS), bf16)

    r, c = iota((4 * HALF, VARS * PATCH), 0), iota((4 * HALF, VARS * PATCH), 1)
    pick = jnp.where((c == PATCH * (r % HALF) + r // HALF) & (r % HALF < VARS), 1.0, 0.0).astype(bf16)
    for v in range(VARS):
        pwf[PATCH * v : PATCH * (v + 1), :] = wide(pw[v])
    terms[: 4 * HALF, :] = mm(pick, pwf[...].astype(bf16)).astype(bf16)
    terms[4 * HALF : 4 * HALF + VARS, :] = ve[...]
    terms[4 * HALF + VARS :, :] = jnp.zeros((TERMS - 4 * HALF - VARS, D), bf16)
    r, c = iota((VARS * PATCH, 4 * HALF), 1), iota((VARS * PATCH, 4 * HALF), 0)
    pick_back = jnp.where((c == PATCH * (r % HALF) + r // HALF) & (r % HALF < VARS), 1.0, 0.0).astype(bf16)
    x3[:, : 4 * HALF] = mm_tn(patches[...], pick_back)
    lane = iota((ROWS, 128), 1)
    x3[:, 4 * HALF :] = jnp.where(lane < VARS, 1.0, 0.0)

    loads["wq"].wait()
    query = mm(jnp.broadcast_to(aq_row, (8, D)).astype(bf16), wq[...])[0:1, :].astype(bf16)
    out_query[...] = jnp.broadcast_to(wide(query), (8, COLS))
    head_of = iota((8, COLS), 1) // HEAD_DIM
    block = jnp.where(
        head_of == iota((8, COLS), 0) % HEADS, jnp.broadcast_to(wide(query), (8, COLS)), 0.0
    ).astype(bf16)
    loads["wk"].wait()
    key_dir = mm_nt(block, wk[...]) * score_scale
    split = in_two(key_dir[:HEADS, :])
    kdir[...] = jnp.concatenate([wide(split), jnp.zeros((120, D), f32)], axis=0).astype(bf16)
    key_parts = mm_nt(split, terms[...])
    kterms[...] = key_parts + pltpu.roll(key_parts, HEADS, 0)
    loads["wv"].wait()
    vterms[...] = mm(terms[...], wv[...]).astype(bf16)

    def fold(v):
        folded = v[:, :128] + v[:, 128:256] + v[:, 256:]
        return folded + pltpu.roll(folded, HALF, 1)

    def thrice(v):
        return jnp.concatenate([v, v, v], axis=1)

    for h in range(HEADS):
        scores = fold(x3[...] * kterms[h : h + 1, :])
        scores = jnp.where(lane % HALF < VARS, scores, -1e30)
        raised = jnp.exp(scores - jnp.max(scores, axis=-1, keepdims=True))
        weights = raised / (0.5 * jnp.sum(raised, axis=-1, keepdims=True))
        soft[h] = weights
        shares[h * ROWS : (h + 1) * ROWS, :] = (x3[...] * thrice(weights)).astype(bf16)

    col_head = iota((ROWS, COLS), 1) // HEAD_DIM

    def pick_heads(stacked):
        total = jnp.zeros((ROWS, COLS), f32)
        for h in range(HEADS):
            total = jnp.where(col_head == h, stacked[h * ROWS : (h + 1) * ROWS, :], total)
        return total

    def spread_heads(value):
        for h in range(HEADS):
            masked[h * ROWS : (h + 1) * ROWS, :] = jnp.where(col_head == h, value, 0.0).astype(bf16)

    mixed[...] = pick_heads(mm(shares[...], vterms[...])).astype(bf16)
    loads["wo"].wait()
    loads["pos"].wait()
    for j in range(RING):
        cols = slice(j * COLS, (j + 1) * COLS)
        part[0, :, cols] = mm(mixed[...], wo[:, cols]).astype(bf16)
    extra = mm(mixed[...], wo[:, own_cols]) + mm(onehot[...], pos[...]) + aggbias_row
    part[0, :, own_cols] = extra.astype(bf16)
    sent = scatter(0)
    started += sent
    stream_own = wide(scattered(0, sent).astype(bf16))
    xhat1, inv1 = norm_parts(stream_own)
    normed[own_rows, :] = (xhat1 * gain1_row + shift1_row).astype(bf16)
    stream[...] = stream_own
    sent = gather(0, normed)
    started += sent
    loads["wqkv"].wait()
    arrived(sent)

    for j in range(3):
        qkv[j] = mm(normed[...], wqkv[j]).astype(bf16)
    spread_heads(qkv[0])
    raw = mm_nt(masked[...], qkv[1]) * score_scale
    for h in range(HEADS):
        rows = slice(h * ROWS, (h + 1) * ROWS)
        score = jnp.where(same_item, raw[rows, :], -1e30)
        raised = jnp.exp(score - jnp.max(score, axis=-1, keepdims=True))
        probs[rows, :] = raised / jnp.sum(raised, axis=-1, keepdims=True)
    attended[...] = pick_heads(mm(probs[...].astype(bf16), qkv[2])).astype(bf16)
    loads["wout"].wait()
    for j in range(RING):
        cols = slice(j * COLS, (j + 1) * COLS)
        part[1, :, cols] = mm(attended[...], wout[:, cols]).astype(bf16)
    sent = scatter(1)
    started += sent
    resid_own = stream[...] + scattered(1, sent) + abias_row
    xhat2, inv2 = norm_parts(resid_own)
    normed2[own_rows, :] = (xhat2 * gain2_row + shift2_row).astype(bf16)
    resid[...] = resid_own
    sent = gather(1, normed2)
    started += sent
    loads["wup"].wait()
    loads["wdown"].wait()
    loads["dy"].wait()
    arrived(sent)

    for j in range(RING):
        cols = slice(j * COLS, (j + 1) * COLS)
        pre = mm(normed2[...], wup[:, cols]) + ubias_row[:, cols]
        half_cdf = 0.5 * (1.0 + lax.erf(pre * root_half))
        active[:, cols] = (pre * half_cdf).astype(bf16)
        slope = half_cdf + pre * jnp.exp(-0.5 * pre * pre) * inv_root_tau
        grad = (mm_nt(dy[...], wdown[cols, :]) * slope).astype(bf16)
        g_pre[:, cols] = grad
        small[8 + j : 9 + j, :] = col_sum(wide(grad))
    for j in range(RING):
        rows = slice(j * COLS, (j + 1) * COLS)
        part[3, :, rows] = mm_nt(g_pre[...], wup[rows, :]).astype(bf16)
    sent3 = scatter(3)
    for j in range(RING):
        cols = slice(j * COLS, (j + 1) * COLS)
        part[2, :, cols] = mm(active[...], wdown[:, cols]).astype(bf16)
    sent2 = scatter(2)
    for j in range(RING):
        cols = slice(j * COLS, (j + 1) * COLS)
        pay[AT_DOWN + j * D : AT_DOWN + (j + 1) * D, :] = mm_tn(active[...], dy[:, cols]).astype(bf16)
    advance(0, 0)
    for j in range(RING):
        cols = slice(j * COLS, (j + 1) * COLS)
        pay[AT_UP + j * D : AT_UP + (j + 1) * D, :] = mm_tn(normed2[...], g_pre[:, cols]).astype(bf16)
    advance(1, 0)
    started += sent3 + sent2
    e2 = scattered(3, sent3)
    g_resid_own = (wide(dy[own_rows, :]) + norm_back(e2, xhat2, inv2, gain2_row)).astype(bf16)
    g_resid[own_rows, :] = g_resid_own
    sent = gather(2, g_resid)
    started += sent
    advance(0, 1)
    result = resid[...] + scattered(2, sent2) + dbias_row
    gain2, shift2 = col_sum(e2 * xhat2), col_sum(e2)
    for j in range(RING):
        put_block[j] = result[:, j * COLS : (j + 1) * COLS].astype(bf16)
    block_sent = [
        remote(put_block.at[lax.rem(y + j, RING)], got_block.at[own_rows],
               end_send.at[0, j - 1], end_recv.at[0, j - 1], j)
        for j in (2, 1, 3)
    ]
    for copy in block_sent:
        copy.start()
    got_block[own_rows, :] = put_block[y]
    arrived(sent)

    spread_heads(mm_nt(g_resid[...], wout[...]).astype(bf16))
    g_probs = mm_nt(masked[...], qkv[2])
    g_v = mm_tn(probs[...].astype(bf16), masked[...]).astype(bf16)
    p = probs[...]
    g_scores = (p * (g_probs - jnp.sum(p * g_probs, axis=-1, keepdims=True))).astype(bf16)
    advance(1, 1)
    g_q = (pick_heads(mm(g_scores, qkv[1])) * score_scale).astype(bf16)
    spread_heads(qkv[0])
    g_k = (mm_tn(g_scores, masked[...]) * score_scale).astype(bf16)
    for j in range(RING):
        rows = slice(j * COLS, (j + 1) * COLS)
        total = mm_nt(g_q, wqkv[0, rows, :]) + mm_nt(g_k, wqkv[1, rows, :])
        part[4, :, rows] = (total + mm_nt(g_v, wqkv[2, rows, :])).astype(bf16)
    sent = scatter(4)
    started += sent
    advance(0, 2)
    for j, g in enumerate((g_q, g_k, g_v)):
        pay[AT_QKV + j * D : AT_QKV + (j + 1) * D, :] = mm_tn(normed[...], g).astype(bf16)
    for j in range(RING):
        cols = slice(j * COLS, (j + 1) * COLS)
        pay[AT_OUT + j * COLS : AT_OUT + (j + 1) * COLS, :] = mm_tn(
            attended[...], g_resid[:, cols]
        ).astype(bf16)
    advance(2, 0)
    advance(1, 2)
    e1 = scattered(4, sent)
    g_stream_own = (
        wide(g_resid[own_rows, :]) + norm_back(e1, xhat1, inv1, gain1_row)
    ).astype(bf16)
    g_stream[own_rows, :] = g_stream_own
    sent = gather(3, g_stream)
    started += sent
    gain1, shift1 = col_sum(e1 * xhat1), col_sum(e1)
    for j in range(RING):
        cols = slice(j * COLS, (j + 1) * COLS)
        for i, v in enumerate((gain1, shift1, gain2, shift2)):
            put_gain[j, i : i + 1, :] = v[:, cols]
        put_gain[j, 4:8, :] = jnp.zeros((4, COLS), f32)
    gain_sent = [
        remote(put_gain.at[lax.rem(y + j, RING)], got_gain.at[j - 1],
               end_send.at[1, j - 1], end_recv.at[1, j - 1], j)
        for j in (2, 1, 3)
    ]
    for copy in gain_sent:
        copy.start()
    advance(0, 3)
    advance(1, 3)
    advance(2, 1)
    arrived(sent)

    spread_heads(mm_nt(g_stream[...], wo[...]).astype(bf16))
    by_term = mm_nt(masked[...], vterms[...])
    grad_patch = jnp.zeros((ROWS, 4 * HALF), f32)
    for h in range(HEADS):
        mine = by_term[h * ROWS : (h + 1) * ROWS, :]
        weights = soft[h]
        g_weights = fold(x3[...] * mine)
        g_sc = weights * (
            g_weights - 0.5 * jnp.sum(weights * g_weights, axis=-1, keepdims=True)
        )
        g_sc2 = jnp.concatenate([g_sc, g_sc], axis=1)
        w2 = jnp.concatenate([weights, weights], axis=1)
        grad_patch = grad_patch + g_sc2 * kterms[h : h + 1, : 4 * HALF] + w2 * mine[:, : 4 * HALF]
        sums = col_sum(x3[...] * thrice(g_sc))
        score_sum[h : h + 1, :] = sums
    value_sum = mm_tn(shares[...], masked[...]).astype(bf16)
    pay[AT_REST : AT_REST + 256, :] = value_sum[:256, :]
    pay[AT_REST + HALF_REST : AT_REST + HALF_REST + 128, :] = value_sum[256:, :]
    head_cols = iota((HEADS, COLS), 1)
    spot = jnp.where((head_cols % HEADS == iota((HEADS, COLS), 0)) & (head_cols < 8), 1.0, 0.0).astype(bf16)
    across = mm_tn(score_sum[...].astype(bf16), spot).astype(bf16)
    for n in range(TERMS // 16):
        c, j = n // 16, n % 16
        at = AT_REST + c * HALF_REST + 256 + 16 * ((2 * j) % 16 + j // 8)
        pay[at : at + 16, :] = across[16 * n : 16 * (n + 1), :]
    g_own = g_stream[:, own_cols]
    pay[AT_POS : AT_POS + LONGEST, :] = mm_tn(onehot[...], g_own)[:LONGEST, :].astype(bf16)
    for j in range(RING):
        cols = slice(j * COLS, (j + 1) * COLS)
        at = AT_REST + (j // 2) * HALF_REST + 512 + (j % 2) * COLS
        pay[at : at + COLS, :] = mm_tn(mixed[...], g_stream[:, cols]).astype(bf16)
    advance(3, 0)
    along = in_two(mm(in_two(score_sum[...]), terms[...])[:HEADS] + mm(in_two(score_sum[...]), terms[...])[HEADS:])
    head_of = iota((8, COLS), 1) // HEAD_DIM
    g_query = col_sum(jnp.where(head_of == iota((8, COLS), 0) % HEADS, mm(along, wk[...]), 0.0)) * score_scale
    both_parts = mm_nt(in_two(jnp.broadcast_to(g_query, (HEADS, COLS))), wq[...])
    g_aq = both_parts[0:1, :] + both_parts[HEADS : HEADS + 1, :]
    for j in range(RING):
        put_aq[j] = jnp.broadcast_to(g_aq[:, j * COLS : (j + 1) * COLS], (8, COLS))
    aq_sent = [
        remote(put_aq.at[lax.rem(y + j, RING)], got_aq.at[j - 1],
               end_send.at[3, j - 1], end_recv.at[3, j - 1], j)
        for j in (2, 1, 3)
    ]
    for copy in aq_sent:
        copy.start()
    low_patch = grad_patch.astype(bf16)
    width = VARS * PATCH // RING
    r, c = iota((width, 4 * HALF), 1), iota((width, 4 * HALF), 0)
    for j in range(RING):
        pick_own = jnp.where(
            (c + width * j == PATCH * (r % HALF) + r // HALF) & (r % HALF < VARS), 1.0, 0.0
        ).astype(bf16)
        put_patch[j] = mm_nt(pick_own, low_patch).astype(bf16)
    patch_sent = [
        remote(put_patch.at[lax.rem(y + j, RING)], got_patch.at[j - 1],
               end_send.at[2, j - 1], end_recv.at[2, j - 1], j)
        for j in (2, 1, 3)
    ]
    for copy in patch_sent:
        copy.start()
    small[0:1, :] = col_sum(wide(g_own))
    small[5:6, :] = col_sum(wide(g_resid[:, own_cols]))
    small[6:7, :] = col_sum(wide(dy[:, own_cols]))
    small[12:32, :] = jnp.zeros((20, COLS), f32)
    arrived(gain_sent)
    small[1:5, :] = (put_gain[y] + got_gain[0] + got_gain[1] + got_gain[2])[0:4, :]

    def vector_step(i, start):
        dim = ("core",) + ring
        copy = to_partner(rd_out.at[i], rd_in.at[i], rd_send.at[i], rd_recv.at[i], dim[i])
        if start:
            launch(copy)
        else:
            copy.wait_recv()
            value = rd_out[i] + rd_in[i]
            if i < 4:
                rd_out[i + 1] = value
                vector_step(i + 1, True)
            else:
                out_small[...] = value

    def terms_rows(steps):
        return rows_at(*region(AT_TERMS + pipe * 256, 256, orders[0], steps))

    def terms_doubling(t):
        rows = terms_rows(t + 1)
        return to_partner(tot.at[rows], tot.at[rows], extra_send.at[t], extra_recv.at[t], orders[0][t])

    def terms_core():
        rows = rows_at(AT_TERMS + pipe * 256, 256)
        return to_partner(tot.at[rows], tot.at[rows], extra_send.at[4], extra_recv.at[4], "core")

    terms_sent = [
        remote(put_terms.at[lax.rem(y + j, RING)], got_terms.at[j - 1],
               end_send.at[4, j - 1], end_recv.at[4, j - 1], j)
        for j in (2, 1, 3)
    ]

    def terms_step(i):
        if i == 0:
            value_rows = tot[rows_at(*part_of(3, 0, 4)), :]
            score_rows = tot[rows_at(*part_of(3, 1, 4)), :]
            total = mm_nt(value_rows, wv[...]) + mm(score_rows[:, :128], kdir[...])
            for j in range(RING):
                put_terms[j] = total[:, j * COLS : (j + 1) * COLS].astype(bf16)
            for copy in terms_sent:
                launch(copy)
        elif i == 1:
            arrived(terms_sent)
            total = wide(put_terms[y]) + wide(got_terms[0]) + wide(got_terms[1]) + wide(got_terms[2])
            tot[terms_rows(4), :] = total.astype(bf16)
            launch(terms_doubling(3))
        elif i < 6:
            t = 5 - i
            terms_doubling(t).wait_recv()
            launch(terms_doubling(t - 1) if t else terms_core())
        else:
            terms_core().wait_recv()
            save(AT_TERMS, 512, 4).start()

    stages = {0: 4, 1: 4, 2: 2, 3: 1}
    extra, vector = 0, -1
    while extra <= 6:
        for seg in (3, 2, 1, 0):
            if stages[seg] <= 10:
                advance(seg, stages[seg])
                stages[seg] += 1
        if stages[3] > 5:
            terms_step(extra)
            extra += 1
        if vector < 0:
            arrived(aq_sent)
            small[7:8, :] = (put_aq[y] + got_aq[0] + got_aq[1] + got_aq[2])[0:1, :]
            rd_out[0] = small[...]
            vector_step(0, True)
            vector = 0
        elif vector < 5:
            vector_step(vector, False)
            vector += 1
    arrived(patch_sent)
    out_patch[...] = (
        wide(put_patch[y]) + wide(got_patch[0]) + wide(got_patch[1]) + wide(got_patch[2])
    )
    arrived(block_sent)
    out_block[...] = got_block[...]
    out_terms[...] = terms[...]
    for copy in started + block_sent + gain_sent + patch_sent + aq_sent:
        copy.wait_send()
    for i, (at, count) in enumerate(SEGMENTS + ((AT_TERMS, 512),)):
        save(at, count, i).wait()


VMEM_LIMIT = 60 * 1024 * 1024


def run_chain(lengths, *args):
    vmem = pl.BlockSpec(memory_space=pltpu.VMEM)
    hbm = pl.BlockSpec(memory_space=pl.ANY)
    V = pltpu.VMEM
    low = lambda *s: V(s, bf16)
    full = lambda *s: V(s, f32)
    weights = args[-len(WEIGHTS):]
    scratch = [low(*w.shape) if w.shape[0] != LONGEST else low(128, COLS) for w in weights]
    scratch += [
        full(VARS * PATCH, D), low(TERMS, D), low(HEADS * ROWS, TERMS), low(TERMS, COLS), full(8, TERMS),
        low(128, D), full(HEADS, ROWS, 128), full(ROWS, TERMS), low(ROWS, 128),
        low(5, ROWS, D), low(5, 3, OWN, D), full(OWN, D), low(ROWS, D), full(OWN, D),
        low(ROWS, D), low(ROWS, D), low(ROWS, D),
        low(ROWS, COLS), low(3, ROWS, COLS), full(HEADS * ROWS, ROWS), low(ROWS, COLS),
        low(ROWS, D), low(ROWS, D), low(HEADS * ROWS, COLS),
        low(ROWS, COLS), low(RING, OWN, COLS), low(3, 48, ROWS), low(RING, 48, ROWS),
        full(3, 8, COLS), full(RING, 8, COLS), full(SMALL, COLS), full(HEADS, TERMS),
        full(3, 8, COLS), full(RING, 8, COLS), low(3, 16, COLS), low(RING, 16, COLS),
        full(5, SMALL, COLS), full(5, SMALL, COLS),
        low(PAY, COLS), low(ALL, COLS), low(PAY * 31 // 32, COLS),
    ]
    dma = pltpu.SemaphoreType.DMA
    scratch += [
        dma((len(weights),)), dma((5, 3)), dma((5, 3)), dma((4, 3)), dma((4, 3)), dma((5, 3)), dma((5, 3)),
        dma((4, 34)), dma((4, 34)), dma((5,)), dma((5,)), dma((5,)), dma((5,)), dma((5,)),
    ]
    return pl.pallas_call(
        chain,
        out_shape=(
            jax.ShapeDtypeStruct((ROWS, COLS), bf16),
            jax.ShapeDtypeStruct((48, ROWS), f32),
            jax.ShapeDtypeStruct((ALL, COLS), bf16),
            jax.ShapeDtypeStruct((TERMS, D), bf16),
            jax.ShapeDtypeStruct((SMALL, COLS), f32),
            jax.ShapeDtypeStruct((8, COLS), f32),
        ),
        in_specs=[pl.BlockSpec(memory_space=pltpu.SMEM)]
        + [vmem] * (len(args) - len(weights)) + [hbm] * len(weights),
        out_specs=(vmem, vmem, hbm, vmem, vmem, vmem),
        scratch_shapes=scratch,
        compiler_params=pltpu.CompilerParams(
            collective_id=0, has_side_effects=True, vmem_limit_bytes=VMEM_LIMIT
        ),
    )(lengths, *args)


VECTORS = (0, 7, 1, 2, 5, 3, 4, 6)


def finish(
    all_in, block_in, patch_in, terms, small, query, aq_in, hk,
    o_block, o_patch, o_down, o_up, o_out, o_qkv, o_wo, o_wv, o_wk, o_wq,
    o_pw, o_ve, o_pos, *rest,
):
    o_vectors, o_upbias = rest[:8], rest[8]
    tot, wk, down, up, out, qkv, wo, gv, gk, gq, load_sem, save_sem = rest[9:]
    spans = SEGMENTS + ((AT_TERMS, 512),)
    order = (3, 0, 1, 2, 4)
    loads = {
        i: pltpu.make_async_copy(all_in.at[pl.ds(at, n)], tot.at[pl.ds(at, n)], load_sem.at[i])
        for i, (at, n) in enumerate(spans)
    }
    get_k = pltpu.make_async_copy(hk, wk, load_sem.at[5])
    for i in order[:1]:
        loads[i].start()
    get_k.start()
    for i in order[1:]:
        loads[i].start()
    saves = [
        pltpu.make_async_copy(block_in, o_block, save_sem.at[8]),
        pltpu.make_async_copy(patch_in, o_patch, save_sem.at[9]),
    ]
    for copy in saves:
        copy.start()

    def store(i, src, dst):
        copy = pltpu.make_async_copy(src, dst, save_sem.at[i])
        copy.start()
        saves.append(copy)

    loads[3].wait()
    value_sum = jnp.concatenate(
        [tot[AT_REST : AT_REST + 256, :], tot[AT_REST + HALF_REST : AT_REST + HALF_REST + 128, :]], axis=0
    )
    gv[...] = mm_tn(terms[...], value_sum)
    store(0, gv, o_wv)
    for j in range(RING):
        at = AT_REST + (j // 2) * HALF_REST + 512 + (j % 2) * COLS
        wo[:, j * COLS : (j + 1) * COLS] = wide(tot[at : at + COLS, :])
    store(1, wo, o_wo)
    o_pos[...] = wide(tot[AT_POS : AT_POS + LONGEST, :])
    rows = []
    for n in range(TERMS // 16):
        c, j = n // 16, n % 16
        at = AT_REST + c * HALF_REST + 256 + 16 * ((2 * j) % 16 + j // 8)
        rows.append(tot[at : at + 16, :128])
    across = jnp.concatenate(rows, axis=0)
    along = in_two(mm_tn(across, terms[...])[:HEADS, :])
    head_of = iota((8, COLS), 1) // HEAD_DIM
    mine = head_of == iota((8, COLS), 0) % HEADS
    block = jnp.where(mine, query[...], 0.0).astype(bf16)
    gk[...] = mm_tn(along, block) * score_scale
    store(2, gk, o_wk)
    get_k.wait()
    g_query = col_sum(jnp.where(mine, mm(along, wk[...]), 0.0)) * score_scale
    row = iota((8, D), 0)
    aq = jnp.where(row < 2, jnp.broadcast_to(as_row(aq_in), (8, D)), 0.0).astype(bf16)
    high = wide(g_query.astype(bf16))
    both = jnp.where(
        iota((8, COLS), 0) == 0,
        jnp.broadcast_to(high, (8, COLS)), jnp.broadcast_to(g_query - high, (8, COLS)),
    ).astype(bf16)
    gq[...] = mm_tn(aq, both)
    store(3, gq, o_wq)

    loads[0].wait()
    for j in range(RING):
        down[:, j * COLS : (j + 1) * COLS] = wide(tot[AT_DOWN + j * D : AT_DOWN + (j + 1) * D, :])
    store(4, down, o_down)
    loads[1].wait()
    for j in range(RING):
        up[:, j * COLS : (j + 1) * COLS] = wide(tot[AT_UP + j * D : AT_UP + (j + 1) * D, :])
    store(5, up, o_up)
    loads[2].wait()
    for j in range(3):
        qkv[j] = wide(tot[AT_QKV + j * D : AT_QKV + (j + 1) * D, :])
    store(6, qkv, o_qkv)
    for j in range(RING):
        out[:, j * COLS : (j + 1) * COLS] = wide(tot[AT_OUT + j * COLS : AT_OUT + (j + 1) * COLS, :])
    store(7, out, o_out)
    loads[4].wait()
    for p in range(PATCH):
        o_pw[:, p, :] = wide(tot[AT_TERMS + HALF * p : AT_TERMS + HALF * p + VARS, :])
    o_ve[...] = wide(tot[AT_TERMS + 4 * HALF : AT_TERMS + 4 * HALF + VARS, :])
    for ref, i in zip(o_vectors, VECTORS):
        ref[0:1, :] = small[i : i + 1, :128]
        ref[1:2, :] = small[i : i + 1, 128:]
    for j in range(RING):
        o_upbias[2 * j : 2 * j + 1, :] = small[8 + j : 9 + j, :128]
        o_upbias[2 * j + 1 : 2 * j + 2, :] = small[8 + j : 9 + j, 128:]
    for copy in saves:
        copy.wait()


def run_finish(*args):
    vmem = pl.BlockSpec(memory_space=pltpu.VMEM)
    hbm = pl.BlockSpec(memory_space=pl.ANY)
    full = lambda *s: pltpu.VMEM(s, f32)
    shape = lambda *s: jax.ShapeDtypeStruct(s, f32)
    big = [(D, D), (D, D), (COLS, D), (3, D, COLS), (COLS, D), (D, COLS), (D, COLS), (D, COLS)]
    return pl.pallas_call(
        finish,
        out_shape=[jax.ShapeDtypeStruct((ROWS, COLS), bf16), shape(48, ROWS)]
        + [shape(*s) for s in big]
        + [shape(VARS, PATCH, COLS), shape(VARS, COLS), shape(LONGEST, COLS)]
        + [shape(2, 128)] * 8 + [shape(8, 128)],
        in_specs=[hbm, hbm, hbm, vmem, vmem, vmem, vmem, hbm],
        out_specs=[hbm] * 10 + [vmem] * 12,
        scratch_shapes=[
            pltpu.VMEM((ALL, COLS), bf16), pltpu.VMEM((D, COLS), bf16),
            full(D, D), full(D, D), full(COLS, D), full(3, D, COLS), full(COLS, D),
            full(D, COLS), full(D, COLS), full(D, COLS),
            pltpu.SemaphoreType.DMA((6,)), pltpu.SemaphoreType.DMA((10,)),
        ],
        compiler_params=pltpu.CompilerParams(vmem_limit_bytes=VMEM_LIMIT),
    )(*args)


def shards(
    patches, item_lengths, cotangent, patch_weight, var_embed, agg_query, agg_wq, agg_wk, agg_wv,
    agg_wo, agg_bias, pos_table, first_gain, first_shift, attn_qkv, attn_out, attn_bias,
    second_gain, second_shift, mlp_up, up_bias, mlp_down, down_bias,
):
    tiled = lambda v: v.reshape(v.shape[0] // 128, 128)
    block, patch, summed, terms, small, query = run_chain(
        item_lengths, patches.T, patch_weight, var_embed, tiled(agg_query), tiled(first_gain),
        tiled(first_shift), tiled(attn_bias), tiled(second_gain), tiled(second_shift),
        tiled(down_bias), tiled(up_bias), tiled(agg_bias),
        agg_wq, agg_wk, agg_wv, agg_wo, pos_table, attn_qkv.transpose(1, 0, 2), attn_out,
        mlp_up, mlp_down, cotangent,
    )
    (
        block, patch, g_down, g_up, g_out, g_qkv, g_wo, g_wv, g_wk, g_wq, g_pw, g_ve, g_pos,
        g_agg_bias, g_aq, g_gain1, g_shift1, g_attn_bias, g_gain2, g_shift2, g_down_bias, g_up_bias,
    ) = run_finish(summed, block, patch, terms, small, query, tiled(agg_query), agg_wk)
    flat = lambda v: v.reshape(-1)
    return (
        block, patch.T, g_pw, g_ve, flat(g_aq), g_wq, g_wk, g_wv, g_wo, flat(g_agg_bias), g_pos,
        flat(g_gain1), flat(g_shift1), g_qkv.transpose(1, 0, 2), g_out, flat(g_attn_bias),
        flat(g_gain2), flat(g_shift2), g_up, flat(g_up_bias), g_down, flat(g_down_bias),
    )


def solution(mesh):
    rows = P(("dp", "pipe"), None)
    cols = P(None, "tensor")
    split = P("tensor", None)
    part = P("tensor")
    both = P(("dp", "pipe"), "tensor")
    last = P(None, None, "tensor")
    return jax.shard_map(
        shards,
        mesh=mesh,
        in_specs=(
            rows, P("dp", None), rows, P(), P(), P(), cols, cols, cols, split, part, cols, P(), P(),
            last, split, P(), P(), P(), cols, part, split, P(),
        ),
        out_specs=(
            both, both, last, cols, part, cols, cols, cols, split, part, cols, part, part, last,
            split, part, part, part, cols, part, split, part,
        ),
        check_vma=False,
    )
```

```python
import jax
import jax.numpy as jnp
from jax import lax
from jax.experimental import pallas as pl
from jax.experimental.pallas import tpu as pltpu
from jax.sharding import PartitionSpec as P

D = 1024
HEAD_DIM = 64
VARS = 48
PATCH = 4
LONGEST = 96
RING = 4
ROWS = 128
OWN = ROWS // RING
COLS = D // RING
HEADS = COLS // HEAD_DIM
HALF = 64
TERMS = 6 * HALF

AT_DOWN = 0
AT_UP = 4096
AT_OUT = 8192
AT_QKV = 9216
AT_WO = 12288
AT_LAST = 13312
PAY = 14336
AT_TERMS = PAY
ALL = PAY + 512
SEGMENTS = ((AT_DOWN, 4096), (AT_UP, 4096), (AT_OUT, 4096), (AT_WO, 1024), (AT_LAST, 1024))
CUBE = (True, True, False, False, False)
HALF_LAST = 512
AT_POS = AT_LAST + HALF_LAST + 128
SMALL = 32

norm_eps = 1e-05
root_half = 0.7071067811865476
inv_root_tau = 0.3989422804014327
score_scale = HEAD_DIM ** (-0.5)
highest = lax.Precision.HIGHEST
f32 = jnp.float32
bf16 = jnp.bfloat16
MESH = pl.DeviceIdType.MESH


def wide(v):
    return v.astype(f32)


def dot(left, right, dims, precision=None):
    return lax.dot_general(left, right, (dims, ((), ())), precision=precision, preferred_element_type=f32)


def mm(a, b, **kw):
    return dot(a, b, ((1,), (0,)), **kw)


def mm_nt(a, b, **kw):
    return dot(a, b, ((1,), (1,)), **kw)


def mm_tn(a, b, **kw):
    return dot(a, b, ((0,), (0,)), **kw)


def iota(shape, axis):
    return lax.broadcasted_iota(jnp.int32, shape, axis)


def norm_parts(x):
    centred = x - jnp.mean(x, axis=-1, keepdims=True)
    inverse = lax.rsqrt(jnp.mean(centred * centred, axis=-1, keepdims=True) + norm_eps)
    return centred * inverse, inverse


def norm_back(grad, xhat, inverse, gain):
    scaled = grad * gain
    return inverse * (
        scaled
        - jnp.mean(scaled, axis=-1, keepdims=True)
        - xhat * jnp.mean(scaled * xhat, axis=-1, keepdims=True)
    )


def col_sum(a):
    return jnp.sum(a, axis=0, keepdims=True)


WEIGHTS = (
    "patches", "pw", "ve", "aq", "gain1", "shift1", "abias", "gain2", "shift2", "dbias", "ubias", "aggbias",
    "wq", "wk", "wv", "wo", "pos", "wqkv", "wout", "wup", "wdown", "dy",
)
EARLY = ("aq", "wq", "pw", "ve", "wk", "wv", "patches", "wo", "pos", "aggbias")


def as_row(ref):
    value = wide(ref[...])
    return jnp.concatenate([value[i : i + 1, :] for i in range(value.shape[0])], axis=1)


def in_two(value):
    high = wide(value.astype(bf16))
    return jnp.concatenate([high, value - high], axis=0).astype(bf16)


def score_place(n):
    c, j = n // 16, n % 16
    return AT_LAST + c * HALF_LAST + 256 + 16 * (4 * (j % 4) + j // 4)


def chain(
    lengths, hpatches, hpw, hve, haq, hgain1, hshift1, habias, hgain2, hshift2, hdbias,
    hubias, haggbias,
    hq, hk, hv, ho, hpos, hqkv, hout, hup, hdown, hdy,
    out_block, out_patch, out_all, out_terms, out_small, out_query,
    patches, pw, ve, aq_in, gain1_in, shift1_in, abias_in, gain2_in, shift2_in, dbias_in,
    ubias_in, aggbias_in,
    wq, wk, wv, wo, pos, wqkv, wout, wup, wdown, dy,
    pwf, terms, shares, vterms, kterms, kdir, soft, x3, onehot,
    part, rs_in, stream, normed, resid, normed2, g_resid, g_stream,
    mixed, qkv, probs, attended, active, g_pre, masked,
    got_block, put_block, got_patch, put_patch, got_gain, put_gain, small, score_sum,
    got_aq, put_aq, got_terms, put_terms, rd_out, rd_in, query_row, total_small, patch_sum,
    pay, tot, sum_in,
    load_sem, rs_send, rs_recv, ag_send, ag_recv, end_send, end_recv,
    sum_send, sum_recv, extra_send, extra_recv, rd_send, rd_recv, save_sem,
):
    y = lax.axis_index("tensor")
    pipe = lax.axis_index("pipe")
    dp = lax.axis_index("dp")
    x, z = lax.rem(dp, 4), dp // 4
    own_rows = pl.ds(pl.multiple_of(y * OWN, OWN), OWN)
    own_cols = pl.ds(pl.multiple_of(y * COLS, COLS), COLS)
    barrier = pltpu.get_barrier_semaphore()
    rings = {"x": (x, lambda q: {"dp": 4 * z + q}), "z": (z, lambda q: {"dp": 4 * q + x})}
    neighbours = [{"pipe": 1 - pipe}]
    for j in (1, 2, 3):
        neighbours.append({"tensor": lax.rem(y + j, RING)})
        neighbours += [at(lax.rem(p + j, RING)) for p, at in rings.values()]
    for device in neighbours:
        pl.semaphore_signal(barrier, inc=1, device_id=device, device_id_type=MESH)
    dims = {
        "core": (pipe, {"pipe": 1 - pipe}),
        "xa": (lax.rem((x + 1) // 2, 2), {"dp": dp + 1 - 2 * lax.rem(x, 2)}),
        "xb": (x // 2, {"dp": 4 * z + 3 - x}),
        "za": (lax.rem((z + 1) // 2, 2), {"dp": dp + 4 - 8 * lax.rem(z, 2)}),
        "zb": (z // 2, {"dp": 4 * (3 - z) + x}),
    }
    ring = ("xa", "za", "xb", "zb")
    orders = [ring[k:] + ring[:k] for k in range(4)]
    ring_orders = (("x", "z"), ("z", "x"))
    loads = {
        name: pltpu.make_async_copy(src, dst, load_sem.at[i])
        for i, (name, src, dst) in enumerate(zip(
            WEIGHTS,
            (hpatches, hpw, hve, haq, hgain1, hshift1, habias, hgain2, hshift2, hdbias, hubias, haggbias,
             hq, hk, hv, ho, hpos, hqkv, hout, hup, hdown, hdy),
            (patches, pw, ve, aq_in, gain1_in, shift1_in, abias_in, gain2_in, shift2_in, dbias_in,
             ubias_in, aggbias_in,
             wq, wk, wv, wo, pos.at[pl.ds(0, LONGEST)], wqkv, wout, wup, wdown, dy),
        ))
    }
    for name in EARLY + tuple(name for name in WEIGHTS if name not in EARLY):
        loads[name].start()

    started = []

    def to_partner(src, dst, send, recv, dim):
        return pltpu.make_async_remote_copy(
            src_ref=src, dst_ref=dst, send_sem=send, recv_sem=recv,
            device_id=dims[dim][1], device_id_type=MESH,
        )

    def rows_at(start, length):
        return pl.ds(pl.multiple_of(start, 16), length)

    def region(base, length, order, steps):
        for dim in order[:steps]:
            length //= 2
            base = base + dims[dim][0] * length
        return base, length

    def part_of(seg, k, steps):
        at, count = SEGMENTS[seg]
        return region(at + pipe * (count // 2) + k * (count // 8), count // 8, orders[k], steps)

    in_at = {}
    place_in = 0
    for seg, (_, count) in enumerate(SEGMENTS):
        in_at[seg, "core"] = place_in
        place_in += count // 2
        for s in range(4):
            for k in range(4):
                if CUBE[seg]:
                    in_at[seg, s, k] = place_in
                    place_in += count // 16 >> s
        for s in range(2):
            for k in range(2):
                if not CUBE[seg]:
                    in_at[seg, s, k] = place_in
                    place_in += 3 * (count // 16 >> 2 * s)
    assert place_in <= sum_in.shape[0]

    def core_halving(seg):
        at, count = SEGMENTS[seg]
        half = count // 2
        return to_partner(
            pay.at[rows_at(at + (1 - pipe) * half, half)], sum_in.at[pl.ds(in_at[seg, "core"], half)],
            sum_send.at[seg, 0], sum_recv.at[seg, 0], "core",
        )

    def halving(seg, s, k):
        base, length = part_of(seg, k, s)
        dim = orders[k][s]
        length //= 2
        at = 1 + 4 * s + k
        return to_partner(
            pay.at[rows_at(base + (1 - dims[dim][0]) * length, length)],
            sum_in.at[pl.ds(in_at[seg, s, k], length)], sum_send.at[seg, at], sum_recv.at[seg, at], dim,
        )

    def doubling(seg, t, k):
        rows = rows_at(*part_of(seg, k, t + 1))
        at = 17 + 4 * t + k
        return to_partner(
            tot.at[rows], tot.at[rows], sum_send.at[seg, at], sum_recv.at[seg, at], orders[k][t]
        )

    def core_doubling(seg):
        at, count = SEGMENTS[seg]
        rows = rows_at(at + pipe * (count // 2), count // 2)
        return to_partner(tot.at[rows], tot.at[rows], sum_send.at[seg, 33], sum_recv.at[seg, 33], "core")

    def ring_copy(src_rows, src, dst, sems, at, dim, j):
        position, device = rings[dim]
        return pltpu.make_async_remote_copy(
            src_ref=src.at[src_rows], dst_ref=dst, send_sem=sems[0].at[at], recv_sem=sems[1].at[at],
            device_id=device(lax.rem(position + j, RING)), device_id_type=MESH,
        )

    def share(base, length, order, steps):
        for dim in order[:steps]:
            length //= RING
            base = base + rings[dim][0] * length
        return base, length

    def share_of(seg, k, steps):
        at, count = SEGMENTS[seg]
        return share(at + pipe * (count // 2) + k * (count // 4), count // 4, ring_orders[k], steps)

    def ring_scatter(seg, s, k):
        base, length = share_of(seg, k, s)
        length //= RING
        dim = ring_orders[k][s]
        position = rings[dim][0]
        sems = (sum_send.at[seg], sum_recv.at[seg])
        return [
            ring_copy(
                rows_at(base + lax.rem(position + j, RING) * length, length), pay,
                sum_in.at[pl.ds(in_at[seg, s, k] + (j - 1) * length, length)],
                sems, 1 + 6 * s + 3 * k + j - 1, dim, j,
            )
            for j in (2, 1, 3)
        ]

    def ring_gather(base_length, dim, sems, at):
        rows = rows_at(*base_length)
        return [ring_copy(rows, tot, tot.at[rows], sems, at + j - 1, dim, j) for j in (2, 1, 3)]

    def ring_gather_of(seg, t, k):
        sems = (sum_send.at[seg], sum_recv.at[seg])
        return ring_gather(share_of(seg, k, t + 1), ring_orders[k][t], sems, 13 + 6 * t + 3 * k)

    def ring_advance(seg, stage):
        at, count = SEGMENTS[seg]
        if stage == 0:
            launch(core_halving(seg))
        elif stage == 1:
            core_halving(seg).wait_recv()
            quarter = count // 4
            for k in range(2):
                rows = rows_at(at + pipe * (count // 2) + k * quarter, quarter)
                came = pl.ds(in_at[seg, "core"] + k * quarter, quarter)
                pay[rows, :] = pay[rows, :] + sum_in[came, :]
                for copy in ring_scatter(seg, 0, k):
                    launch(copy)
        elif stage <= 3:
            s = stage - 2
            for k in range(2):
                arrived(ring_scatter(seg, s, k))
                base, length = share_of(seg, k, s + 1)
                rows = rows_at(base, length)
                total = wide(pay[rows, :])
                for j in range(3):
                    total = total + wide(sum_in[pl.ds(in_at[seg, s, k] + j * length, length), :])
                if s == 0:
                    pay[rows, :] = total.astype(bf16)
                    copies = ring_scatter(seg, 1, k)
                else:
                    tot[rows, :] = total.astype(bf16)
                    copies = ring_gather_of(seg, 1, k)
                for copy in copies:
                    launch(copy)
        elif stage <= 5:
            t = 5 - stage
            for k in range(2):
                arrived(ring_gather_of(seg, t, k))
                if t:
                    for copy in ring_gather_of(seg, 0, k):
                        launch(copy)
            if t == 0:
                launch(core_doubling(seg))
        else:
            core_doubling(seg).wait_recv()
            save(at, count, seg).start()

    def arrived(copies):
        for c in copies:
            c.wait_recv()

    def save(at, count, i):
        return pltpu.make_async_copy(tot.at[pl.ds(at, count)], out_all.at[pl.ds(at, count)], save_sem.at[i])

    def launch(copy):
        copy.start()
        started.append(copy)

    def advance(seg, stage):
        if not CUBE[seg]:
            return ring_advance(seg, stage)
        at, count = SEGMENTS[seg]
        if stage == 0:
            launch(core_halving(seg))
        elif stage == 1:
            core_halving(seg).wait_recv()
            quarter = count // 8
            for k in range(4):
                rows = rows_at(at + pipe * (count // 2) + k * quarter, quarter)
                came = pl.ds(in_at[seg, "core"] + k * quarter, quarter)
                pay[rows, :] = pay[rows, :] + sum_in[came, :]
                launch(halving(seg, 0, k))
        elif stage <= 5:
            s = stage - 2
            for k in range(4):
                halving(seg, s, k).wait_recv()
                base, length = part_of(seg, k, s + 1)
                rows = rows_at(base, length)
                total = pay[rows, :] + sum_in[pl.ds(in_at[seg, s, k], length), :]
                if s < 3:
                    pay[rows, :] = total
                    launch(halving(seg, s + 1, k))
                else:
                    tot[rows, :] = total
                    launch(doubling(seg, 3, k))
        elif stage <= 9:
            t = 9 - stage
            for k in range(4):
                doubling(seg, t, k).wait_recv()
                if t:
                    launch(doubling(seg, t - 1, k))
            if t == 0:
                launch(core_doubling(seg))
        else:
            core_doubling(seg).wait_recv()
            save(at, count, seg).start()

    def remote(src, dst, send, recv, j):
        return pltpu.make_async_remote_copy(
            src_ref=src, dst_ref=dst, send_sem=send, recv_sem=recv,
            device_id={"tensor": lax.rem(y + j, RING)}, device_id_type=MESH,
        )

    def rows_of(j):
        return pl.ds(pl.multiple_of(lax.rem(y + j, RING) * OWN, OWN), OWN)

    def scatter(phase):
        copies = [
            remote(part.at[phase, rows_of(j)], rs_in.at[phase, j - 1],
                   rs_send.at[phase, j - 1], rs_recv.at[phase, j - 1], j)
            for j in (2, 1, 3)
        ]
        for c in copies:
            c.start()
        return copies

    def scattered(phase, copies):
        total = wide(part[phase, own_rows, :])
        for c in copies:
            c.wait_recv()
        for j in range(3):
            total = total + wide(rs_in[phase, j])
        return total

    def gather(phase, full):
        copies = [
            remote(full.at[own_rows], full.at[own_rows],
                   ag_send.at[phase, j - 1], ag_recv.at[phase, j - 1], j)
            for j in (2, 1, 3)
        ]
        for c in copies:
            c.start()
        return copies

    for c in range(2):
        at = AT_LAST + c * HALF_LAST
        pay[at : at + HALF_LAST, :] = jnp.zeros((HALF_LAST, COLS), bf16)

    first, second = lengths[pipe, 0], lengths[pipe, 1]
    both = first + second

    def segment_of(r):
        return (r >= first).astype(jnp.int32) + (r >= both).astype(jnp.int32)

    same_item = segment_of(iota((ROWS, ROWS), 0)) == segment_of(iota((ROWS, ROWS), 1))
    row = iota((ROWS, 128), 0)
    place = row - jnp.where(row >= first, first, 0) - jnp.where(row >= both, second, 0)
    onehot[...] = jnp.where(place == iota((ROWS, 128), 1), 1.0, 0.0).astype(bf16)
    pos[LONGEST:, :] = jnp.zeros((128 - LONGEST, COLS), bf16)

    loads["pw"].wait()
    loads["ve"].wait()
    r, c = iota((4 * HALF, VARS * PATCH), 0), iota((4 * HALF, VARS * PATCH), 1)
    pick = jnp.where((c == PATCH * (r % HALF) + r // HALF) & (r % HALF < VARS), 1.0, 0.0).astype(bf16)
    for v in range(VARS):
        pwf[PATCH * v : PATCH * (v + 1), :] = wide(pw[v])
    terms[: 4 * HALF, :] = mm(pick, pwf[...].astype(bf16)).astype(bf16)
    terms[4 * HALF : 4 * HALF + VARS, :] = ve[...]
    terms[4 * HALF + VARS :, :] = jnp.zeros((TERMS - 4 * HALF - VARS, D), bf16)
    r, c = iota((VARS * PATCH, 4 * HALF), 1), iota((VARS * PATCH, 4 * HALF), 0)
    pick_back = jnp.where((c == PATCH * (r % HALF) + r // HALF) & (r % HALF < VARS), 1.0, 0.0).astype(bf16)
    loads["patches"].wait()
    x3[:, : 4 * HALF] = mm_tn(patches[...], pick_back)
    lane = iota((ROWS, 128), 1)
    x3[:, 4 * HALF :] = jnp.where(lane < VARS, 1.0, 0.0)

    loads["wq"].wait()
    loads["aq"].wait()
    aq_row = as_row(aq_in)
    query = mm(jnp.broadcast_to(aq_row, (8, D)).astype(bf16), wq[...])[0:1, :].astype(bf16)
    query_row[...] = jnp.broadcast_to(wide(query), (8, COLS))
    exports = [
        pltpu.make_async_copy(query_row, out_query, save_sem.at[6]),
        pltpu.make_async_copy(terms, out_terms, save_sem.at[7]),
    ]
    for copy in exports:
        copy.start()
    head_of = iota((8, COLS), 1) // HEAD_DIM
    block = jnp.where(
        head_of == iota((8, COLS), 0) % HEADS, jnp.broadcast_to(wide(query), (8, COLS)), 0.0
    ).astype(bf16)
    loads["wk"].wait()
    key_dir = mm_nt(block, wk[...]) * score_scale
    split = in_two(key_dir[:HEADS, :])
    kdir[...] = jnp.concatenate([wide(split), jnp.zeros((120, D), f32)], axis=0).astype(bf16)
    key_parts = mm_nt(split, terms[...])
    kterms[...] = key_parts + pltpu.roll(key_parts, HEADS, 0)
    loads["wv"].wait()
    vterms[...] = mm(terms[...], wv[...]).astype(bf16)

    def fold(v):
        folded = v[:, :128] + v[:, 128:256] + v[:, 256:]
        return folded + pltpu.roll(folded, HALF, 1)

    def thrice(v):
        return jnp.concatenate([v, v, v], axis=1)

    for h in range(HEADS):
        scores = fold(x3[...] * kterms[h : h + 1, :])
        scores = jnp.where(lane % HALF < VARS, scores, -1e30)
        raised = jnp.exp(scores - jnp.max(scores, axis=-1, keepdims=True))
        weights = raised / (0.5 * jnp.sum(raised, axis=-1, keepdims=True))
        soft[h] = weights
        shares[h * ROWS : (h + 1) * ROWS, :] = (x3[...] * thrice(weights)).astype(bf16)

    col_head = iota((ROWS, COLS), 1) // HEAD_DIM

    def pick_heads(stacked):
        total = jnp.zeros((ROWS, COLS), f32)
        for h in range(HEADS):
            total = jnp.where(col_head == h, stacked[h * ROWS : (h + 1) * ROWS, :], total)
        return total

    def spread_heads(value):
        for h in range(HEADS):
            masked[h * ROWS : (h + 1) * ROWS, :] = jnp.where(col_head == h, value, 0.0).astype(bf16)

    mixed[...] = pick_heads(mm(shares[...], vterms[...])).astype(bf16)
    loads["wo"].wait()
    loads["pos"].wait()
    loads["aggbias"].wait()
    aggbias_row = as_row(aggbias_in)
    for j in range(RING):
        cols = slice(j * COLS, (j + 1) * COLS)
        part[0, :, cols] = mm(mixed[...], wo[:, cols]).astype(bf16)
    extra = mm(mixed[...], wo[:, own_cols]) + mm(onehot[...], pos[...]) + aggbias_row
    part[0, :, own_cols] = extra.astype(bf16)
    pl.semaphore_wait(barrier, len(neighbours))
    sent = scatter(0)
    for name in ("gain1", "shift1", "abias", "gain2", "shift2", "dbias", "ubias"):
        loads[name].wait()
    gain1_row, shift1_row = as_row(gain1_in), as_row(shift1_in)
    abias_row, gain2_row, shift2_row = as_row(abias_in), as_row(gain2_in), as_row(shift2_in)
    dbias_row, ubias_row = as_row(dbias_in), as_row(ubias_in)
    started += sent
    stream_own = wide(scattered(0, sent).astype(bf16))
    xhat1, inv1 = norm_parts(stream_own)
    normed[own_rows, :] = (xhat1 * gain1_row + shift1_row).astype(bf16)
    stream[...] = stream_own
    sent = gather(0, normed)
    started += sent
    loads["wqkv"].wait()
    arrived(sent)

    for j in range(3):
        qkv[j] = mm(normed[...], wqkv[j]).astype(bf16)
    spread_heads(qkv[0])
    raw = mm_nt(masked[...], qkv[1]) * score_scale
    for h in range(HEADS):
        rows = slice(h * ROWS, (h + 1) * ROWS)
        score = jnp.where(same_item, raw[rows, :], -1e30)
        raised = jnp.exp(score - jnp.max(score, axis=-1, keepdims=True))
        probs[rows, :] = raised / jnp.sum(raised, axis=-1, keepdims=True)
    attended[...] = pick_heads(mm(probs[...].astype(bf16), qkv[2])).astype(bf16)
    loads["wout"].wait()
    for j in range(RING):
        cols = slice(j * COLS, (j + 1) * COLS)
        part[1, :, cols] = mm(attended[...], wout[:, cols]).astype(bf16)
    sent = scatter(1)
    started += sent
    resid_own = stream[...] + scattered(1, sent) + abias_row
    xhat2, inv2 = norm_parts(resid_own)
    normed2[own_rows, :] = (xhat2 * gain2_row + shift2_row).astype(bf16)
    resid[...] = resid_own
    sent = gather(1, normed2)
    started += sent
    loads["wup"].wait()
    loads["wdown"].wait()
    loads["dy"].wait()
    arrived(sent)

    for j in range(RING):
        cols = slice(j * COLS, (j + 1) * COLS)
        pre = mm(normed2[...], wup[:, cols]) + ubias_row[:, cols]
        half_cdf = 0.5 * (1.0 + lax.erf(pre * root_half))
        active[:, cols] = (pre * half_cdf).astype(bf16)
        slope = half_cdf + pre * jnp.exp(-0.5 * pre * pre) * inv_root_tau
        grad = (mm_nt(dy[...], wdown[cols, :]) * slope).astype(bf16)
        g_pre[:, cols] = grad
        small[8 + j : 9 + j, :] = col_sum(wide(grad))
    for j in range(RING):
        rows = slice(j * COLS, (j + 1) * COLS)
        part[3, :, rows] = mm_nt(g_pre[...], wup[rows, :]).astype(bf16)
    sent3 = scatter(3)
    for j in range(RING):
        cols = slice(j * COLS, (j + 1) * COLS)
        part[2, :, cols] = mm(active[...], wdown[:, cols]).astype(bf16)
    sent2 = scatter(2)
    for j in range(RING):
        cols = slice(j * COLS, (j + 1) * COLS)
        pay[AT_DOWN + j * D : AT_DOWN + (j + 1) * D, :] = mm_tn(active[...], dy[:, cols]).astype(bf16)
    advance(0, 0)
    for j in range(RING):
        cols = slice(j * COLS, (j + 1) * COLS)
        pay[AT_UP + j * D : AT_UP + (j + 1) * D, :] = mm_tn(normed2[...], g_pre[:, cols]).astype(bf16)
    advance(1, 0)
    started += sent3 + sent2
    advance(0, 1)
    advance(1, 1)
    e2 = scattered(3, sent3)
    g_resid_own = (wide(dy[own_rows, :]) + norm_back(e2, xhat2, inv2, gain2_row)).astype(bf16)
    g_resid[own_rows, :] = g_resid_own
    sent = gather(2, g_resid)
    started += sent
    result = resid[...] + scattered(2, sent2) + dbias_row
    gain2, shift2 = col_sum(e2 * xhat2), col_sum(e2)
    for j in range(RING):
        put_block[j] = result[:, j * COLS : (j + 1) * COLS].astype(bf16)
    block_sent = [
        remote(put_block.at[lax.rem(y + j, RING)], got_block.at[own_rows],
               end_send.at[0, j - 1], end_recv.at[0, j - 1], j)
        for j in (2, 1, 3)
    ]
    for copy in block_sent:
        copy.start()
    got_block[own_rows, :] = put_block[y]
    advance(0, 2)
    advance(1, 2)
    arrived(sent)

    spread_heads(mm_nt(g_resid[...], wout[...]).astype(bf16))
    g_probs = mm_nt(masked[...], qkv[2])
    g_v = mm_tn(probs[...].astype(bf16), masked[...]).astype(bf16)
    p = probs[...]
    g_scores = (p * (g_probs - jnp.sum(p * g_probs, axis=-1, keepdims=True))).astype(bf16)
    g_q = (pick_heads(mm(g_scores, qkv[1])) * score_scale).astype(bf16)
    spread_heads(qkv[0])
    g_k = (mm_tn(g_scores, masked[...]) * score_scale).astype(bf16)
    for j in range(RING):
        rows = slice(j * COLS, (j + 1) * COLS)
        total = mm_nt(g_q, wqkv[0, rows, :]) + mm_nt(g_k, wqkv[1, rows, :])
        part[4, :, rows] = (total + mm_nt(g_v, wqkv[2, rows, :])).astype(bf16)
    sent = scatter(4)
    started += sent
    for j, g in enumerate((g_q, g_k, g_v)):
        pay[AT_QKV + j * D : AT_QKV + (j + 1) * D, :] = mm_tn(normed[...], g).astype(bf16)
    for j in range(RING):
        cols = slice(j * COLS, (j + 1) * COLS)
        pay[AT_OUT + j * COLS : AT_OUT + (j + 1) * COLS, :] = mm_tn(
            attended[...], g_resid[:, cols]
        ).astype(bf16)
    advance(2, 0)
    advance(0, 3)
    advance(1, 3)
    advance(2, 1)
    advance(0, 4)
    advance(1, 4)
    e1 = scattered(4, sent)
    g_stream_own = (
        wide(g_resid[own_rows, :]) + norm_back(e1, xhat1, inv1, gain1_row)
    ).astype(bf16)
    g_stream[own_rows, :] = g_stream_own
    sent = gather(3, g_stream)
    started += sent
    gain1, shift1 = col_sum(e1 * xhat1), col_sum(e1)
    for j in range(RING):
        cols = slice(j * COLS, (j + 1) * COLS)
        for i, v in enumerate((gain1, shift1, gain2, shift2)):
            put_gain[j, i : i + 1, :] = v[:, cols]
        put_gain[j, 4:8, :] = jnp.zeros((4, COLS), f32)
    gain_sent = [
        remote(put_gain.at[lax.rem(y + j, RING)], got_gain.at[j - 1],
               end_send.at[1, j - 1], end_recv.at[1, j - 1], j)
        for j in (2, 1, 3)
    ]
    for copy in gain_sent:
        copy.start()
    advance(0, 5)
    advance(1, 5)
    advance(2, 2)
    advance(0, 6)
    arrived(sent)

    spread_heads(mm_nt(g_stream[...], wo[...]).astype(bf16))
    by_term = mm_nt(masked[...], vterms[...])
    grad_patch = jnp.zeros((ROWS, 4 * HALF), f32)
    for h in range(HEADS):
        mine = by_term[h * ROWS : (h + 1) * ROWS, :]
        weights = soft[h]
        g_weights = fold(x3[...] * mine)
        g_sc = weights * (
            g_weights - 0.5 * jnp.sum(weights * g_weights, axis=-1, keepdims=True)
        )
        g_sc2 = jnp.concatenate([g_sc, g_sc], axis=1)
        w2 = jnp.concatenate([weights, weights], axis=1)
        grad_patch = grad_patch + g_sc2 * kterms[h : h + 1, : 4 * HALF] + w2 * mine[:, : 4 * HALF]
        sums = col_sum(x3[...] * thrice(g_sc))
        score_sum[h : h + 1, :] = sums
    value_sum = mm_tn(shares[...], masked[...]).astype(bf16)
    pay[AT_LAST : AT_LAST + 256, :] = value_sum[:256, :]
    pay[AT_LAST + HALF_LAST : AT_LAST + HALF_LAST + 128, :] = value_sum[256:, :]
    head_cols = iota((HEADS, COLS), 1)
    spot = jnp.where((head_cols % HEADS == iota((HEADS, COLS), 0)) & (head_cols < 8), 1.0, 0.0).astype(bf16)
    across = mm_tn(score_sum[...].astype(bf16), spot).astype(bf16)
    for n in range(TERMS // 16):
        at = score_place(n)
        pay[at : at + 16, :] = across[16 * n : 16 * (n + 1), :]
    g_own = g_stream[:, own_cols]
    pay[AT_POS : AT_POS + LONGEST, :] = mm_tn(onehot[...], g_own)[:LONGEST, :].astype(bf16)
    advance(4, 0)
    for j in range(RING):
        cols = slice(j * COLS, (j + 1) * COLS)
        pay[AT_WO + j * COLS : AT_WO + (j + 1) * COLS, :] = mm_tn(
            mixed[...], g_stream[:, cols]
        ).astype(bf16)
    advance(3, 0)
    along = mm(in_two(score_sum[...]), terms[...])
    along = in_two(along[:HEADS] + along[HEADS:])
    head_of = iota((8, COLS), 1) // HEAD_DIM
    g_query = col_sum(jnp.where(head_of == iota((8, COLS), 0) % HEADS, mm(along, wk[...]), 0.0)) * score_scale
    both_parts = mm_nt(in_two(jnp.broadcast_to(g_query, (HEADS, COLS))), wq[...])
    g_aq = both_parts[0:1, :] + both_parts[HEADS : HEADS + 1, :]
    for j in range(RING):
        put_aq[j] = jnp.broadcast_to(g_aq[:, j * COLS : (j + 1) * COLS], (8, COLS))
    aq_sent = [
        remote(put_aq.at[lax.rem(y + j, RING)], got_aq.at[j - 1],
               end_send.at[3, j - 1], end_recv.at[3, j - 1], j)
        for j in (2, 1, 3)
    ]
    for copy in aq_sent:
        copy.start()
    low_patch = grad_patch.astype(bf16)
    width = VARS * PATCH // RING
    r, c = iota((width, 4 * HALF), 1), iota((width, 4 * HALF), 0)
    for j in range(RING):
        pick_own = jnp.where(
            (c + width * j == PATCH * (r % HALF) + r // HALF) & (r % HALF < VARS), 1.0, 0.0
        ).astype(bf16)
        put_patch[j] = mm_nt(pick_own, low_patch).astype(bf16)
    patch_sent = [
        remote(put_patch.at[lax.rem(y + j, RING)], got_patch.at[j - 1],
               end_send.at[2, j - 1], end_recv.at[2, j - 1], j)
        for j in (2, 1, 3)
    ]
    for copy in patch_sent:
        copy.start()
    small[0:1, :] = col_sum(wide(g_own))
    small[5:6, :] = col_sum(wide(g_resid[:, own_cols]))
    small[6:7, :] = col_sum(wide(dy[:, own_cols]))
    small[12:32, :] = jnp.zeros((20, COLS), f32)
    arrived(gain_sent)
    small[1:5, :] = (put_gain[y] + got_gain[0] + got_gain[1] + got_gain[2])[0:4, :]

    def vector_copies(i):
        if i == 0:
            return [to_partner(rd_out.at[0], rd_in.at[0], rd_send.at[0], rd_recv.at[0], "core")]
        position, device = rings["xz"[i - 1]]
        return [
            pltpu.make_async_remote_copy(
                src_ref=rd_out.at[i], dst_ref=rd_in.at[3 * i - 3 + j],
                send_sem=rd_send.at[3 * i - 3 + j], recv_sem=rd_recv.at[3 * i - 3 + j],
                device_id=device(lax.rem(position + j, RING)), device_id_type=MESH,
            )
            for j in (2, 1, 3)
        ]

    def vector_step(i):
        if i == 0:
            arrived(aq_sent)
            small[7:8, :] = (put_aq[y] + got_aq[0] + got_aq[1] + got_aq[2])[0:1, :]
            rd_out[0] = small[...]
        else:
            arrived(vector_copies(i - 1))
            value = rd_out[i - 1]
            for j in range(1 if i == 1 else 3):
                value = value + rd_in[0 if i == 1 else 3 * i - 5 + j]
            if i == 3:
                total_small[...] = value
                copy = pltpu.make_async_copy(total_small, out_small, save_sem.at[8])
                copy.start()
                exports.append(copy)
                return
            rd_out[i] = value
        for copy in vector_copies(i):
            launch(copy)

    terms_base = AT_TERMS + pipe * 256

    def terms_gather(t):
        return ring_gather(
            share(terms_base, 256, ring_orders[0], t + 1), ring_orders[0][t], (extra_send, extra_recv), 3 * t
        )

    def terms_core():
        rows = rows_at(terms_base, 256)
        return to_partner(tot.at[rows], tot.at[rows], extra_send.at[6], extra_recv.at[6], "core")

    terms_sent = [
        remote(put_terms.at[lax.rem(y + j, RING)], got_terms.at[j - 1],
               end_send.at[4, j - 1], end_recv.at[4, j - 1], j)
        for j in (2, 1, 3)
    ]

    def terms_step(i):
        if i == 0:
            value_rows = tot[rows_at(*share_of(4, 0, 2)), :]
            score_rows = tot[rows_at(*share_of(4, 1, 2)), :]
            total = mm_nt(value_rows, wv[...]) + mm(score_rows[:, :128], kdir[...])
            for j in range(RING):
                put_terms[j] = total[:, j * COLS : (j + 1) * COLS].astype(bf16)
            for copy in terms_sent:
                launch(copy)
        elif i == 1:
            arrived(terms_sent)
            total = wide(put_terms[y]) + wide(got_terms[0]) + wide(got_terms[1]) + wide(got_terms[2])
            tot[rows_at(*share(terms_base, 256, ring_orders[0], 2)), :] = total.astype(bf16)
            for copy in terms_gather(1):
                launch(copy)
        elif i == 2:
            arrived(terms_gather(1))
            for copy in terms_gather(0):
                launch(copy)
        elif i == 3:
            arrived(terms_gather(0))
            launch(terms_core())
        else:
            terms_core().wait_recv()
            save(AT_TERMS, 512, 5).start()

    order = (
        (4, 1), (3, 1), (1, 6), (0, 7), (2, 3), "v", (4, 2), (3, 2), (1, 7), (0, 8), "v", (2, 4), (4, 3), "t",
        (3, 3), (1, 8), (0, 9), "v", (4, 4), "t", (3, 4), (2, 5), (1, 9), (0, 10), "v", (4, 5), "t", (3, 5),
        (2, 6), (1, 10), "t", (4, 6), (3, 6), "t",
    )
    next_of = {"t": 0, "v": 0}
    for step in order:
        if step == "t":
            terms_step(next_of["t"])
            next_of["t"] += 1
        elif step == "v":
            vector_step(next_of["v"])
            next_of["v"] += 1
        else:
            advance(*step)
    assert next_of == {"t": 5, "v": 4}
    arrived(patch_sent)
    patch_sum[...] = (
        wide(put_patch[y]) + wide(got_patch[0]) + wide(got_patch[1]) + wide(got_patch[2])
    )
    arrived(block_sent)
    exports += [
        pltpu.make_async_copy(patch_sum, out_patch, save_sem.at[9]),
        pltpu.make_async_copy(got_block, out_block, save_sem.at[10]),
    ]
    for copy in exports[-2:]:
        copy.start()
    for copy in started + block_sent + gain_sent + patch_sent + aq_sent:
        copy.wait_send()
    for i, (at, count) in enumerate(SEGMENTS + ((AT_TERMS, 512),)):
        save(at, count, i).wait()
    for copy in exports:
        copy.wait()


VMEM_LIMIT = 60 * 1024 * 1024


def run_chain(lengths, *args):
    hbm = pl.BlockSpec(memory_space=pl.ANY)
    V = pltpu.VMEM
    low = lambda *s: V(s, bf16)
    full = lambda *s: V(s, f32)
    scratch = [low(*w.shape) if w.shape[0] != LONGEST else low(128, COLS) for w in args]
    scratch += [
        full(VARS * PATCH, D), low(TERMS, D), low(HEADS * ROWS, TERMS), low(TERMS, COLS), full(8, TERMS),
        low(128, D), full(HEADS, ROWS, 128), full(ROWS, TERMS), low(ROWS, 128),
        low(5, ROWS, D), low(5, 3, OWN, D), full(OWN, D), low(ROWS, D), full(OWN, D),
        low(ROWS, D), low(ROWS, D), low(ROWS, D),
        low(ROWS, COLS), low(3, ROWS, COLS), full(HEADS * ROWS, ROWS), low(ROWS, COLS),
        low(ROWS, D), low(ROWS, D), low(HEADS * ROWS, COLS),
        low(ROWS, COLS), low(RING, OWN, COLS), low(3, 48, ROWS), low(RING, 48, ROWS),
        full(3, 8, COLS), full(RING, 8, COLS), full(SMALL, COLS), full(HEADS, TERMS),
        full(3, 8, COLS), full(RING, 8, COLS), low(3, 16, COLS), low(RING, 16, COLS),
        full(3, SMALL, COLS), full(7, SMALL, COLS), full(8, COLS), full(SMALL, COLS), full(48, ROWS),
        low(PAY, COLS), low(ALL, COLS), low(PAY * 31 // 32, COLS),
    ]
    dma = pltpu.SemaphoreType.DMA
    scratch += [
        dma((len(args),)), dma((5, 3)), dma((5, 3)), dma((4, 3)), dma((4, 3)), dma((5, 3)), dma((5, 3)),
        dma((5, 34)), dma((5, 34)), dma((7,)), dma((7,)), dma((7,)), dma((7,)), dma((11,)),
    ]
    return pl.pallas_call(
        chain,
        out_shape=(
            jax.ShapeDtypeStruct((ROWS, COLS), bf16),
            jax.ShapeDtypeStruct((48, ROWS), f32),
            jax.ShapeDtypeStruct((ALL, COLS), bf16),
            jax.ShapeDtypeStruct((TERMS, D), bf16),
            jax.ShapeDtypeStruct((SMALL, COLS), f32),
            jax.ShapeDtypeStruct((8, COLS), f32),
        ),
        in_specs=[pl.BlockSpec(memory_space=pltpu.SMEM)] + [hbm] * len(args),
        out_specs=[hbm] * 6,
        scratch_shapes=scratch,
        compiler_params=pltpu.CompilerParams(
            collective_id=0, has_side_effects=True, vmem_limit_bytes=VMEM_LIMIT
        ),
    )(lengths, *args)


VECTORS = (0, 7, 1, 2, 5, 3, 4, 6)


def finish(
    all_in, block_in, patch_in, terms_in, small_in, query_in, aq_from, hk,
    o_block, o_patch, o_down, o_up, o_out, o_qkv, o_wo, o_wv, o_wk, o_wq,
    o_pw, o_ve, o_pos, *rest,
):
    o_vectors, o_upbias = rest[:8], rest[8]
    (
        tot, wk, terms, small, query, aq_in, down, up, out, qkv, wo, gv, gk, gq, load_sem, save_sem,
    ) = rest[9:]
    spans = SEGMENTS + ((AT_TERMS, 512),)
    loads = [
        pltpu.make_async_copy(all_in.at[pl.ds(at, n)], tot.at[pl.ds(at, n)], load_sem.at[i])
        for i, (at, n) in enumerate(spans)
    ] + [
        pltpu.make_async_copy(src, dst, load_sem.at[6 + i])
        for i, (src, dst) in enumerate((
            (hk, wk), (terms_in, terms), (small_in, small), (query_in, query), (aq_from, aq_in)
        ))
    ]
    for copy in loads:
        copy.start()
    saves = [
        pltpu.make_async_copy(block_in, o_block, save_sem.at[8]),
        pltpu.make_async_copy(patch_in, o_patch, save_sem.at[9]),
    ]
    for copy in saves:
        copy.start()

    def store(i, src, dst):
        copy = pltpu.make_async_copy(src, dst, save_sem.at[i])
        copy.start()
        saves.append(copy)

    loads[0].wait()
    for j in range(RING):
        down[:, j * COLS : (j + 1) * COLS] = wide(tot[AT_DOWN + j * D : AT_DOWN + (j + 1) * D, :])
    store(4, down, o_down)
    loads[1].wait()
    for j in range(RING):
        up[:, j * COLS : (j + 1) * COLS] = wide(tot[AT_UP + j * D : AT_UP + (j + 1) * D, :])
    store(5, up, o_up)
    loads[2].wait()
    for j in range(3):
        qkv[j] = wide(tot[AT_QKV + j * D : AT_QKV + (j + 1) * D, :])
    store(6, qkv, o_qkv)
    for j in range(RING):
        out[:, j * COLS : (j + 1) * COLS] = wide(tot[AT_OUT + j * COLS : AT_OUT + (j + 1) * COLS, :])
    store(7, out, o_out)
    loads[3].wait()
    for j in range(RING):
        wo[:, j * COLS : (j + 1) * COLS] = wide(tot[AT_WO + j * COLS : AT_WO + (j + 1) * COLS, :])
    store(1, wo, o_wo)
    for copy in loads[4:]:
        copy.wait()
    value_sum = jnp.concatenate(
        [tot[AT_LAST : AT_LAST + 256, :], tot[AT_LAST + HALF_LAST : AT_LAST + HALF_LAST + 128, :]], axis=0
    )
    gv[...] = mm_tn(terms[...], value_sum)
    store(0, gv, o_wv)
    across = jnp.concatenate(
        [tot[score_place(n) : score_place(n) + 16, :128] for n in range(TERMS // 16)], axis=0
    )
    along = in_two(mm_tn(across, terms[...])[:HEADS, :])
    head_of = iota((8, COLS), 1) // HEAD_DIM
    mine = head_of == iota((8, COLS), 0) % HEADS
    block = jnp.where(mine, query[...], 0.0).astype(bf16)
    gk[...] = mm_tn(along, block) * score_scale
    store(2, gk, o_wk)
    g_query = col_sum(jnp.where(mine, mm(along, wk[...]), 0.0)) * score_scale
    row = iota((8, D), 0)
    aq = jnp.where(row < 2, jnp.broadcast_to(as_row(aq_in), (8, D)), 0.0).astype(bf16)
    high = wide(g_query.astype(bf16))
    both = jnp.where(
        iota((8, COLS), 0) == 0,
        jnp.broadcast_to(high, (8, COLS)), jnp.broadcast_to(g_query - high, (8, COLS)),
    ).astype(bf16)
    gq[...] = mm_tn(aq, both)
    store(3, gq, o_wq)
    o_pos[...] = wide(tot[AT_POS : AT_POS + LONGEST, :])
    for p in range(PATCH):
        o_pw[:, p, :] = wide(tot[AT_TERMS + HALF * p : AT_TERMS + HALF * p + VARS, :])
    o_ve[...] = wide(tot[AT_TERMS + 4 * HALF : AT_TERMS + 4 * HALF + VARS, :])
    for ref, i in zip(o_vectors, VECTORS):
        ref[0:1, :] = small[i : i + 1, :128]
        ref[1:2, :] = small[i : i + 1, 128:]
    for j in range(RING):
        o_upbias[2 * j : 2 * j + 1, :] = small[8 + j : 9 + j, :128]
        o_upbias[2 * j + 1 : 2 * j + 2, :] = small[8 + j : 9 + j, 128:]
    for copy in saves:
        copy.wait()


def run_finish(*args):
    vmem = pl.BlockSpec(memory_space=pltpu.VMEM)
    hbm = pl.BlockSpec(memory_space=pl.ANY)
    full = lambda *s: pltpu.VMEM(s, f32)
    shape = lambda *s: jax.ShapeDtypeStruct(s, f32)
    big = [(D, D), (D, D), (COLS, D), (3, D, COLS), (COLS, D), (D, COLS), (D, COLS), (D, COLS)]
    return pl.pallas_call(
        finish,
        out_shape=[jax.ShapeDtypeStruct((ROWS, COLS), bf16), shape(48, ROWS)]
        + [shape(*s) for s in big]
        + [shape(VARS, PATCH, COLS), shape(VARS, COLS), shape(LONGEST, COLS)]
        + [shape(2, 128)] * 8 + [shape(8, 128)],
        in_specs=[hbm] * 8,
        out_specs=[hbm] * 10 + [vmem] * 12,
        scratch_shapes=[
            pltpu.VMEM((ALL, COLS), bf16), pltpu.VMEM((D, COLS), bf16), pltpu.VMEM((TERMS, D), bf16),
            full(SMALL, COLS), full(8, COLS), pltpu.VMEM((8, 128), bf16),
            full(D, D), full(D, D), full(COLS, D), full(3, D, COLS), full(COLS, D),
            full(D, COLS), full(D, COLS), full(D, COLS),
            pltpu.SemaphoreType.DMA((11,)), pltpu.SemaphoreType.DMA((10,)),
        ],
        compiler_params=pltpu.CompilerParams(vmem_limit_bytes=VMEM_LIMIT),
    )(*args)


def shards(
    patches, item_lengths, cotangent, patch_weight, var_embed, agg_query, agg_wq, agg_wk, agg_wv,
    agg_wo, agg_bias, pos_table, first_gain, first_shift, attn_qkv, attn_out, attn_bias,
    second_gain, second_shift, mlp_up, up_bias, mlp_down, down_bias,
):
    tiled = lambda v: v.reshape(v.shape[0] // 128, 128)
    block, patch, summed, terms, small, query = run_chain(
        item_lengths, patches.T, patch_weight, var_embed, tiled(agg_query), tiled(first_gain),
        tiled(first_shift), tiled(attn_bias), tiled(second_gain), tiled(second_shift),
        tiled(down_bias), tiled(up_bias), tiled(agg_bias),
        agg_wq, agg_wk, agg_wv, agg_wo, pos_table, attn_qkv.transpose(1, 0, 2), attn_out,
        mlp_up, mlp_down, cotangent,
    )
    (
        block, patch, g_down, g_up, g_out, g_qkv, g_wo, g_wv, g_wk, g_wq, g_pw, g_ve, g_pos,
        g_agg_bias, g_aq, g_gain1, g_shift1, g_attn_bias, g_gain2, g_shift2, g_down_bias, g_up_bias,
    ) = run_finish(summed, block, patch, terms, small, query, tiled(agg_query), agg_wk)
    flat = lambda v: v.reshape(-1)
    return (
        block, patch.T, g_pw, g_ve, flat(g_aq), g_wq, g_wk, g_wv, g_wo, flat(g_agg_bias), g_pos,
        flat(g_gain1), flat(g_shift1), g_qkv.transpose(1, 0, 2), g_out, flat(g_attn_bias),
        flat(g_gain2), flat(g_shift2), g_up, flat(g_up_bias), g_down, flat(g_down_bias),
    )


def solution(mesh):
    rows = P(("dp", "pipe"), None)
    cols = P(None, "tensor")
    split = P("tensor", None)
    part = P("tensor")
    both = P(("dp", "pipe"), "tensor")
    last = P(None, None, "tensor")
    return jax.shard_map(
        shards,
        mesh=mesh,
        in_specs=(
            rows, P("dp", None), rows, P(), P(), P(), cols, cols, cols, split, part, cols, P(), P(),
            last, split, P(), P(), P(), cols, part, split, P(),
        ),
        out_specs=(
            both, both, last, cols, part, cols, cols, cols, split, part, cols, part, part, last,
            split, part, part, part, cols, part, split, part,
        ),
        check_vma=False,
    )
```

```python
import jax
import jax.numpy as jnp
from jax import lax
from jax.experimental import pallas as pl
from jax.experimental.pallas import tpu as pltpu
from jax.sharding import PartitionSpec as P

D = 1024
HEAD_DIM = 64
VARS = 48
PATCH = 4
LONGEST = 96
RING = 4
ROWS = 128
OWN = ROWS // RING
COLS = D // RING
HEADS = COLS // HEAD_DIM
HALF = 64
TERMS = 6 * HALF

AT_DOWN = 0
AT_UP = 4096
AT_OUT = 8192
AT_QKV = 9216
AT_WO = 12288
AT_LAST = 13312
PAY = 14336
AT_TERMS = PAY
ALL = PAY + 512
SEGMENTS = ((AT_DOWN, 4096), (AT_UP, 4096), (AT_OUT, 4096), (AT_WO, 1024), (AT_LAST, 1024))
CUBE = (True, True, False, False, False)
HALF_LAST = 512
AT_POS = AT_LAST + HALF_LAST + 128
SMALL = 32

norm_eps = 1e-05
root_half = 0.7071067811865476
inv_root_tau = 0.3989422804014327
score_scale = HEAD_DIM ** (-0.5)
highest = lax.Precision.HIGHEST
f32 = jnp.float32
bf16 = jnp.bfloat16
MESH = pl.DeviceIdType.MESH


def wide(v):
    return v.astype(f32)


def dot(left, right, dims, precision=None):
    return lax.dot_general(left, right, (dims, ((), ())), precision=precision, preferred_element_type=f32)


def mm(a, b, **kw):
    return dot(a, b, ((1,), (0,)), **kw)


def mm_nt(a, b, **kw):
    return dot(a, b, ((1,), (1,)), **kw)


def mm_tn(a, b, **kw):
    return dot(a, b, ((0,), (0,)), **kw)


def iota(shape, axis):
    return lax.broadcasted_iota(jnp.int32, shape, axis)


def norm_parts(x):
    centred = x - jnp.mean(x, axis=-1, keepdims=True)
    inverse = lax.rsqrt(jnp.mean(centred * centred, axis=-1, keepdims=True) + norm_eps)
    return centred * inverse, inverse


def norm_back(grad, xhat, inverse, gain):
    scaled = grad * gain
    return inverse * (
        scaled
        - jnp.mean(scaled, axis=-1, keepdims=True)
        - xhat * jnp.mean(scaled * xhat, axis=-1, keepdims=True)
    )


def col_sum(a):
    return jnp.sum(a, axis=0, keepdims=True)


WEIGHTS = (
    "patches", "pw", "ve", "aq", "gain1", "shift1", "abias", "gain2", "shift2", "dbias", "ubias", "aggbias",
    "wq", "wk", "wv", "wo", "pos", "wqkv", "wout", "wup", "wdown", "dy",
)
EARLY = ("aq", "wq", "pw", "ve", "wk", "wv", "patches", "wo", "pos", "aggbias")


def as_row(ref):
    value = wide(ref[...])
    return jnp.concatenate([value[i : i + 1, :] for i in range(value.shape[0])], axis=1)


def in_two(value):
    high = wide(value.astype(bf16))
    return jnp.concatenate([high, value - high], axis=0).astype(bf16)


def score_place(n):
    c, j = n // 16, n % 16
    return AT_LAST + c * HALF_LAST + 256 + 16 * (4 * (j % 4) + j // 4)


POINTS = {
    "up": ((0, 1), (1, 1)),
    "e2": (),
    "block": ((0, 2),),
    "out": ((0, 3), (1, 2), (2, 1), (0, 4)),
    "e1": ((1, 3),),
    "last": ((1, 4), (2, 2), (0, 5)),
    "wo": ((4, 1),),
}
TAIL = (
    (1, 5), (3, 1), (0, 6), (2, 3), "v", (1, 6), (4, 2), "v", (3, 2), (0, 7), (2, 4), (1, 7), (4, 3), "t", "v",
    (3, 3), (0, 8), "t", (2, 5), (1, 8), (4, 4), "v", (3, 4), (2, 6), (0, 9), "t", (1, 9), (0, 10), (4, 5),
    (1, 10), "t", (3, 5), (4, 6), "t", (3, 6),
)


def chain(
    lengths, hpatches, hpw, hve, haq, hgain1, hshift1, habias, hgain2, hshift2, hdbias,
    hubias, haggbias,
    hq, hk, hv, ho, hpos, hqkv, hout, hup, hdown, hdy,
    out_block, out_patch, out_all, out_terms, out_small, out_query,
    patches, pw, ve, aq_in, gain1_in, shift1_in, abias_in, gain2_in, shift2_in, dbias_in,
    ubias_in, aggbias_in,
    wq, wk, wv, wo, pos, wqkv, wout, wup, wdown, dy,
    pwf, terms, shares, vterms, kterms, kdir, soft, x3, onehot,
    part, rs_in, stream, normed, resid, normed2, g_resid, g_stream,
    mixed, qkv, probs, attended, active, g_pre, masked,
    got_block, put_block, got_patch, put_patch, got_gain, put_gain, small, score_sum,
    got_aq, put_aq, got_terms, put_terms, rd_out, rd_in, query_row, total_small, patch_sum,
    pay, tot, sum_in,
    load_sem, y_send, rs_recv, ag_recv, end_recv, sum_send, sum_recv, extra_recv, rd_recv, other_send, save_sem,
):
    y = lax.axis_index("tensor")
    pipe = lax.axis_index("pipe")
    dp = lax.axis_index("dp")
    x, z = lax.rem(dp, 4), dp // 4
    own_rows = pl.ds(pl.multiple_of(y * OWN, OWN), OWN)
    own_cols = pl.ds(pl.multiple_of(y * COLS, COLS), COLS)
    barrier = pltpu.get_barrier_semaphore()
    rings = {"x": (x, lambda q: {"dp": 4 * z + q}), "z": (z, lambda q: {"dp": 4 * q + x})}
    neighbours = [{"pipe": 1 - pipe}]
    for j in (1, 2, 3):
        neighbours.append({"tensor": lax.rem(y + j, RING)})
        neighbours += [at(lax.rem(p + j, RING)) for p, at in rings.values()]
    for device in neighbours:
        pl.semaphore_signal(barrier, inc=1, device_id=device, device_id_type=MESH)
    dims = {
        "core": (pipe, {"pipe": 1 - pipe}),
        "xa": (lax.rem((x + 1) // 2, 2), {"dp": dp + 1 - 2 * lax.rem(x, 2)}),
        "xb": (x // 2, {"dp": 4 * z + 3 - x}),
        "za": (lax.rem((z + 1) // 2, 2), {"dp": dp + 4 - 8 * lax.rem(z, 2)}),
        "zb": (z // 2, {"dp": 4 * (3 - z) + x}),
    }
    ring = ("xa", "za", "xb", "zb")
    orders = [ring[k:] + ring[:k] for k in range(4)]
    ring_orders = (("x", "z"), ("z", "x"))
    loads = {
        name: pltpu.make_async_copy(src, dst, load_sem.at[i])
        for i, (name, src, dst) in enumerate(zip(
            WEIGHTS,
            (hpatches, hpw, hve, haq, hgain1, hshift1, habias, hgain2, hshift2, hdbias, hubias, haggbias,
             hq, hk, hv, ho, hpos, hqkv, hout, hup, hdown, hdy),
            (patches, pw, ve, aq_in, gain1_in, shift1_in, abias_in, gain2_in, shift2_in, dbias_in,
             ubias_in, aggbias_in,
             wq, wk, wv, wo, pos.at[pl.ds(0, LONGEST)], wqkv, wout, wup, wdown, dy),
        ))
    }
    for name in EARLY + tuple(name for name in WEIGHTS if name not in EARLY):
        loads[name].start()

    def wait_for(like, sem):
        pltpu.make_async_copy(like, like, sem).wait()

    def wait_rows(count, sem):
        wait_for(tot.at[pl.ds(0, count)], sem)

    sent_rows = [0] * len(SEGMENTS)

    def to_partner(src, dst, send, recv, dim):
        return pltpu.make_async_remote_copy(
            src_ref=src, dst_ref=dst, send_sem=send, recv_sem=recv,
            device_id=dims[dim][1], device_id_type=MESH,
        )

    def rows_at(start, length):
        return pl.ds(pl.multiple_of(start, 16), length)

    def region(base, length, order, steps):
        for dim in order[:steps]:
            length //= 2
            base = base + dims[dim][0] * length
        return base, length

    def part_of(seg, k, steps):
        at, count = SEGMENTS[seg]
        return region(at + pipe * (count // 2) + k * (count // 8), count // 8, orders[k], steps)

    in_at = {}
    place_in = 0
    for seg, (_, count) in enumerate(SEGMENTS):
        in_at[seg, "core"] = place_in
        place_in += count // 2
        for s in range(4):
            for k in range(4):
                if CUBE[seg]:
                    in_at[seg, s, k] = place_in
                    place_in += count // 16 >> s
        for s in range(2):
            for k in range(2):
                if not CUBE[seg]:
                    in_at[seg, s, k] = place_in
                    place_in += 3 * (count // 16 >> 2 * s)
    assert place_in <= sum_in.shape[0]

    def core_halving(seg):
        at, count = SEGMENTS[seg]
        half = count // 2
        return to_partner(
            pay.at[rows_at(at + (1 - pipe) * half, half)], sum_in.at[pl.ds(in_at[seg, "core"], half)],
            sum_send.at[seg], sum_recv.at[seg, 0], "core",
        )

    def halving(seg, s, k):
        base, length = part_of(seg, k, s)
        dim = orders[k][s]
        length //= 2
        return to_partner(
            pay.at[rows_at(base + (1 - dims[dim][0]) * length, length)],
            sum_in.at[pl.ds(in_at[seg, s, k], length)], sum_send.at[seg], sum_recv.at[seg, 1 + s], dim,
        )

    def doubling(seg, t, k):
        rows = rows_at(*part_of(seg, k, t + 1))
        return to_partner(
            tot.at[rows], tot.at[rows], sum_send.at[seg], sum_recv.at[seg, 5 + t], orders[k][t]
        )

    def core_doubling(seg):
        at, count = SEGMENTS[seg]
        rows = rows_at(at + pipe * (count // 2), count // 2)
        return to_partner(tot.at[rows], tot.at[rows], sum_send.at[seg], sum_recv.at[seg, 9], "core")

    def ring_copy(src_rows, src, dst, sems, dim, j):
        position, device = rings[dim]
        return pltpu.make_async_remote_copy(
            src_ref=src.at[src_rows], dst_ref=dst, send_sem=sems[0], recv_sem=sems[1],
            device_id=device(lax.rem(position + j, RING)), device_id_type=MESH,
        )

    def share(base, length, order, steps):
        for dim in order[:steps]:
            length //= RING
            base = base + rings[dim][0] * length
        return base, length

    def share_of(seg, k, steps):
        at, count = SEGMENTS[seg]
        return share(at + pipe * (count // 2) + k * (count // 4), count // 4, ring_orders[k], steps)

    def ring_scatter(seg, s, k):
        base, length = share_of(seg, k, s)
        length //= RING
        dim = ring_orders[k][s]
        position = rings[dim][0]
        sems = (sum_send.at[seg], sum_recv.at[seg, 1 + s])
        return [
            ring_copy(
                rows_at(base + lax.rem(position + j, RING) * length, length), pay,
                sum_in.at[pl.ds(in_at[seg, s, k] + (j - 1) * length, length)],
                sems, dim, j,
            )
            for j in (2, 1, 3)
        ]

    def ring_gather(base_length, dim, sems):
        rows = rows_at(*base_length)
        return [ring_copy(rows, tot, tot.at[rows], sems, dim, j) for j in (2, 1, 3)]

    def ring_gather_of(seg, t, k):
        sems = (sum_send.at[seg], sum_recv.at[seg, 3 + t])
        return ring_gather(share_of(seg, k, t + 1), ring_orders[k][t], sems)

    def launch_all(seg, copies, rows):
        for copy in copies:
            copy.start()
        sent_rows[seg] += len(copies) * rows

    def ring_advance(seg, stage):
        at, count = SEGMENTS[seg]
        half, quarter = count // 2, count // 4
        if stage == 0:
            launch_all(seg, [core_halving(seg)], half)
        elif stage == 1:
            wait_rows(half, sum_recv.at[seg, 0])
            for k in range(2):
                rows = rows_at(at + pipe * half + k * quarter, quarter)
                came = pl.ds(in_at[seg, "core"] + k * quarter, quarter)
                pay[rows, :] = pay[rows, :] + sum_in[came, :]
                launch_all(seg, ring_scatter(seg, 0, k), quarter // 4)
        elif stage <= 3:
            s = stage - 2
            length = quarter >> 2 * (s + 1)
            wait_rows(6 * length, sum_recv.at[seg, 1 + s])
            for k in range(2):
                rows = rows_at(*share_of(seg, k, s + 1))
                total = wide(pay[rows, :])
                for j in range(3):
                    total = total + wide(sum_in[pl.ds(in_at[seg, s, k] + j * length, length), :])
                if s == 0:
                    pay[rows, :] = total.astype(bf16)
                    launch_all(seg, ring_scatter(seg, 1, k), length // 4)
                else:
                    tot[rows, :] = total.astype(bf16)
                    launch_all(seg, ring_gather_of(seg, 1, k), length)
        elif stage <= 5:
            t = 5 - stage
            length = quarter >> 2 * (t + 1)
            wait_rows(6 * length, sum_recv.at[seg, 3 + t])
            if t:
                for k in range(2):
                    launch_all(seg, ring_gather_of(seg, 0, k), quarter // 4)
            else:
                launch_all(seg, [core_doubling(seg)], half)
        else:
            wait_rows(half, sum_recv.at[seg, 9])
            save(at, count, seg).start()

    def save(at, count, i):
        return pltpu.make_async_copy(tot.at[pl.ds(at, count)], out_all.at[pl.ds(at, count)], save_sem.at[i])

    def advance(seg, stage):
        if not CUBE[seg]:
            return ring_advance(seg, stage)
        at, count = SEGMENTS[seg]
        half, quarter = count // 2, count // 8
        if stage == 0:
            launch_all(seg, [core_halving(seg)], half)
        elif stage == 1:
            wait_rows(half, sum_recv.at[seg, 0])
            for k in range(4):
                rows = rows_at(at + pipe * half + k * quarter, quarter)
                came = pl.ds(in_at[seg, "core"] + k * quarter, quarter)
                pay[rows, :] = pay[rows, :] + sum_in[came, :]
                launch_all(seg, [halving(seg, 0, k)], quarter // 2)
        elif stage <= 5:
            s = stage - 2
            length = quarter >> (s + 1)
            wait_rows(4 * length, sum_recv.at[seg, 1 + s])
            for k in range(4):
                rows = rows_at(*part_of(seg, k, s + 1))
                total = pay[rows, :] + sum_in[pl.ds(in_at[seg, s, k], length), :]
                if s < 3:
                    pay[rows, :] = total
                    launch_all(seg, [halving(seg, s + 1, k)], length // 2)
                else:
                    tot[rows, :] = total
                    launch_all(seg, [doubling(seg, 3, k)], length)
        elif stage <= 9:
            t = 9 - stage
            length = quarter >> (t + 1)
            wait_rows(4 * length, sum_recv.at[seg, 5 + t])
            if t:
                for k in range(4):
                    launch_all(seg, [doubling(seg, t - 1, k)], 2 * length)
            else:
                launch_all(seg, [core_doubling(seg)], half)
        else:
            wait_rows(half, sum_recv.at[seg, 9])
            save(at, count, seg).start()

    def point(name):
        for seg, stage in POINTS[name]:
            advance(seg, stage)

    def remote(src, dst, send, recv, j):
        return pltpu.make_async_remote_copy(
            src_ref=src, dst_ref=dst, send_sem=send, recv_sem=recv,
            device_id={"tensor": lax.rem(y + j, RING)}, device_id_type=MESH,
        )

    def rows_of(j):
        return pl.ds(pl.multiple_of(lax.rem(y + j, RING) * OWN, OWN), OWN)

    def scatter(phase):
        for j in (2, 1, 3):
            remote(part.at[phase, rows_of(j)], rs_in.at[phase, j - 1], y_send.at[0], rs_recv.at[phase], j).start()

    def scattered(phase):
        total = wide(part[phase, own_rows, :])
        wait_for(rs_in.at[phase], rs_recv.at[phase])
        for j in range(3):
            total = total + wide(rs_in[phase, j])
        return total

    def gather(phase, full):
        for j in (2, 1, 3):
            remote(full.at[own_rows], full.at[own_rows], y_send.at[1], ag_recv.at[phase], j).start()

    def gathered(phase):
        wait_for(part.at[phase, pl.ds(0, 3 * OWN)], ag_recv.at[phase])

    def exchange(i, put, got):
        for j in (2, 1, 3):
            remote(put.at[lax.rem(y + j, RING)], got.at[j - 1], y_send.at[2 + i], end_recv.at[i], j).start()

    for c in range(2):
        at = AT_LAST + c * HALF_LAST
        pay[at : at + HALF_LAST, :] = jnp.zeros((HALF_LAST, COLS), bf16)

    first, second = lengths[pipe, 0], lengths[pipe, 1]
    both = first + second

    def segment_of(r):
        return (r >= first).astype(jnp.int32) + (r >= both).astype(jnp.int32)

    same_item = segment_of(iota((ROWS, ROWS), 0)) == segment_of(iota((ROWS, ROWS), 1))
    row = iota((ROWS, 128), 0)
    place = row - jnp.where(row >= first, first, 0) - jnp.where(row >= both, second, 0)
    onehot[...] = jnp.where(place == iota((ROWS, 128), 1), 1.0, 0.0).astype(bf16)
    pos[LONGEST:, :] = jnp.zeros((128 - LONGEST, COLS), bf16)

    loads["pw"].wait()
    loads["ve"].wait()
    r, c = iota((4 * HALF, VARS * PATCH), 0), iota((4 * HALF, VARS * PATCH), 1)
    pick = jnp.where((c == PATCH * (r % HALF) + r // HALF) & (r % HALF < VARS), 1.0, 0.0).astype(bf16)
    for v in range(VARS):
        pwf[PATCH * v : PATCH * (v + 1), :] = wide(pw[v])
    terms[: 4 * HALF, :] = mm(pick, pwf[...].astype(bf16)).astype(bf16)
    terms[4 * HALF : 4 * HALF + VARS, :] = ve[...]
    terms[4 * HALF + VARS :, :] = jnp.zeros((TERMS - 4 * HALF - VARS, D), bf16)
    r, c = iota((VARS * PATCH, 4 * HALF), 1), iota((VARS * PATCH, 4 * HALF), 0)
    pick_back = jnp.where((c == PATCH * (r % HALF) + r // HALF) & (r % HALF < VARS), 1.0, 0.0).astype(bf16)
    loads["patches"].wait()
    x3[:, : 4 * HALF] = mm_tn(patches[...], pick_back)
    lane = iota((ROWS, 128), 1)
    x3[:, 4 * HALF :] = jnp.where(lane < VARS, 1.0, 0.0)

    loads["wq"].wait()
    loads["aq"].wait()
    aq_row = as_row(aq_in)
    query = mm(jnp.broadcast_to(aq_row, (8, D)).astype(bf16), wq[...])[0:1, :].astype(bf16)
    query_row[...] = jnp.broadcast_to(wide(query), (8, COLS))
    exports = [
        pltpu.make_async_copy(query_row, out_query, save_sem.at[6]),
        pltpu.make_async_copy(terms, out_terms, save_sem.at[7]),
    ]
    for copy in exports:
        copy.start()
    head_of = iota((8, COLS), 1) // HEAD_DIM
    block = jnp.where(
        head_of == iota((8, COLS), 0) % HEADS, jnp.broadcast_to(wide(query), (8, COLS)), 0.0
    ).astype(bf16)
    loads["wk"].wait()
    key_dir = mm_nt(block, wk[...]) * score_scale
    split = in_two(key_dir[:HEADS, :])
    kdir[...] = jnp.concatenate([wide(split), jnp.zeros((120, D), f32)], axis=0).astype(bf16)
    key_parts = mm_nt(split, terms[...])
    kterms[...] = key_parts + pltpu.roll(key_parts, HEADS, 0)
    loads["wv"].wait()
    vterms[...] = mm(terms[...], wv[...]).astype(bf16)

    def fold(v):
        folded = v[:, :128] + v[:, 128:256] + v[:, 256:]
        return folded + pltpu.roll(folded, HALF, 1)

    def thrice(v):
        return jnp.concatenate([v, v, v], axis=1)

    for h in range(HEADS):
        scores = fold(x3[...] * kterms[h : h + 1, :])
        scores = jnp.where(lane % HALF < VARS, scores, -1e30)
        raised = jnp.exp(scores - jnp.max(scores, axis=-1, keepdims=True))
        weights = raised / (0.5 * jnp.sum(raised, axis=-1, keepdims=True))
        soft[h] = weights
        shares[h * ROWS : (h + 1) * ROWS, :] = (x3[...] * thrice(weights)).astype(bf16)

    col_head = iota((ROWS, COLS), 1) // HEAD_DIM

    def pick_heads(stacked):
        total = jnp.zeros((ROWS, COLS), f32)
        for h in range(HEADS):
            total = jnp.where(col_head == h, stacked[h * ROWS : (h + 1) * ROWS, :], total)
        return total

    def spread_heads(value):
        for h in range(HEADS):
            masked[h * ROWS : (h + 1) * ROWS, :] = jnp.where(col_head == h, value, 0.0).astype(bf16)

    mixed[...] = pick_heads(mm(shares[...], vterms[...])).astype(bf16)
    loads["wo"].wait()
    loads["pos"].wait()
    loads["aggbias"].wait()
    aggbias_row = as_row(aggbias_in)
    for j in range(RING):
        cols = slice(j * COLS, (j + 1) * COLS)
        part[0, :, cols] = mm(mixed[...], wo[:, cols]).astype(bf16)
    extra = mm(mixed[...], wo[:, own_cols]) + mm(onehot[...], pos[...]) + aggbias_row
    part[0, :, own_cols] = extra.astype(bf16)
    pl.semaphore_wait(barrier, len(neighbours))
    scatter(0)
    for name in ("gain1", "shift1", "abias", "gain2", "shift2", "dbias", "ubias"):
        loads[name].wait()
    gain1_row, shift1_row = as_row(gain1_in), as_row(shift1_in)
    abias_row, gain2_row, shift2_row = as_row(abias_in), as_row(gain2_in), as_row(shift2_in)
    dbias_row, ubias_row = as_row(dbias_in), as_row(ubias_in)
    stream_own = wide(scattered(0).astype(bf16))
    xhat1, inv1 = norm_parts(stream_own)
    normed[own_rows, :] = (xhat1 * gain1_row + shift1_row).astype(bf16)
    stream[...] = stream_own
    gather(0, normed)
    loads["wqkv"].wait()
    gathered(0)

    for j in range(3):
        qkv[j] = mm(normed[...], wqkv[j]).astype(bf16)
    spread_heads(qkv[0])
    raw = mm_nt(masked[...], qkv[1]) * score_scale
    for h in range(HEADS):
        rows = slice(h * ROWS, (h + 1) * ROWS)
        score = jnp.where(same_item, raw[rows, :], -1e30)
        raised = jnp.exp(score - jnp.max(score, axis=-1, keepdims=True))
        probs[rows, :] = raised / jnp.sum(raised, axis=-1, keepdims=True)
    attended[...] = pick_heads(mm(probs[...].astype(bf16), qkv[2])).astype(bf16)
    loads["wout"].wait()
    for j in range(RING):
        cols = slice(j * COLS, (j + 1) * COLS)
        part[1, :, cols] = mm(attended[...], wout[:, cols]).astype(bf16)
    scatter(1)
    resid_own = stream[...] + scattered(1) + abias_row
    xhat2, inv2 = norm_parts(resid_own)
    normed2[own_rows, :] = (xhat2 * gain2_row + shift2_row).astype(bf16)
    resid[...] = resid_own
    gather(1, normed2)
    loads["wup"].wait()
    loads["wdown"].wait()
    loads["dy"].wait()
    gathered(1)

    for j in range(RING):
        cols = slice(j * COLS, (j + 1) * COLS)
        pre = mm(normed2[...], wup[:, cols]) + ubias_row[:, cols]
        half_cdf = 0.5 * (1.0 + lax.erf(pre * root_half))
        active[:, cols] = (pre * half_cdf).astype(bf16)
        slope = half_cdf + pre * jnp.exp(-0.5 * pre * pre) * inv_root_tau
        grad = (mm_nt(dy[...], wdown[cols, :]) * slope).astype(bf16)
        g_pre[:, cols] = grad
        small[8 + j : 9 + j, :] = col_sum(wide(grad))
    for j in range(RING):
        rows = slice(j * COLS, (j + 1) * COLS)
        part[3, :, rows] = mm_nt(g_pre[...], wup[rows, :]).astype(bf16)
    scatter(3)
    for j in range(RING):
        cols = slice(j * COLS, (j + 1) * COLS)
        part[2, :, cols] = mm(active[...], wdown[:, cols]).astype(bf16)
    scatter(2)
    for j in range(RING):
        cols = slice(j * COLS, (j + 1) * COLS)
        pay[AT_DOWN + j * D : AT_DOWN + (j + 1) * D, :] = mm_tn(active[...], dy[:, cols]).astype(bf16)
    advance(0, 0)
    for j in range(RING):
        cols = slice(j * COLS, (j + 1) * COLS)
        pay[AT_UP + j * D : AT_UP + (j + 1) * D, :] = mm_tn(normed2[...], g_pre[:, cols]).astype(bf16)
    advance(1, 0)
    point("up")
    e2 = scattered(3)
    g_resid_own = (wide(dy[own_rows, :]) + norm_back(e2, xhat2, inv2, gain2_row)).astype(bf16)
    g_resid[own_rows, :] = g_resid_own
    gather(2, g_resid)
    point("e2")
    result = resid[...] + scattered(2) + dbias_row
    gain2, shift2 = col_sum(e2 * xhat2), col_sum(e2)
    for j in range(RING):
        put_block[j] = result[:, j * COLS : (j + 1) * COLS].astype(bf16)
    for j in (2, 1, 3):
        remote(put_block.at[lax.rem(y + j, RING)], got_block.at[own_rows], y_send.at[2], end_recv.at[0], j).start()
    got_block[own_rows, :] = put_block[y]
    point("block")
    gathered(2)

    spread_heads(mm_nt(g_resid[...], wout[...]).astype(bf16))
    g_probs = mm_nt(masked[...], qkv[2])
    g_v = mm_tn(probs[...].astype(bf16), masked[...]).astype(bf16)
    p = probs[...]
    g_scores = (p * (g_probs - jnp.sum(p * g_probs, axis=-1, keepdims=True))).astype(bf16)
    g_q = (pick_heads(mm(g_scores, qkv[1])) * score_scale).astype(bf16)
    spread_heads(qkv[0])
    g_k = (mm_tn(g_scores, masked[...]) * score_scale).astype(bf16)
    for j in range(RING):
        rows = slice(j * COLS, (j + 1) * COLS)
        total = mm_nt(g_q, wqkv[0, rows, :]) + mm_nt(g_k, wqkv[1, rows, :])
        part[4, :, rows] = (total + mm_nt(g_v, wqkv[2, rows, :])).astype(bf16)
    scatter(4)
    for j, g in enumerate((g_q, g_k, g_v)):
        pay[AT_QKV + j * D : AT_QKV + (j + 1) * D, :] = mm_tn(normed[...], g).astype(bf16)
    for j in range(RING):
        cols = slice(j * COLS, (j + 1) * COLS)
        pay[AT_OUT + j * COLS : AT_OUT + (j + 1) * COLS, :] = mm_tn(
            attended[...], g_resid[:, cols]
        ).astype(bf16)
    advance(2, 0)
    point("out")
    e1 = scattered(4)
    g_stream_own = (
        wide(g_resid[own_rows, :]) + norm_back(e1, xhat1, inv1, gain1_row)
    ).astype(bf16)
    g_stream[own_rows, :] = g_stream_own
    gather(3, g_stream)
    gain1, shift1 = col_sum(e1 * xhat1), col_sum(e1)
    for j in range(RING):
        cols = slice(j * COLS, (j + 1) * COLS)
        for i, v in enumerate((gain1, shift1, gain2, shift2)):
            put_gain[j, i : i + 1, :] = v[:, cols]
        put_gain[j, 4:8, :] = jnp.zeros((4, COLS), f32)
    exchange(1, put_gain, got_gain)
    point("e1")
    gathered(3)

    spread_heads(mm_nt(g_stream[...], wo[...]).astype(bf16))
    by_term = mm_nt(masked[...], vterms[...])
    grad_patch = jnp.zeros((ROWS, 4 * HALF), f32)
    for h in range(HEADS):
        mine = by_term[h * ROWS : (h + 1) * ROWS, :]
        weights = soft[h]
        g_weights = fold(x3[...] * mine)
        g_sc = weights * (
            g_weights - 0.5 * jnp.sum(weights * g_weights, axis=-1, keepdims=True)
        )
        g_sc2 = jnp.concatenate([g_sc, g_sc], axis=1)
        w2 = jnp.concatenate([weights, weights], axis=1)
        grad_patch = grad_patch + g_sc2 * kterms[h : h + 1, : 4 * HALF] + w2 * mine[:, : 4 * HALF]
        sums = col_sum(x3[...] * thrice(g_sc))
        score_sum[h : h + 1, :] = sums
    value_sum = mm_tn(shares[...], masked[...]).astype(bf16)
    pay[AT_LAST : AT_LAST + 256, :] = value_sum[:256, :]
    pay[AT_LAST + HALF_LAST : AT_LAST + HALF_LAST + 128, :] = value_sum[256:, :]
    head_cols = iota((HEADS, COLS), 1)
    spot = jnp.where((head_cols % HEADS == iota((HEADS, COLS), 0)) & (head_cols < 8), 1.0, 0.0).astype(bf16)
    across = mm_tn(score_sum[...].astype(bf16), spot).astype(bf16)
    for n in range(TERMS // 16):
        at = score_place(n)
        pay[at : at + 16, :] = across[16 * n : 16 * (n + 1), :]
    g_own = g_stream[:, own_cols]
    pay[AT_POS : AT_POS + LONGEST, :] = mm_tn(onehot[...], g_own)[:LONGEST, :].astype(bf16)
    advance(4, 0)
    point("last")
    for j in range(RING):
        cols = slice(j * COLS, (j + 1) * COLS)
        pay[AT_WO + j * COLS : AT_WO + (j + 1) * COLS, :] = mm_tn(
            mixed[...], g_stream[:, cols]
        ).astype(bf16)
    advance(3, 0)
    point("wo")
    along = mm(in_two(score_sum[...]), terms[...])
    along = in_two(along[:HEADS] + along[HEADS:])
    head_of = iota((8, COLS), 1) // HEAD_DIM
    g_query = col_sum(jnp.where(head_of == iota((8, COLS), 0) % HEADS, mm(along, wk[...]), 0.0)) * score_scale
    both_parts = mm_nt(in_two(jnp.broadcast_to(g_query, (HEADS, COLS))), wq[...])
    g_aq = both_parts[0:1, :] + both_parts[HEADS : HEADS + 1, :]
    for j in range(RING):
        put_aq[j] = jnp.broadcast_to(g_aq[:, j * COLS : (j + 1) * COLS], (8, COLS))
    exchange(3, put_aq, got_aq)
    low_patch = grad_patch.astype(bf16)
    width = VARS * PATCH // RING
    r, c = iota((width, 4 * HALF), 1), iota((width, 4 * HALF), 0)
    for j in range(RING):
        pick_own = jnp.where(
            (c + width * j == PATCH * (r % HALF) + r // HALF) & (r % HALF < VARS), 1.0, 0.0
        ).astype(bf16)
        put_patch[j] = mm_nt(pick_own, low_patch).astype(bf16)
    exchange(2, put_patch, got_patch)
    small[0:1, :] = col_sum(wide(g_own))
    small[5:6, :] = col_sum(wide(g_resid[:, own_cols]))
    small[6:7, :] = col_sum(wide(dy[:, own_cols]))
    small[12:32, :] = jnp.zeros((20, COLS), f32)
    wait_for(got_gain, end_recv.at[1])
    small[1:5, :] = (put_gain[y] + got_gain[0] + got_gain[1] + got_gain[2])[0:4, :]

    def vector_step(i):
        if i == 0:
            wait_for(got_aq, end_recv.at[3])
            small[7:8, :] = (put_aq[y] + got_aq[0] + got_aq[1] + got_aq[2])[0:1, :]
            rd_out[0] = small[...]
            to_partner(rd_out.at[0], rd_in.at[0], other_send.at[0], rd_recv.at[0], "core").start()
            return
        at, n = (0, 1) if i == 1 else (3 * i - 5, 3)
        wait_for(rd_in.at[pl.ds(at, n)], rd_recv.at[i - 1])
        value = rd_out[i - 1]
        for j in range(n):
            value = value + rd_in[at + j]
        if i == 3:
            total_small[...] = value
            copy = pltpu.make_async_copy(total_small, out_small, save_sem.at[8])
            copy.start()
            exports.append(copy)
            return
        rd_out[i] = value
        position, device = rings["xz"[i - 1]]
        for j in (2, 1, 3):
            pltpu.make_async_remote_copy(
                src_ref=rd_out.at[i], dst_ref=rd_in.at[3 * i - 3 + j], send_sem=other_send.at[0],
                recv_sem=rd_recv.at[i], device_id=device(lax.rem(position + j, RING)), device_id_type=MESH,
            ).start()

    terms_base = AT_TERMS + pipe * 256

    def terms_gather(t):
        dim = ring_orders[0][t]
        for copy in ring_gather(
            share(terms_base, 256, ring_orders[0], t + 1), dim, (other_send.at[1], extra_recv.at[t])
        ):
            copy.start()

    def terms_step(i):
        if i == 0:
            value_rows = tot[rows_at(*share_of(4, 0, 2)), :]
            score_rows = tot[rows_at(*share_of(4, 1, 2)), :]
            total = mm_nt(value_rows, wv[...]) + mm(score_rows[:, :128], kdir[...])
            for j in range(RING):
                put_terms[j] = total[:, j * COLS : (j + 1) * COLS].astype(bf16)
            exchange(4, put_terms, got_terms)
        elif i == 1:
            wait_for(got_terms, end_recv.at[4])
            total = wide(put_terms[y]) + wide(got_terms[0]) + wide(got_terms[1]) + wide(got_terms[2])
            tot[rows_at(*share(terms_base, 256, ring_orders[0], 2)), :] = total.astype(bf16)
            terms_gather(1)
        elif i == 2:
            wait_rows(48, extra_recv.at[1])
            terms_gather(0)
        elif i == 3:
            wait_rows(192, extra_recv.at[0])
            rows = rows_at(terms_base, 256)
            to_partner(tot.at[rows], tot.at[rows], other_send.at[1], extra_recv.at[2], "core").start()
        else:
            wait_rows(256, extra_recv.at[2])
            save(AT_TERMS, 512, 5).start()

    next_of = {"t": 0, "v": 0}
    for step in TAIL:
        if step == "t":
            terms_step(next_of["t"])
            next_of["t"] += 1
        elif step == "v":
            vector_step(next_of["v"])
            next_of["v"] += 1
        else:
            advance(*step)
    assert next_of == {"t": 5, "v": 4}
    wait_for(got_patch, end_recv.at[2])
    patch_sum[...] = (
        wide(put_patch[y]) + wide(got_patch[0]) + wide(got_patch[1]) + wide(got_patch[2])
    )
    wait_for(pay.at[pl.ds(0, 3 * OWN)], end_recv.at[0])
    exports += [
        pltpu.make_async_copy(patch_sum, out_patch, save_sem.at[9]),
        pltpu.make_async_copy(got_block, out_block, save_sem.at[10]),
    ]
    for copy in exports[-2:]:
        copy.start()
    for seg in range(len(SEGMENTS)):
        wait_rows(sent_rows[seg], sum_send.at[seg])
    wait_for(rs_in, y_send.at[0])
    wait_for(terms, y_send.at[1])
    wait_for(pay.at[pl.ds(0, 3 * OWN)], y_send.at[2])
    for i, got in ((1, got_gain), (2, got_patch), (3, got_aq), (4, got_terms)):
        wait_for(got, y_send.at[2 + i])
    wait_for(rd_in, other_send.at[0])
    wait_rows(3 * 16 + 3 * 64 + 256, other_send.at[1])
    for i, (at, count) in enumerate(SEGMENTS + ((AT_TERMS, 512),)):
        save(at, count, i).wait()
    for copy in exports:
        copy.wait()


MAIN_VMEM = 44 * 1024 * 1024
FINISH_VMEM = 36 * 1024 * 1024


def run_chain(lengths, *args):
    hbm = pl.BlockSpec(memory_space=pl.ANY)
    V = pltpu.VMEM
    low = lambda *s: V(s, bf16)
    full = lambda *s: V(s, f32)
    scratch = [low(*w.shape) if w.shape[0] != LONGEST else low(128, COLS) for w in args]
    scratch += [
        full(VARS * PATCH, D), low(TERMS, D), low(HEADS * ROWS, TERMS), low(TERMS, COLS), full(8, TERMS),
        low(128, D), full(HEADS, ROWS, 128), full(ROWS, TERMS), low(ROWS, 128),
        low(5, ROWS, D), low(5, 3, OWN, D), full(OWN, D), low(ROWS, D), full(OWN, D),
        low(ROWS, D), low(ROWS, D), low(ROWS, D),
        low(ROWS, COLS), low(3, ROWS, COLS), full(HEADS * ROWS, ROWS), low(ROWS, COLS),
        low(ROWS, D), low(ROWS, D), low(HEADS * ROWS, COLS),
        low(ROWS, COLS), low(RING, OWN, COLS), low(3, 48, ROWS), low(RING, 48, ROWS),
        full(3, 8, COLS), full(RING, 8, COLS), full(SMALL, COLS), full(HEADS, TERMS),
        full(3, 8, COLS), full(RING, 8, COLS), low(3, 16, COLS), low(RING, 16, COLS),
        full(3, SMALL, COLS), full(7, SMALL, COLS), full(8, COLS), full(SMALL, COLS), full(48, ROWS),
        low(PAY, COLS), low(ALL, COLS), low(PAY * 31 // 32, COLS),
    ]
    dma = pltpu.SemaphoreType.DMA
    scratch += [
        dma((len(args),)), dma((7,)), dma((5,)), dma((4,)), dma((5,)), dma((5,)), dma((5, 10)), dma((3,)),
        dma((3,)), dma((2,)), dma((11,)),
    ]
    return pl.pallas_call(
        chain,
        out_shape=(
            jax.ShapeDtypeStruct((ROWS, COLS), bf16),
            jax.ShapeDtypeStruct((48, ROWS), f32),
            jax.ShapeDtypeStruct((ALL, COLS), bf16),
            jax.ShapeDtypeStruct((TERMS, D), bf16),
            jax.ShapeDtypeStruct((SMALL, COLS), f32),
            jax.ShapeDtypeStruct((8, COLS), f32),
        ),
        in_specs=[pl.BlockSpec(memory_space=pltpu.SMEM)] + [hbm] * len(args),
        out_specs=[hbm] * 6,
        scratch_shapes=scratch,
        compiler_params=pltpu.CompilerParams(
            collective_id=0, has_side_effects=True, vmem_limit_bytes=MAIN_VMEM
        ),
    )(lengths, *args)


VECTORS = (0, 7, 1, 2, 5, 3, 4, 6)


def finish(
    all_in, block_in, patch_in, terms_in, small_in, query_in, aq_from, hk,
    o_block, o_patch, o_down, o_up, o_out, o_qkv, o_wo, o_wv, o_wk, o_wq,
    o_pw, o_ve, o_pos, *rest,
):
    o_vectors, o_upbias = rest[:8], rest[8]
    (
        tot, wk, terms, small, query, aq_in, down, up, out, qkv, wo, gv, gk, gq, load_sem, save_sem,
    ) = rest[9:]
    spans = SEGMENTS + ((AT_TERMS, 512),)
    loads = [
        pltpu.make_async_copy(all_in.at[pl.ds(at, n)], tot.at[pl.ds(at, n)], load_sem.at[i])
        for i, (at, n) in enumerate(spans)
    ] + [
        pltpu.make_async_copy(src, dst, load_sem.at[6 + i])
        for i, (src, dst) in enumerate((
            (hk, wk), (terms_in, terms), (small_in, small), (query_in, query), (aq_from, aq_in)
        ))
    ]
    for copy in loads[:2]:
        copy.start()
    saves = [
        pltpu.make_async_copy(block_in, o_block, save_sem.at[8]),
        pltpu.make_async_copy(patch_in, o_patch, save_sem.at[9]),
    ]

    def store(i, src, dst):
        copy = pltpu.make_async_copy(src, dst, save_sem.at[i])
        copy.start()
        saves.append(copy)

    loads[0].wait()
    for j in range(RING):
        down[:, j * COLS : (j + 1) * COLS] = wide(tot[AT_DOWN + j * D : AT_DOWN + (j + 1) * D, :])
    store(4, down, o_down)
    for copy in loads[2:] + saves[:2]:
        copy.start()
    loads[1].wait()
    for j in range(RING):
        up[:, j * COLS : (j + 1) * COLS] = wide(tot[AT_UP + j * D : AT_UP + (j + 1) * D, :])
    store(5, up, o_up)
    loads[2].wait()
    for j in range(3):
        qkv[j] = wide(tot[AT_QKV + j * D : AT_QKV + (j + 1) * D, :])
    store(6, qkv, o_qkv)
    for j in range(RING):
        out[:, j * COLS : (j + 1) * COLS] = wide(tot[AT_OUT + j * COLS : AT_OUT + (j + 1) * COLS, :])
    store(7, out, o_out)
    loads[3].wait()
    for j in range(RING):
        wo[:, j * COLS : (j + 1) * COLS] = wide(tot[AT_WO + j * COLS : AT_WO + (j + 1) * COLS, :])
    store(1, wo, o_wo)
    for copy in loads[4:]:
        copy.wait()
    value_sum = jnp.concatenate(
        [tot[AT_LAST : AT_LAST + 256, :], tot[AT_LAST + HALF_LAST : AT_LAST + HALF_LAST + 128, :]], axis=0
    )
    gv[...] = mm_tn(terms[...], value_sum)
    store(0, gv, o_wv)
    across = jnp.concatenate(
        [tot[score_place(n) : score_place(n) + 16, :128] for n in range(TERMS // 16)], axis=0
    )
    along = in_two(mm_tn(across, terms[...])[:HEADS, :])
    head_of = iota((8, COLS), 1) // HEAD_DIM
    mine = head_of == iota((8, COLS), 0) % HEADS
    block = jnp.where(mine, query[...], 0.0).astype(bf16)
    gk[...] = mm_tn(along, block) * score_scale
    store(2, gk, o_wk)
    g_query = col_sum(jnp.where(mine, mm(along, wk[...]), 0.0)) * score_scale
    row = iota((8, D), 0)
    aq = jnp.where(row < 2, jnp.broadcast_to(as_row(aq_in), (8, D)), 0.0).astype(bf16)
    high = wide(g_query.astype(bf16))
    both = jnp.where(
        iota((8, COLS), 0) == 0,
        jnp.broadcast_to(high, (8, COLS)), jnp.broadcast_to(g_query - high, (8, COLS)),
    ).astype(bf16)
    gq[...] = mm_tn(aq, both)
    store(3, gq, o_wq)
    o_pos[...] = wide(tot[AT_POS : AT_POS + LONGEST, :])
    for p in range(PATCH):
        o_pw[:, p, :] = wide(tot[AT_TERMS + HALF * p : AT_TERMS + HALF * p + VARS, :])
    o_ve[...] = wide(tot[AT_TERMS + 4 * HALF : AT_TERMS + 4 * HALF + VARS, :])
    for ref, i in zip(o_vectors, VECTORS):
        ref[0:1, :] = small[i : i + 1, :128]
        ref[1:2, :] = small[i : i + 1, 128:]
    for j in range(RING):
        o_upbias[2 * j : 2 * j + 1, :] = small[8 + j : 9 + j, :128]
        o_upbias[2 * j + 1 : 2 * j + 2, :] = small[8 + j : 9 + j, 128:]
    for copy in saves:
        copy.wait()


def run_finish(*args):
    vmem = pl.BlockSpec(memory_space=pltpu.VMEM)
    hbm = pl.BlockSpec(memory_space=pl.ANY)
    full = lambda *s: pltpu.VMEM(s, f32)
    shape = lambda *s: jax.ShapeDtypeStruct(s, f32)
    big = [(D, D), (D, D), (COLS, D), (3, D, COLS), (COLS, D), (D, COLS), (D, COLS), (D, COLS)]
    return pl.pallas_call(
        finish,
        out_shape=[jax.ShapeDtypeStruct((ROWS, COLS), bf16), shape(48, ROWS)]
        + [shape(*s) for s in big]
        + [shape(VARS, PATCH, COLS), shape(VARS, COLS), shape(LONGEST, COLS)]
        + [shape(2, 128)] * 8 + [shape(8, 128)],
        in_specs=[hbm] * 8,
        out_specs=[hbm] * 10 + [vmem] * 12,
        scratch_shapes=[
            pltpu.VMEM((ALL, COLS), bf16), pltpu.VMEM((D, COLS), bf16), pltpu.VMEM((TERMS, D), bf16),
            full(SMALL, COLS), full(8, COLS), pltpu.VMEM((8, 128), bf16),
            full(D, D), full(D, D), full(COLS, D), full(3, D, COLS), full(COLS, D),
            full(D, COLS), full(D, COLS), full(D, COLS),
            pltpu.SemaphoreType.DMA((11,)), pltpu.SemaphoreType.DMA((10,)),
        ],
        compiler_params=pltpu.CompilerParams(vmem_limit_bytes=FINISH_VMEM),
    )(*args)


def shards(
    patches, item_lengths, cotangent, patch_weight, var_embed, agg_query, agg_wq, agg_wk, agg_wv,
    agg_wo, agg_bias, pos_table, first_gain, first_shift, attn_qkv, attn_out, attn_bias,
    second_gain, second_shift, mlp_up, up_bias, mlp_down, down_bias,
):
    tiled = lambda v: v.reshape(v.shape[0] // 128, 128)
    block, patch, summed, terms, small, query = run_chain(
        item_lengths, patches.T, patch_weight, var_embed, tiled(agg_query), tiled(first_gain),
        tiled(first_shift), tiled(attn_bias), tiled(second_gain), tiled(second_shift),
        tiled(down_bias), tiled(up_bias), tiled(agg_bias),
        agg_wq, agg_wk, agg_wv, agg_wo, pos_table, attn_qkv.transpose(1, 0, 2), attn_out,
        mlp_up, mlp_down, cotangent,
    )
    (
        block, patch, g_down, g_up, g_out, g_qkv, g_wo, g_wv, g_wk, g_wq, g_pw, g_ve, g_pos,
        g_agg_bias, g_aq, g_gain1, g_shift1, g_attn_bias, g_gain2, g_shift2, g_down_bias, g_up_bias,
    ) = run_finish(summed, block, patch, terms, small, query, tiled(agg_query), agg_wk)
    flat = lambda v: v.reshape(-1)
    return (
        block, patch.T, g_pw, g_ve, flat(g_aq), g_wq, g_wk, g_wv, g_wo, flat(g_agg_bias), g_pos,
        flat(g_gain1), flat(g_shift1), g_qkv.transpose(1, 0, 2), g_out, flat(g_attn_bias),
        flat(g_gain2), flat(g_shift2), g_up, flat(g_up_bias), g_down, flat(g_down_bias),
    )


def solution(mesh):
    rows = P(("dp", "pipe"), None)
    cols = P(None, "tensor")
    split = P("tensor", None)
    part = P("tensor")
    both = P(("dp", "pipe"), "tensor")
    last = P(None, None, "tensor")
    return jax.shard_map(
        shards,
        mesh=mesh,
        in_specs=(
            rows, P("dp", None), rows, P(), P(), P(), cols, cols, cols, split, part, cols, P(), P(),
            last, split, P(), P(), P(), cols, part, split, P(),
        ),
        out_specs=(
            both, both, last, cols, part, cols, cols, cols, split, part, cols, part, part, last,
            split, part, part, part, cols, part, split, part,
        ),
        check_vma=False,
    )
```

```python
import jax
import jax.numpy as jnp
from jax import lax
from jax.experimental import pallas as pl
from jax.experimental.pallas import tpu as pltpu
from jax.sharding import PartitionSpec as P

D = 1024
HEAD_DIM = 64
VARS = 48
PATCH = 4
LONGEST = 96
RING = 4
ROWS = 128
OWN = ROWS // RING
COLS = D // RING
HEADS = COLS // HEAD_DIM
HALF = 64
TERMS = 6 * HALF

AT_DOWN = 0
AT_UP = 4096
AT_OUT = 8192
AT_QKV = 9216
AT_WO = 12288
AT_LAST = 13312
PAY = 14336
AT_TERMS = PAY
ALL = PAY + 512
SEGMENTS = ((AT_DOWN, 4096), (AT_UP, 4096), (AT_OUT, 4096), (AT_WO, 1024), (AT_LAST, 1024))
CUBE = (True, True, False, False, False)
HALF_LAST = 512
AT_POS = AT_LAST + HALF_LAST + 128
SMALL = 32

norm_eps = 1e-05
root_half = 0.7071067811865476
inv_root_tau = 0.3989422804014327
score_scale = HEAD_DIM ** (-0.5)
highest = lax.Precision.HIGHEST
f32 = jnp.float32
bf16 = jnp.bfloat16
MESH = pl.DeviceIdType.MESH


def wide(v):
    return v.astype(f32)


def dot(left, right, dims, precision=None):
    return lax.dot_general(left, right, (dims, ((), ())), precision=precision, preferred_element_type=f32)


def mm(a, b, **kw):
    return dot(a, b, ((1,), (0,)), **kw)


def mm_nt(a, b, **kw):
    return dot(a, b, ((1,), (1,)), **kw)


def mm_tn(a, b, **kw):
    return dot(a, b, ((0,), (0,)), **kw)


def iota(shape, axis):
    return lax.broadcasted_iota(jnp.int32, shape, axis)


def norm_parts(x):
    centred = x - jnp.mean(x, axis=-1, keepdims=True)
    inverse = lax.rsqrt(jnp.mean(centred * centred, axis=-1, keepdims=True) + norm_eps)
    return centred * inverse, inverse


def norm_back(grad, xhat, inverse, gain):
    scaled = grad * gain
    return inverse * (
        scaled
        - jnp.mean(scaled, axis=-1, keepdims=True)
        - xhat * jnp.mean(scaled * xhat, axis=-1, keepdims=True)
    )


def col_sum(a):
    return jnp.sum(a, axis=0, keepdims=True)


WEIGHTS = (
    "patches", "pw", "ve", "aq", "gain1", "shift1", "abias", "gain2", "shift2", "dbias", "ubias", "aggbias",
    "wq", "wk", "wv", "wo", "pos", "wqkv", "wout", "wup", "wdown", "dy",
)
EARLY = ("aq", "wq", "pw", "ve", "wk", "wv", "patches", "wo", "pos", "aggbias")


def as_row(ref):
    value = wide(ref[...])
    return jnp.concatenate([value[i : i + 1, :] for i in range(value.shape[0])], axis=1)


def in_two(value):
    high = wide(value.astype(bf16))
    return jnp.concatenate([high, value - high], axis=0).astype(bf16)


def score_place(n):
    c, j = n // 16, n % 16
    return AT_LAST + c * HALF_LAST + 256 + 16 * (4 * (j % 4) + j // 4)


POINTS = {
    "up": ((0, 1), (1, 1)),
    "e2": (),
    "block": ((0, 2),),
    "out": ((0, 3), (1, 2), (2, 1), (0, 4)),
    "e1": ((1, 3),),
    "last": ((1, 4), (2, 2), (0, 5)),
    "wo": ((4, 1),),
}
TAIL = (
    (1, 5), (3, 1), (0, 6), (2, 3), "v", (1, 6), (4, 2), "v", (3, 2), (0, 7), (2, 4), (1, 7), (4, 3), "t", "v",
    (3, 3), (0, 8), "t", (2, 5), (1, 8), (4, 4), "v", (3, 4), (2, 6), (0, 9), "t", (1, 9), (0, 10), (4, 5),
    (1, 10), "t", (3, 5), (4, 6), "t", (3, 6),
)


def chain(
    lengths, hpatches, hpw, hve, haq, hgain1, hshift1, habias, hgain2, hshift2, hdbias,
    hubias, haggbias,
    hq, hk, hv, ho, hpos, hqkv, hout, hup, hdown, hdy,
    got_block, patch_sum, tot, terms, total_small, query_row,
    patches, pw, ve, aq_in, gain1_in, shift1_in, abias_in, gain2_in, shift2_in, dbias_in,
    ubias_in, aggbias_in,
    wq, wk, wv, wo, pos, wqkv, wout, wup, wdown, dy,
    pwf, shares, vterms, kterms, kdir, soft, x3, onehot,
    part, rs_in, stream, normed, resid, normed2, g_resid, g_stream,
    mixed, qkv, probs, attended, active, g_pre, masked,
    put_block, got_patch, put_patch, got_gain, put_gain, small, score_sum,
    got_aq, put_aq, got_terms, put_terms, rd_out, rd_in,
    pay, sum_in,
    load_sem, y_send, rs_recv, ag_recv, end_recv, sum_send, sum_recv, extra_recv, rd_recv, other_send,
):
    y = lax.axis_index("tensor")
    pipe = lax.axis_index("pipe")
    dp = lax.axis_index("dp")
    x, z = lax.rem(dp, 4), dp // 4
    own_rows = pl.ds(pl.multiple_of(y * OWN, OWN), OWN)
    own_cols = pl.ds(pl.multiple_of(y * COLS, COLS), COLS)
    barrier = pltpu.get_barrier_semaphore()
    rings = {"x": (x, lambda q: {"dp": 4 * z + q}), "z": (z, lambda q: {"dp": 4 * q + x})}
    neighbours = [{"pipe": 1 - pipe}]
    for j in (1, 2, 3):
        neighbours.append({"tensor": lax.rem(y + j, RING)})
        neighbours += [at(lax.rem(p + j, RING)) for p, at in rings.values()]
    for device in neighbours:
        pl.semaphore_signal(barrier, inc=1, device_id=device, device_id_type=MESH)
    dims = {
        "core": (pipe, {"pipe": 1 - pipe}),
        "xa": (lax.rem((x + 1) // 2, 2), {"dp": dp + 1 - 2 * lax.rem(x, 2)}),
        "xb": (x // 2, {"dp": 4 * z + 3 - x}),
        "za": (lax.rem((z + 1) // 2, 2), {"dp": dp + 4 - 8 * lax.rem(z, 2)}),
        "zb": (z // 2, {"dp": 4 * (3 - z) + x}),
    }
    ring = ("xa", "za", "xb", "zb")
    orders = [ring[k:] + ring[:k] for k in range(4)]
    ring_orders = (("x", "z"), ("z", "x"))
    loads = {
        name: pltpu.make_async_copy(src, dst, load_sem.at[i])
        for i, (name, src, dst) in enumerate(zip(
            WEIGHTS,
            (hpatches, hpw, hve, haq, hgain1, hshift1, habias, hgain2, hshift2, hdbias, hubias, haggbias,
             hq, hk, hv, ho, hpos, hqkv, hout, hup, hdown, hdy),
            (patches, pw, ve, aq_in, gain1_in, shift1_in, abias_in, gain2_in, shift2_in, dbias_in,
             ubias_in, aggbias_in,
             wq, wk, wv, wo, pos.at[pl.ds(0, LONGEST)], wqkv, wout, wup, wdown, dy),
        ))
    }
    for name in EARLY + tuple(name for name in WEIGHTS if name not in EARLY):
        loads[name].start()

    def wait_for(like, sem):
        pltpu.make_async_copy(like, like, sem).wait()

    def wait_rows(count, sem):
        wait_for(tot.at[pl.ds(0, count)], sem)

    sent_rows = [0] * len(SEGMENTS)

    def to_partner(src, dst, send, recv, dim):
        return pltpu.make_async_remote_copy(
            src_ref=src, dst_ref=dst, send_sem=send, recv_sem=recv,
            device_id=dims[dim][1], device_id_type=MESH,
        )

    def rows_at(start, length):
        return pl.ds(pl.multiple_of(start, 16), length)

    def region(base, length, order, steps):
        for dim in order[:steps]:
            length //= 2
            base = base + dims[dim][0] * length
        return base, length

    def part_of(seg, k, steps):
        at, count = SEGMENTS[seg]
        return region(at + pipe * (count // 2) + k * (count // 8), count // 8, orders[k], steps)

    in_at = {}
    place_in = 0
    for seg, (_, count) in enumerate(SEGMENTS):
        in_at[seg, "core"] = place_in
        place_in += count // 2
        for s in range(4):
            for k in range(4):
                if CUBE[seg]:
                    in_at[seg, s, k] = place_in
                    place_in += count // 16 >> s
        for s in range(2):
            for k in range(2):
                if not CUBE[seg]:
                    in_at[seg, s, k] = place_in
                    place_in += 3 * (count // 16 >> 2 * s)
    assert place_in <= sum_in.shape[0]

    def core_halving(seg):
        at, count = SEGMENTS[seg]
        half = count // 2
        return to_partner(
            pay.at[rows_at(at + (1 - pipe) * half, half)], sum_in.at[pl.ds(in_at[seg, "core"], half)],
            sum_send.at[seg], sum_recv.at[seg, 0], "core",
        )

    def halving(seg, s, k):
        base, length = part_of(seg, k, s)
        dim = orders[k][s]
        length //= 2
        return to_partner(
            pay.at[rows_at(base + (1 - dims[dim][0]) * length, length)],
            sum_in.at[pl.ds(in_at[seg, s, k], length)], sum_send.at[seg], sum_recv.at[seg, 1 + s], dim,
        )

    def doubling(seg, t, k):
        rows = rows_at(*part_of(seg, k, t + 1))
        return to_partner(
            tot.at[rows], tot.at[rows], sum_send.at[seg], sum_recv.at[seg, 5 + t], orders[k][t]
        )

    def core_doubling(seg):
        at, count = SEGMENTS[seg]
        rows = rows_at(at + pipe * (count // 2), count // 2)
        return to_partner(tot.at[rows], tot.at[rows], sum_send.at[seg], sum_recv.at[seg, 9], "core")

    def ring_copy(src_rows, src, dst, sems, dim, j):
        position, device = rings[dim]
        return pltpu.make_async_remote_copy(
            src_ref=src.at[src_rows], dst_ref=dst, send_sem=sems[0], recv_sem=sems[1],
            device_id=device(lax.rem(position + j, RING)), device_id_type=MESH,
        )

    def share(base, length, order, steps):
        for dim in order[:steps]:
            length //= RING
            base = base + rings[dim][0] * length
        return base, length

    def share_of(seg, k, steps):
        at, count = SEGMENTS[seg]
        return share(at + pipe * (count // 2) + k * (count // 4), count // 4, ring_orders[k], steps)

    def ring_scatter(seg, s, k):
        base, length = share_of(seg, k, s)
        length //= RING
        dim = ring_orders[k][s]
        position = rings[dim][0]
        sems = (sum_send.at[seg], sum_recv.at[seg, 1 + s])
        return [
            ring_copy(
                rows_at(base + lax.rem(position + j, RING) * length, length), pay,
                sum_in.at[pl.ds(in_at[seg, s, k] + (j - 1) * length, length)],
                sems, dim, j,
            )
            for j in (2, 1, 3)
        ]

    def ring_gather(base_length, dim, sems):
        rows = rows_at(*base_length)
        return [ring_copy(rows, tot, tot.at[rows], sems, dim, j) for j in (2, 1, 3)]

    def ring_gather_of(seg, t, k):
        sems = (sum_send.at[seg], sum_recv.at[seg, 3 + t])
        return ring_gather(share_of(seg, k, t + 1), ring_orders[k][t], sems)

    def launch_all(seg, copies, rows):
        for copy in copies:
            copy.start()
        sent_rows[seg] += len(copies) * rows

    def ring_advance(seg, stage):
        at, count = SEGMENTS[seg]
        half, quarter = count // 2, count // 4
        if stage == 0:
            launch_all(seg, [core_halving(seg)], half)
        elif stage == 1:
            wait_rows(half, sum_recv.at[seg, 0])
            for k in range(2):
                rows = rows_at(at + pipe * half + k * quarter, quarter)
                came = pl.ds(in_at[seg, "core"] + k * quarter, quarter)
                pay[rows, :] = pay[rows, :] + sum_in[came, :]
                launch_all(seg, ring_scatter(seg, 0, k), quarter // 4)
        elif stage <= 3:
            s = stage - 2
            length = quarter >> 2 * (s + 1)
            wait_rows(6 * length, sum_recv.at[seg, 1 + s])
            for k in range(2):
                rows = rows_at(*share_of(seg, k, s + 1))
                total = wide(pay[rows, :])
                for j in range(3):
                    total = total + wide(sum_in[pl.ds(in_at[seg, s, k] + j * length, length), :])
                if s == 0:
                    pay[rows, :] = total.astype(bf16)
                    launch_all(seg, ring_scatter(seg, 1, k), length // 4)
                else:
                    tot[rows, :] = total.astype(bf16)
                    launch_all(seg, ring_gather_of(seg, 1, k), length)
        elif stage <= 5:
            t = 5 - stage
            length = quarter >> 2 * (t + 1)
            wait_rows(6 * length, sum_recv.at[seg, 3 + t])
            if t:
                for k in range(2):
                    launch_all(seg, ring_gather_of(seg, 0, k), quarter // 4)
            else:
                launch_all(seg, [core_doubling(seg)], half)
        else:
            wait_rows(half, sum_recv.at[seg, 9])

    def advance(seg, stage):
        if not CUBE[seg]:
            return ring_advance(seg, stage)
        at, count = SEGMENTS[seg]
        half, quarter = count // 2, count // 8
        if stage == 0:
            launch_all(seg, [core_halving(seg)], half)
        elif stage == 1:
            wait_rows(half, sum_recv.at[seg, 0])
            for k in range(4):
                rows = rows_at(at + pipe * half + k * quarter, quarter)
                came = pl.ds(in_at[seg, "core"] + k * quarter, quarter)
                pay[rows, :] = pay[rows, :] + sum_in[came, :]
                launch_all(seg, [halving(seg, 0, k)], quarter // 2)
        elif stage <= 5:
            s = stage - 2
            length = quarter >> (s + 1)
            wait_rows(4 * length, sum_recv.at[seg, 1 + s])
            for k in range(4):
                rows = rows_at(*part_of(seg, k, s + 1))
                total = pay[rows, :] + sum_in[pl.ds(in_at[seg, s, k], length), :]
                if s < 3:
                    pay[rows, :] = total
                    launch_all(seg, [halving(seg, s + 1, k)], length // 2)
                else:
                    tot[rows, :] = total
                    launch_all(seg, [doubling(seg, 3, k)], length)
        elif stage <= 9:
            t = 9 - stage
            length = quarter >> (t + 1)
            wait_rows(4 * length, sum_recv.at[seg, 5 + t])
            if t:
                for k in range(4):
                    launch_all(seg, [doubling(seg, t - 1, k)], 2 * length)
            else:
                launch_all(seg, [core_doubling(seg)], half)
        else:
            wait_rows(half, sum_recv.at[seg, 9])

    def point(name):
        for seg, stage in POINTS[name]:
            advance(seg, stage)

    def remote(src, dst, send, recv, j):
        return pltpu.make_async_remote_copy(
            src_ref=src, dst_ref=dst, send_sem=send, recv_sem=recv,
            device_id={"tensor": lax.rem(y + j, RING)}, device_id_type=MESH,
        )

    def rows_of(j):
        return pl.ds(pl.multiple_of(lax.rem(y + j, RING) * OWN, OWN), OWN)

    def scatter(phase):
        for j in (2, 1, 3):
            remote(part.at[phase, rows_of(j)], rs_in.at[phase, j - 1], y_send.at[0], rs_recv.at[phase], j).start()

    def scattered(phase):
        total = wide(part[phase, own_rows, :])
        wait_for(rs_in.at[phase], rs_recv.at[phase])
        for j in range(3):
            total = total + wide(rs_in[phase, j])
        return total

    def gather(phase, full):
        for j in (2, 1, 3):
            remote(full.at[own_rows], full.at[own_rows], y_send.at[1], ag_recv.at[phase], j).start()

    def gathered(phase):
        wait_for(part.at[phase, pl.ds(0, 3 * OWN)], ag_recv.at[phase])

    def exchange(i, put, got):
        for j in (2, 1, 3):
            remote(put.at[lax.rem(y + j, RING)], got.at[j - 1], y_send.at[2 + i], end_recv.at[i], j).start()

    for c in range(2):
        at = AT_LAST + c * HALF_LAST
        pay[at : at + HALF_LAST, :] = jnp.zeros((HALF_LAST, COLS), bf16)

    first, second = lengths[pipe, 0], lengths[pipe, 1]
    both = first + second

    def segment_of(r):
        return (r >= first).astype(jnp.int32) + (r >= both).astype(jnp.int32)

    same_item = segment_of(iota((ROWS, ROWS), 0)) == segment_of(iota((ROWS, ROWS), 1))
    row = iota((ROWS, 128), 0)
    place = row - jnp.where(row >= first, first, 0) - jnp.where(row >= both, second, 0)
    onehot[...] = jnp.where(place == iota((ROWS, 128), 1), 1.0, 0.0).astype(bf16)
    pos[LONGEST:, :] = jnp.zeros((128 - LONGEST, COLS), bf16)

    loads["pw"].wait()
    loads["ve"].wait()
    r, c = iota((4 * HALF, VARS * PATCH), 0), iota((4 * HALF, VARS * PATCH), 1)
    pick = jnp.where((c == PATCH * (r % HALF) + r // HALF) & (r % HALF < VARS), 1.0, 0.0).astype(bf16)
    for v in range(VARS):
        pwf[PATCH * v : PATCH * (v + 1), :] = wide(pw[v])
    terms[: 4 * HALF, :] = mm(pick, pwf[...].astype(bf16)).astype(bf16)
    terms[4 * HALF : 4 * HALF + VARS, :] = ve[...]
    terms[4 * HALF + VARS :, :] = jnp.zeros((TERMS - 4 * HALF - VARS, D), bf16)
    r, c = iota((VARS * PATCH, 4 * HALF), 1), iota((VARS * PATCH, 4 * HALF), 0)
    pick_back = jnp.where((c == PATCH * (r % HALF) + r // HALF) & (r % HALF < VARS), 1.0, 0.0).astype(bf16)
    loads["patches"].wait()
    x3[:, : 4 * HALF] = mm_tn(patches[...], pick_back)
    lane = iota((ROWS, 128), 1)
    x3[:, 4 * HALF :] = jnp.where(lane < VARS, 1.0, 0.0)

    loads["wq"].wait()
    loads["aq"].wait()
    aq_row = as_row(aq_in)
    query = mm(jnp.broadcast_to(aq_row, (8, D)).astype(bf16), wq[...])[0:1, :].astype(bf16)
    query_row[...] = jnp.broadcast_to(wide(query), (8, COLS))
    head_of = iota((8, COLS), 1) // HEAD_DIM
    block = jnp.where(
        head_of == iota((8, COLS), 0) % HEADS, jnp.broadcast_to(wide(query), (8, COLS)), 0.0
    ).astype(bf16)
    loads["wk"].wait()
    key_dir = mm_nt(block, wk[...]) * score_scale
    split = in_two(key_dir[:HEADS, :])
    kdir[...] = jnp.concatenate([wide(split), jnp.zeros((120, D), f32)], axis=0).astype(bf16)
    key_parts = mm_nt(split, terms[...])
    kterms[...] = key_parts + pltpu.roll(key_parts, HEADS, 0)
    loads["wv"].wait()
    vterms[...] = mm(terms[...], wv[...]).astype(bf16)

    def fold(v):
        folded = v[:, :128] + v[:, 128:256] + v[:, 256:]
        return folded + pltpu.roll(folded, HALF, 1)

    def thrice(v):
        return jnp.concatenate([v, v, v], axis=1)

    for h in range(HEADS):
        scores = fold(x3[...] * kterms[h : h + 1, :])
        scores = jnp.where(lane % HALF < VARS, scores, -1e30)
        raised = jnp.exp(scores - jnp.max(scores, axis=-1, keepdims=True))
        weights = raised / (0.5 * jnp.sum(raised, axis=-1, keepdims=True))
        soft[h] = weights
        shares[h * ROWS : (h + 1) * ROWS, :] = (x3[...] * thrice(weights)).astype(bf16)

    col_head = iota((ROWS, COLS), 1) // HEAD_DIM

    def pick_heads(stacked):
        total = jnp.zeros((ROWS, COLS), f32)
        for h in range(HEADS):
            total = jnp.where(col_head == h, stacked[h * ROWS : (h + 1) * ROWS, :], total)
        return total

    def spread_heads(value):
        for h in range(HEADS):
            masked[h * ROWS : (h + 1) * ROWS, :] = jnp.where(col_head == h, value, 0.0).astype(bf16)

    mixed[...] = pick_heads(mm(shares[...], vterms[...])).astype(bf16)
    loads["wo"].wait()
    loads["pos"].wait()
    loads["aggbias"].wait()
    aggbias_row = as_row(aggbias_in)
    for j in range(RING):
        cols = slice(j * COLS, (j + 1) * COLS)
        part[0, :, cols] = mm(mixed[...], wo[:, cols]).astype(bf16)
    extra = mm(mixed[...], wo[:, own_cols]) + mm(onehot[...], pos[...]) + aggbias_row
    part[0, :, own_cols] = extra.astype(bf16)
    pl.semaphore_wait(barrier, len(neighbours))
    scatter(0)
    for name in ("gain1", "shift1", "abias", "gain2", "shift2", "dbias", "ubias"):
        loads[name].wait()
    gain1_row, shift1_row = as_row(gain1_in), as_row(shift1_in)
    abias_row, gain2_row, shift2_row = as_row(abias_in), as_row(gain2_in), as_row(shift2_in)
    dbias_row, ubias_row = as_row(dbias_in), as_row(ubias_in)
    stream_own = wide(scattered(0).astype(bf16))
    xhat1, inv1 = norm_parts(stream_own)
    normed[own_rows, :] = (xhat1 * gain1_row + shift1_row).astype(bf16)
    stream[...] = stream_own
    gather(0, normed)
    loads["wqkv"].wait()
    gathered(0)

    for j in range(3):
        qkv[j] = mm(normed[...], wqkv[j]).astype(bf16)
    spread_heads(qkv[0])
    raw = mm_nt(masked[...], qkv[1]) * score_scale
    for h in range(HEADS):
        rows = slice(h * ROWS, (h + 1) * ROWS)
        score = jnp.where(same_item, raw[rows, :], -1e30)
        raised = jnp.exp(score - jnp.max(score, axis=-1, keepdims=True))
        probs[rows, :] = raised / jnp.sum(raised, axis=-1, keepdims=True)
    attended[...] = pick_heads(mm(probs[...].astype(bf16), qkv[2])).astype(bf16)
    loads["wout"].wait()
    for j in range(RING):
        cols = slice(j * COLS, (j + 1) * COLS)
        part[1, :, cols] = mm(attended[...], wout[:, cols]).astype(bf16)
    scatter(1)
    resid_own = stream[...] + scattered(1) + abias_row
    xhat2, inv2 = norm_parts(resid_own)
    normed2[own_rows, :] = (xhat2 * gain2_row + shift2_row).astype(bf16)
    resid[...] = resid_own
    gather(1, normed2)
    loads["wup"].wait()
    loads["wdown"].wait()
    loads["dy"].wait()
    gathered(1)

    for j in range(RING):
        cols = slice(j * COLS, (j + 1) * COLS)
        pre = mm(normed2[...], wup[:, cols]) + ubias_row[:, cols]
        half_cdf = 0.5 * (1.0 + lax.erf(pre * root_half))
        active[:, cols] = (pre * half_cdf).astype(bf16)
        slope = half_cdf + pre * jnp.exp(-0.5 * pre * pre) * inv_root_tau
        grad = (mm_nt(dy[...], wdown[cols, :]) * slope).astype(bf16)
        g_pre[:, cols] = grad
        small[8 + j : 9 + j, :] = col_sum(wide(grad))
    for j in range(RING):
        rows = slice(j * COLS, (j + 1) * COLS)
        part[3, :, rows] = mm_nt(g_pre[...], wup[rows, :]).astype(bf16)
    scatter(3)
    for j in range(RING):
        cols = slice(j * COLS, (j + 1) * COLS)
        part[2, :, cols] = mm(active[...], wdown[:, cols]).astype(bf16)
    scatter(2)
    for j in range(RING):
        cols = slice(j * COLS, (j + 1) * COLS)
        pay[AT_DOWN + j * D : AT_DOWN + (j + 1) * D, :] = mm_tn(active[...], dy[:, cols]).astype(bf16)
    advance(0, 0)
    for j in range(RING):
        cols = slice(j * COLS, (j + 1) * COLS)
        pay[AT_UP + j * D : AT_UP + (j + 1) * D, :] = mm_tn(normed2[...], g_pre[:, cols]).astype(bf16)
    advance(1, 0)
    point("up")
    e2 = scattered(3)
    g_resid_own = (wide(dy[own_rows, :]) + norm_back(e2, xhat2, inv2, gain2_row)).astype(bf16)
    g_resid[own_rows, :] = g_resid_own
    gather(2, g_resid)
    point("e2")
    result = resid[...] + scattered(2) + dbias_row
    gain2, shift2 = col_sum(e2 * xhat2), col_sum(e2)
    for j in range(RING):
        put_block[j] = result[:, j * COLS : (j + 1) * COLS].astype(bf16)
    for j in (2, 1, 3):
        remote(put_block.at[lax.rem(y + j, RING)], got_block.at[own_rows], y_send.at[2], end_recv.at[0], j).start()
    got_block[own_rows, :] = put_block[y]
    point("block")
    gathered(2)

    spread_heads(mm_nt(g_resid[...], wout[...]).astype(bf16))
    g_probs = mm_nt(masked[...], qkv[2])
    g_v = mm_tn(probs[...].astype(bf16), masked[...]).astype(bf16)
    p = probs[...]
    g_scores = (p * (g_probs - jnp.sum(p * g_probs, axis=-1, keepdims=True))).astype(bf16)
    g_q = (pick_heads(mm(g_scores, qkv[1])) * score_scale).astype(bf16)
    spread_heads(qkv[0])
    g_k = (mm_tn(g_scores, masked[...]) * score_scale).astype(bf16)
    for j in range(RING):
        rows = slice(j * COLS, (j + 1) * COLS)
        total = mm_nt(g_q, wqkv[0, rows, :]) + mm_nt(g_k, wqkv[1, rows, :])
        part[4, :, rows] = (total + mm_nt(g_v, wqkv[2, rows, :])).astype(bf16)
    scatter(4)
    for j, g in enumerate((g_q, g_k, g_v)):
        pay[AT_QKV + j * D : AT_QKV + (j + 1) * D, :] = mm_tn(normed[...], g).astype(bf16)
    for j in range(RING):
        cols = slice(j * COLS, (j + 1) * COLS)
        pay[AT_OUT + j * COLS : AT_OUT + (j + 1) * COLS, :] = mm_tn(
            attended[...], g_resid[:, cols]
        ).astype(bf16)
    advance(2, 0)
    point("out")
    e1 = scattered(4)
    g_stream_own = (
        wide(g_resid[own_rows, :]) + norm_back(e1, xhat1, inv1, gain1_row)
    ).astype(bf16)
    g_stream[own_rows, :] = g_stream_own
    gather(3, g_stream)
    gain1, shift1 = col_sum(e1 * xhat1), col_sum(e1)
    for j in range(RING):
        cols = slice(j * COLS, (j + 1) * COLS)
        for i, v in enumerate((gain1, shift1, gain2, shift2)):
            put_gain[j, i : i + 1, :] = v[:, cols]
        put_gain[j, 4:8, :] = jnp.zeros((4, COLS), f32)
    exchange(1, put_gain, got_gain)
    point("e1")
    gathered(3)

    spread_heads(mm_nt(g_stream[...], wo[...]).astype(bf16))
    by_term = mm_nt(masked[...], vterms[...])
    grad_patch = jnp.zeros((ROWS, 4 * HALF), f32)
    for h in range(HEADS):
        mine = by_term[h * ROWS : (h + 1) * ROWS, :]
        weights = soft[h]
        g_weights = fold(x3[...] * mine)
        g_sc = weights * (
            g_weights - 0.5 * jnp.sum(weights * g_weights, axis=-1, keepdims=True)
        )
        g_sc2 = jnp.concatenate([g_sc, g_sc], axis=1)
        w2 = jnp.concatenate([weights, weights], axis=1)
        grad_patch = grad_patch + g_sc2 * kterms[h : h + 1, : 4 * HALF] + w2 * mine[:, : 4 * HALF]
        sums = col_sum(x3[...] * thrice(g_sc))
        score_sum[h : h + 1, :] = sums
    value_sum = mm_tn(shares[...], masked[...]).astype(bf16)
    pay[AT_LAST : AT_LAST + 256, :] = value_sum[:256, :]
    pay[AT_LAST + HALF_LAST : AT_LAST + HALF_LAST + 128, :] = value_sum[256:, :]
    head_cols = iota((HEADS, COLS), 1)
    spot = jnp.where((head_cols % HEADS == iota((HEADS, COLS), 0)) & (head_cols < 8), 1.0, 0.0).astype(bf16)
    across = mm_tn(score_sum[...].astype(bf16), spot).astype(bf16)
    for n in range(TERMS // 16):
        at = score_place(n)
        pay[at : at + 16, :] = across[16 * n : 16 * (n + 1), :]
    g_own = g_stream[:, own_cols]
    pay[AT_POS : AT_POS + LONGEST, :] = mm_tn(onehot[...], g_own)[:LONGEST, :].astype(bf16)
    advance(4, 0)
    point("last")
    for j in range(RING):
        cols = slice(j * COLS, (j + 1) * COLS)
        pay[AT_WO + j * COLS : AT_WO + (j + 1) * COLS, :] = mm_tn(
            mixed[...], g_stream[:, cols]
        ).astype(bf16)
    advance(3, 0)
    point("wo")
    along = mm(in_two(score_sum[...]), terms[...])
    along = in_two(along[:HEADS] + along[HEADS:])
    head_of = iota((8, COLS), 1) // HEAD_DIM
    g_query = col_sum(jnp.where(head_of == iota((8, COLS), 0) % HEADS, mm(along, wk[...]), 0.0)) * score_scale
    both_parts = mm_nt(in_two(jnp.broadcast_to(g_query, (HEADS, COLS))), wq[...])
    g_aq = both_parts[0:1, :] + both_parts[HEADS : HEADS + 1, :]
    for j in range(RING):
        put_aq[j] = jnp.broadcast_to(g_aq[:, j * COLS : (j + 1) * COLS], (8, COLS))
    exchange(3, put_aq, got_aq)
    low_patch = grad_patch.astype(bf16)
    width = VARS * PATCH // RING
    r, c = iota((width, 4 * HALF), 1), iota((width, 4 * HALF), 0)
    for j in range(RING):
        pick_own = jnp.where(
            (c + width * j == PATCH * (r % HALF) + r // HALF) & (r % HALF < VARS), 1.0, 0.0
        ).astype(bf16)
        put_patch[j] = mm_nt(pick_own, low_patch).astype(bf16)
    exchange(2, put_patch, got_patch)
    small[0:1, :] = col_sum(wide(g_own))
    small[5:6, :] = col_sum(wide(g_resid[:, own_cols]))
    small[6:7, :] = col_sum(wide(dy[:, own_cols]))
    small[12:32, :] = jnp.zeros((20, COLS), f32)
    wait_for(got_gain, end_recv.at[1])
    small[1:5, :] = (put_gain[y] + got_gain[0] + got_gain[1] + got_gain[2])[0:4, :]

    def vector_step(i):
        if i == 0:
            wait_for(got_aq, end_recv.at[3])
            small[7:8, :] = (put_aq[y] + got_aq[0] + got_aq[1] + got_aq[2])[0:1, :]
            rd_out[0] = small[...]
            to_partner(rd_out.at[0], rd_in.at[0], other_send.at[0], rd_recv.at[0], "core").start()
            return
        at, n = (0, 1) if i == 1 else (3 * i - 5, 3)
        wait_for(rd_in.at[pl.ds(at, n)], rd_recv.at[i - 1])
        value = rd_out[i - 1]
        for j in range(n):
            value = value + rd_in[at + j]
        if i == 3:
            total_small[...] = value
            return
        rd_out[i] = value
        position, device = rings["xz"[i - 1]]
        for j in (2, 1, 3):
            pltpu.make_async_remote_copy(
                src_ref=rd_out.at[i], dst_ref=rd_in.at[3 * i - 3 + j], send_sem=other_send.at[0],
                recv_sem=rd_recv.at[i], device_id=device(lax.rem(position + j, RING)), device_id_type=MESH,
            ).start()

    terms_base = AT_TERMS + pipe * 256

    def terms_gather(t):
        dim = ring_orders[0][t]
        for copy in ring_gather(
            share(terms_base, 256, ring_orders[0], t + 1), dim, (other_send.at[1], extra_recv.at[t])
        ):
            copy.start()

    def terms_step(i):
        if i == 0:
            value_rows = tot[rows_at(*share_of(4, 0, 2)), :]
            score_rows = tot[rows_at(*share_of(4, 1, 2)), :]
            total = mm_nt(value_rows, wv[...]) + mm(score_rows[:, :128], kdir[...])
            for j in range(RING):
                put_terms[j] = total[:, j * COLS : (j + 1) * COLS].astype(bf16)
            exchange(4, put_terms, got_terms)
        elif i == 1:
            wait_for(got_terms, end_recv.at[4])
            total = wide(put_terms[y]) + wide(got_terms[0]) + wide(got_terms[1]) + wide(got_terms[2])
            tot[rows_at(*share(terms_base, 256, ring_orders[0], 2)), :] = total.astype(bf16)
            terms_gather(1)
        elif i == 2:
            wait_rows(48, extra_recv.at[1])
            terms_gather(0)
        elif i == 3:
            wait_rows(192, extra_recv.at[0])
            rows = rows_at(terms_base, 256)
            to_partner(tot.at[rows], tot.at[rows], other_send.at[1], extra_recv.at[2], "core").start()
        else:
            wait_rows(256, extra_recv.at[2])

    next_of = {"t": 0, "v": 0}
    for step in TAIL:
        if step == "t":
            terms_step(next_of["t"])
            next_of["t"] += 1
        elif step == "v":
            vector_step(next_of["v"])
            next_of["v"] += 1
        else:
            advance(*step)
    assert next_of == {"t": 5, "v": 4}
    wait_for(got_patch, end_recv.at[2])
    patch_sum[...] = (
        wide(put_patch[y]) + wide(got_patch[0]) + wide(got_patch[1]) + wide(got_patch[2])
    )
    wait_for(pay.at[pl.ds(0, 3 * OWN)], end_recv.at[0])
    for seg in range(len(SEGMENTS)):
        wait_rows(sent_rows[seg], sum_send.at[seg])
    wait_for(rs_in, y_send.at[0])
    wait_for(terms, y_send.at[1])
    wait_for(pay.at[pl.ds(0, 3 * OWN)], y_send.at[2])
    for i, got in ((1, got_gain), (2, got_patch), (3, got_aq), (4, got_terms)):
        wait_for(got, y_send.at[2 + i])
    wait_for(rd_in, other_send.at[0])
    wait_rows(3 * 16 + 3 * 64 + 256, other_send.at[1])


MAIN_VMEM = 50 * 1024 * 1024
FINISH_VMEM = 50 * 1024 * 1024


def run_chain(lengths, *args):
    hbm = pl.BlockSpec(memory_space=pl.ANY)
    V = pltpu.VMEM
    low = lambda *s: V(s, bf16)
    full = lambda *s: V(s, f32)
    scratch = [low(*w.shape) if w.shape[0] != LONGEST else low(128, COLS) for w in args]
    scratch += [
        full(VARS * PATCH, D), low(HEADS * ROWS, TERMS), low(TERMS, COLS), full(8, TERMS),
        low(128, D), full(HEADS, ROWS, 128), full(ROWS, TERMS), low(ROWS, 128),
        low(5, ROWS, D), low(5, 3, OWN, D), full(OWN, D), low(ROWS, D), full(OWN, D),
        low(ROWS, D), low(ROWS, D), low(ROWS, D),
        low(ROWS, COLS), low(3, ROWS, COLS), full(HEADS * ROWS, ROWS), low(ROWS, COLS),
        low(ROWS, D), low(ROWS, D), low(HEADS * ROWS, COLS),
        low(RING, OWN, COLS), low(3, 48, ROWS), low(RING, 48, ROWS),
        full(3, 8, COLS), full(RING, 8, COLS), full(SMALL, COLS), full(HEADS, TERMS),
        full(3, 8, COLS), full(RING, 8, COLS), low(3, 16, COLS), low(RING, 16, COLS),
        full(3, SMALL, COLS), full(7, SMALL, COLS),
        low(PAY, COLS), low(PAY * 31 // 32, COLS),
    ]
    dma = pltpu.SemaphoreType.DMA
    scratch += [
        dma((len(args),)), dma((7,)), dma((5,)), dma((4,)), dma((5,)), dma((5,)), dma((5, 10)), dma((3,)),
        dma((3,)), dma((2,)),
    ]
    return pl.pallas_call(
        chain,
        out_shape=(
            low(ROWS, COLS), full(48, ROWS), low(ALL, COLS), low(TERMS, D), full(SMALL, COLS), full(8, COLS),
        ),
        in_specs=[pl.BlockSpec(memory_space=pltpu.SMEM)] + [hbm] * len(args),
        out_specs=[pl.BlockSpec(memory_space=pltpu.VMEM)] * 6,
        scratch_shapes=scratch,
        compiler_params=pltpu.CompilerParams(
            collective_id=0, has_side_effects=True, vmem_limit_bytes=MAIN_VMEM
        ),
    )(lengths, *[pltpu.with_memory_space_constraint(a, pltpu.HBM) for a in args])


VECTORS = (0, 7, 1, 2, 5, 3, 4, 6)


def finish(
    tot, block_in, patch_in, terms, small, query, aq_from, hk,
    o_block, o_patch, o_down, o_up, o_out, o_qkv, o_wo, o_wv, o_wk, o_wq,
    o_pw, o_ve, o_pos, *rest,
):
    o_vectors, o_upbias = rest[:8], rest[8]
    wk, aq_in, down, up, out, qkv, wo, gv, gk, gq, load_sem, save_sem = rest[9:]
    loads = [
        pltpu.make_async_copy(hk, wk, load_sem.at[0]), pltpu.make_async_copy(aq_from, aq_in, load_sem.at[1])
    ]
    for copy in loads:
        copy.start()
    saves = []

    def store(i, src, dst):
        copy = pltpu.make_async_copy(src, dst, save_sem.at[i])
        copy.start()
        saves.append(copy)

    for j in range(RING):
        down[:, j * COLS : (j + 1) * COLS] = wide(tot[AT_DOWN + j * D : AT_DOWN + (j + 1) * D, :])
    store(4, down, o_down)
    for j in range(RING):
        up[:, j * COLS : (j + 1) * COLS] = wide(tot[AT_UP + j * D : AT_UP + (j + 1) * D, :])
    store(5, up, o_up)
    for j in range(3):
        qkv[j] = wide(tot[AT_QKV + j * D : AT_QKV + (j + 1) * D, :])
    store(6, qkv, o_qkv)
    for j in range(RING):
        out[:, j * COLS : (j + 1) * COLS] = wide(tot[AT_OUT + j * COLS : AT_OUT + (j + 1) * COLS, :])
    store(7, out, o_out)
    for j in range(RING):
        wo[:, j * COLS : (j + 1) * COLS] = wide(tot[AT_WO + j * COLS : AT_WO + (j + 1) * COLS, :])
    store(1, wo, o_wo)
    store(8, block_in, o_block)
    store(9, patch_in, o_patch)
    for copy in loads:
        copy.wait()
    value_sum = jnp.concatenate(
        [tot[AT_LAST : AT_LAST + 256, :], tot[AT_LAST + HALF_LAST : AT_LAST + HALF_LAST + 128, :]], axis=0
    )
    gv[...] = mm_tn(terms[...], value_sum)
    store(0, gv, o_wv)
    across = jnp.concatenate(
        [tot[score_place(n) : score_place(n) + 16, :128] for n in range(TERMS // 16)], axis=0
    )
    along = in_two(mm_tn(across, terms[...])[:HEADS, :])
    head_of = iota((8, COLS), 1) // HEAD_DIM
    mine = head_of == iota((8, COLS), 0) % HEADS
    block = jnp.where(mine, query[...], 0.0).astype(bf16)
    gk[...] = mm_tn(along, block) * score_scale
    store(2, gk, o_wk)
    g_query = col_sum(jnp.where(mine, mm(along, wk[...]), 0.0)) * score_scale
    row = iota((8, D), 0)
    aq = jnp.where(row < 2, jnp.broadcast_to(as_row(aq_in), (8, D)), 0.0).astype(bf16)
    high = wide(g_query.astype(bf16))
    both = jnp.where(
        iota((8, COLS), 0) == 0,
        jnp.broadcast_to(high, (8, COLS)), jnp.broadcast_to(g_query - high, (8, COLS)),
    ).astype(bf16)
    gq[...] = mm_tn(aq, both)
    store(3, gq, o_wq)
    o_pos[...] = wide(tot[AT_POS : AT_POS + LONGEST, :])
    for p in range(PATCH):
        o_pw[:, p, :] = wide(tot[AT_TERMS + HALF * p : AT_TERMS + HALF * p + VARS, :])
    o_ve[...] = wide(tot[AT_TERMS + 4 * HALF : AT_TERMS + 4 * HALF + VARS, :])
    for ref, i in zip(o_vectors, VECTORS):
        ref[0:1, :] = small[i : i + 1, :128]
        ref[1:2, :] = small[i : i + 1, 128:]
    for j in range(RING):
        o_upbias[2 * j : 2 * j + 1, :] = small[8 + j : 9 + j, :128]
        o_upbias[2 * j + 1 : 2 * j + 2, :] = small[8 + j : 9 + j, 128:]
    for copy in saves:
        copy.wait()


def run_finish(*args):
    vmem = pl.BlockSpec(memory_space=pltpu.VMEM)
    hbm = pl.BlockSpec(memory_space=pl.ANY)
    full = lambda *s: pltpu.VMEM(s, f32)
    shape = lambda *s: jax.ShapeDtypeStruct(s, f32)
    big = [(D, D), (D, D), (COLS, D), (3, D, COLS), (COLS, D), (D, COLS), (D, COLS), (D, COLS)]
    return pl.pallas_call(
        finish,
        out_shape=[jax.ShapeDtypeStruct((ROWS, COLS), bf16), shape(48, ROWS)]
        + [shape(*s) for s in big]
        + [shape(VARS, PATCH, COLS), shape(VARS, COLS), shape(LONGEST, COLS)]
        + [shape(2, 128)] * 8 + [shape(8, 128)],
        in_specs=[vmem] * 6 + [hbm] * 2,
        out_specs=[hbm] * 10 + [vmem] * 12,
        scratch_shapes=[
            pltpu.VMEM((D, COLS), bf16), pltpu.VMEM((8, 128), bf16),
            full(D, D), full(D, D), full(COLS, D), full(3, D, COLS), full(COLS, D),
            full(D, COLS), full(D, COLS), full(D, COLS),
            pltpu.SemaphoreType.DMA((2,)), pltpu.SemaphoreType.DMA((10,)),
        ],
        compiler_params=pltpu.CompilerParams(vmem_limit_bytes=FINISH_VMEM),
    )(*[pltpu.with_memory_space_constraint(a, pltpu.VMEM if i < 6 else pltpu.HBM) for i, a in enumerate(args)])


def shards(
    patches, item_lengths, cotangent, patch_weight, var_embed, agg_query, agg_wq, agg_wk, agg_wv,
    agg_wo, agg_bias, pos_table, first_gain, first_shift, attn_qkv, attn_out, attn_bias,
    second_gain, second_shift, mlp_up, up_bias, mlp_down, down_bias,
):
    tiled = lambda v: v.reshape(v.shape[0] // 128, 128)
    block, patch, summed, terms, small, query = run_chain(
        item_lengths, patches.T, patch_weight, var_embed, tiled(agg_query), tiled(first_gain),
        tiled(first_shift), tiled(attn_bias), tiled(second_gain), tiled(second_shift),
        tiled(down_bias), tiled(up_bias), tiled(agg_bias),
        agg_wq, agg_wk, agg_wv, agg_wo, pos_table, attn_qkv.transpose(1, 0, 2), attn_out,
        mlp_up, mlp_down, cotangent,
    )
    (
        block, patch, g_down, g_up, g_out, g_qkv, g_wo, g_wv, g_wk, g_wq, g_pw, g_ve, g_pos,
        g_agg_bias, g_aq, g_gain1, g_shift1, g_attn_bias, g_gain2, g_shift2, g_down_bias, g_up_bias,
    ) = run_finish(summed, block, patch, terms, small, query, tiled(agg_query), agg_wk)
    flat = lambda v: v.reshape(-1)
    return (
        block, patch.T, g_pw, g_ve, flat(g_aq), g_wq, g_wk, g_wv, g_wo, flat(g_agg_bias), g_pos,
        flat(g_gain1), flat(g_shift1), g_qkv.transpose(1, 0, 2), g_out, flat(g_attn_bias),
        flat(g_gain2), flat(g_shift2), g_up, flat(g_up_bias), g_down, flat(g_down_bias),
    )


def solution(mesh):
    rows = P(("dp", "pipe"), None)
    cols = P(None, "tensor")
    split = P("tensor", None)
    part = P("tensor")
    both = P(("dp", "pipe"), "tensor")
    last = P(None, None, "tensor")
    return jax.shard_map(
        shards,
        mesh=mesh,
        in_specs=(
            rows, P("dp", None), rows, P(), P(), P(), cols, cols, cols, split, part, cols, P(), P(),
            last, split, P(), P(), P(), cols, part, split, P(),
        ),
        out_specs=(
            both, both, last, cols, part, cols, cols, cols, split, part, cols, part, part, last,
            split, part, part, part, cols, part, split, part,
        ),
        check_vma=False,
    )
```

```python
import jax
import jax.numpy as jnp
from jax import lax
from jax.experimental import pallas as pl
from jax.experimental.pallas import tpu as pltpu
from jax.sharding import PartitionSpec as P

D = 1024
HEAD_DIM = 64
VARS = 48
PATCH = 4
LONGEST = 96
RING = 4
ROWS = 128
OWN = ROWS // RING
COLS = D // RING
HEADS = COLS // HEAD_DIM
HALF = 64
TERMS = 6 * HALF

AT_DOWN = 0
AT_UP = 4096
AT_OUT = 8192
AT_QKV = 9216
AT_WO = 12288
AT_LAST = 13312
PAY = 14336
AT_TERMS = PAY
ALL = PAY + 512
SEGMENTS = ((AT_DOWN, 4096), (AT_UP, 4096), (AT_OUT, 4096), (AT_WO, 1024), (AT_LAST, 1024))
CUBE = (True, True, False, False, False)
HALF_LAST = 512
AT_POS = AT_LAST + HALF_LAST + 128
SMALL = 32

norm_eps = 1e-05
root_half = 0.7071067811865476
inv_root_tau = 0.3989422804014327
score_scale = HEAD_DIM ** (-0.5)
highest = lax.Precision.HIGHEST
f32 = jnp.float32
bf16 = jnp.bfloat16
MESH = pl.DeviceIdType.MESH


def wide(v):
    return v.astype(f32)


def dot(left, right, dims, precision=None):
    return lax.dot_general(left, right, (dims, ((), ())), precision=precision, preferred_element_type=f32)


def mm(a, b, **kw):
    return dot(a, b, ((1,), (0,)), **kw)


def mm_nt(a, b, **kw):
    return dot(a, b, ((1,), (1,)), **kw)


def mm_tn(a, b, **kw):
    return dot(a, b, ((0,), (0,)), **kw)


def iota(shape, axis):
    return lax.broadcasted_iota(jnp.int32, shape, axis)


def norm_parts(x):
    centred = x - jnp.mean(x, axis=-1, keepdims=True)
    inverse = lax.rsqrt(jnp.mean(centred * centred, axis=-1, keepdims=True) + norm_eps)
    return centred * inverse, inverse


def norm_back(grad, xhat, inverse, gain):
    scaled = grad * gain
    return inverse * (
        scaled
        - jnp.mean(scaled, axis=-1, keepdims=True)
        - xhat * jnp.mean(scaled * xhat, axis=-1, keepdims=True)
    )


def col_sum(a):
    return jnp.sum(a, axis=0, keepdims=True)


WEIGHTS = (
    "patches", "pw", "ve", "aq", "gain1", "shift1", "abias", "gain2", "shift2", "dbias", "ubias", "aggbias",
    "wq", "wk", "wv", "wo", "pos", "wqkv", "wout", "wup", "wdown", "dy",
)
EARLY = ("aq", "wq", "pw", "ve", "wk", "wv", "patches", "wo", "pos", "aggbias")


def as_row(ref):
    value = wide(ref[...])
    return jnp.concatenate([value[i : i + 1, :] for i in range(value.shape[0])], axis=1)


def in_two(value):
    high = wide(value.astype(bf16))
    return jnp.concatenate([high, value - high], axis=0).astype(bf16)


def score_place(n):
    c, j = n // 16, n % 16
    return AT_LAST + c * HALF_LAST + 256 + 16 * (4 * (j % 4) + j // 4)


POINTS = {
    "up": ((0, 1), (1, 1)),
    "e2": (),
    "block": ((0, 2),),
    "out": ((0, 3), (1, 2), (2, 1), (0, 4)),
    "e1": ((1, 3),),
    "last": ((1, 4), (2, 2), (0, 5)),
    "wo": ((4, 1),),
}
TAIL = (
    (1, 5), (3, 1), (0, 6), (2, 3), "v", (1, 6), (4, 2), "v", (3, 2), (0, 7), (2, 4), (1, 7), (4, 3), "t", "v",
    (3, 3), (0, 8), "t", (2, 5), (1, 8), (4, 4), "v", (3, 4), (2, 6), (0, 9), "t", (1, 9), (0, 10), (4, 5),
    (1, 10), "t", (3, 5), (4, 6), "t", (3, 6),
)


def chain(
    lengths, hpatches, hpw, hve, haq, hgain1, hshift1, habias, hgain2, hshift2, hdbias,
    hubias, haggbias,
    hq, hk, hv, ho, hpos, hqkv, hout, hup, hdown, hdy,
    got_block, patch_sum, tot, terms, total_small, query_row,
    patches, pw, ve, aq_in, gain1_in, shift1_in, abias_in, gain2_in, shift2_in, dbias_in,
    ubias_in, aggbias_in,
    wq, wk, wv, pos, wqkv, wup, wdown, dy, all_wo, all_out,
    pwf, shares, vterms, kterms, kdir, soft, x3, onehot,
    part, rs_in, stream, normed, resid, normed2, g_resid, g_stream, dbias_rows, block_in,
    put_rows, g_att, g_mixed,
    mixed, qkv, probs, att_all, active, g_pre, masked,
    got_patch, put_patch, got_gain, put_gain, small, score_sum,
    got_aq, put_aq, got_terms, put_terms, rd_out, rd_in,
    pay, sum_in,
    load_sem, y_send, rs_recv, ag_recv, end_recv, sum_send, sum_recv, extra_recv, rd_recv, other_send, weight_recv, weight_send,
):
    y = lax.axis_index("tensor")
    pipe = lax.axis_index("pipe")
    dp = lax.axis_index("dp")
    x, z = lax.rem(dp, 4), dp // 4
    own_rows = pl.ds(pl.multiple_of(y * OWN, OWN), OWN)
    own_cols = pl.ds(pl.multiple_of(y * COLS, COLS), COLS)
    own_block = own_cols
    barrier = pltpu.get_barrier_semaphore()
    rings = {"x": (x, lambda q: {"dp": 4 * z + q}), "z": (z, lambda q: {"dp": 4 * q + x})}
    neighbours = [{"pipe": 1 - pipe}]
    for j in (1, 2, 3):
        neighbours.append({"tensor": lax.rem(y + j, RING)})
        neighbours += [at(lax.rem(p + j, RING)) for p, at in rings.values()]
    for device in neighbours:
        pl.semaphore_signal(barrier, inc=1, device_id=device, device_id_type=MESH)
    dims = {
        "core": (pipe, {"pipe": 1 - pipe}),
        "xa": (lax.rem((x + 1) // 2, 2), {"dp": dp + 1 - 2 * lax.rem(x, 2)}),
        "xb": (x // 2, {"dp": 4 * z + 3 - x}),
        "za": (lax.rem((z + 1) // 2, 2), {"dp": dp + 4 - 8 * lax.rem(z, 2)}),
        "zb": (z // 2, {"dp": 4 * (3 - z) + x}),
    }
    ring = ("xa", "za", "xb", "zb")
    orders = [ring[k:] + ring[:k] for k in range(4)]
    ring_orders = (("x", "z"), ("z", "x"))
    loads = {
        name: pltpu.make_async_copy(src, dst, load_sem.at[i])
        for i, (name, src, dst) in enumerate(zip(
            WEIGHTS,
            (hpatches, hpw, hve, haq, hgain1, hshift1, habias, hgain2, hshift2, hdbias, hubias, haggbias,
             hq, hk, hv, ho, hpos, hqkv, hout, hup, hdown, hdy),
            (patches, pw, ve, aq_in, gain1_in, shift1_in, abias_in, gain2_in, shift2_in, dbias_in,
             ubias_in, aggbias_in,
             wq, wk, wv, all_wo.at[own_block], pos.at[pl.ds(0, LONGEST)], wqkv, all_out.at[own_block],
             wup, wdown, dy),
        ))
    }
    for name in EARLY + tuple(name for name in WEIGHTS if name not in EARLY):
        loads[name].start()

    def wait_for(like, sem):
        pltpu.make_async_copy(like, like, sem).wait()

    def wait_rows(count, sem):
        wait_for(tot.at[pl.ds(0, count)], sem)

    sent_rows = [0] * len(SEGMENTS)

    def to_partner(src, dst, send, recv, dim):
        return pltpu.make_async_remote_copy(
            src_ref=src, dst_ref=dst, send_sem=send, recv_sem=recv,
            device_id=dims[dim][1], device_id_type=MESH,
        )

    def rows_at(start, length):
        return pl.ds(pl.multiple_of(start, 16), length)

    def region(base, length, order, steps):
        for dim in order[:steps]:
            length //= 2
            base = base + dims[dim][0] * length
        return base, length

    def part_of(seg, k, steps):
        at, count = SEGMENTS[seg]
        return region(at + pipe * (count // 2) + k * (count // 8), count // 8, orders[k], steps)

    in_at = {}
    place_in = 0
    for seg, (_, count) in enumerate(SEGMENTS):
        in_at[seg, "core"] = place_in
        place_in += count // 2
        for s in range(4):
            for k in range(4):
                if CUBE[seg]:
                    in_at[seg, s, k] = place_in
                    place_in += count // 16 >> s
        for s in range(2):
            for k in range(2):
                if not CUBE[seg]:
                    in_at[seg, s, k] = place_in
                    place_in += 3 * (count // 16 >> 2 * s)
    assert place_in <= sum_in.shape[0]

    def core_halving(seg):
        at, count = SEGMENTS[seg]
        half = count // 2
        return to_partner(
            pay.at[rows_at(at + (1 - pipe) * half, half)], sum_in.at[pl.ds(in_at[seg, "core"], half)],
            sum_send.at[seg], sum_recv.at[seg, 0], "core",
        )

    def halving(seg, s, k):
        base, length = part_of(seg, k, s)
        dim = orders[k][s]
        length //= 2
        return to_partner(
            pay.at[rows_at(base + (1 - dims[dim][0]) * length, length)],
            sum_in.at[pl.ds(in_at[seg, s, k], length)], sum_send.at[seg], sum_recv.at[seg, 1 + s], dim,
        )

    def doubling(seg, t, k):
        rows = rows_at(*part_of(seg, k, t + 1))
        return to_partner(
            tot.at[rows], tot.at[rows], sum_send.at[seg], sum_recv.at[seg, 5 + t], orders[k][t]
        )

    def core_doubling(seg):
        at, count = SEGMENTS[seg]
        rows = rows_at(at + pipe * (count // 2), count // 2)
        return to_partner(tot.at[rows], tot.at[rows], sum_send.at[seg], sum_recv.at[seg, 9], "core")

    def ring_copy(src_rows, src, dst, sems, dim, j):
        position, device = rings[dim]
        return pltpu.make_async_remote_copy(
            src_ref=src.at[src_rows], dst_ref=dst, send_sem=sems[0], recv_sem=sems[1],
            device_id=device(lax.rem(position + j, RING)), device_id_type=MESH,
        )

    def share(base, length, order, steps):
        for dim in order[:steps]:
            length //= RING
            base = base + rings[dim][0] * length
        return base, length

    def share_of(seg, k, steps):
        at, count = SEGMENTS[seg]
        return share(at + pipe * (count // 2) + k * (count // 4), count // 4, ring_orders[k], steps)

    def ring_scatter(seg, s, k):
        base, length = share_of(seg, k, s)
        length //= RING
        dim = ring_orders[k][s]
        position = rings[dim][0]
        sems = (sum_send.at[seg], sum_recv.at[seg, 1 + s])
        return [
            ring_copy(
                rows_at(base + lax.rem(position + j, RING) * length, length), pay,
                sum_in.at[pl.ds(in_at[seg, s, k] + (j - 1) * length, length)],
                sems, dim, j,
            )
            for j in (2, 1, 3)
        ]

    def ring_gather(base_length, dim, sems):
        rows = rows_at(*base_length)
        return [ring_copy(rows, tot, tot.at[rows], sems, dim, j) for j in (2, 1, 3)]

    def ring_gather_of(seg, t, k):
        sems = (sum_send.at[seg], sum_recv.at[seg, 3 + t])
        return ring_gather(share_of(seg, k, t + 1), ring_orders[k][t], sems)

    def launch_all(seg, copies, rows):
        for copy in copies:
            copy.start()
        sent_rows[seg] += len(copies) * rows

    def ring_advance(seg, stage):
        at, count = SEGMENTS[seg]
        half, quarter = count // 2, count // 4
        if stage == 0:
            launch_all(seg, [core_halving(seg)], half)
        elif stage == 1:
            wait_rows(half, sum_recv.at[seg, 0])
            for k in range(2):
                rows = rows_at(at + pipe * half + k * quarter, quarter)
                came = pl.ds(in_at[seg, "core"] + k * quarter, quarter)
                pay[rows, :] = pay[rows, :] + sum_in[came, :]
                launch_all(seg, ring_scatter(seg, 0, k), quarter // 4)
        elif stage <= 3:
            s = stage - 2
            length = quarter >> 2 * (s + 1)
            wait_rows(6 * length, sum_recv.at[seg, 1 + s])
            for k in range(2):
                rows = rows_at(*share_of(seg, k, s + 1))
                total = wide(pay[rows, :])
                for j in range(3):
                    total = total + wide(sum_in[pl.ds(in_at[seg, s, k] + j * length, length), :])
                if s == 0:
                    pay[rows, :] = total.astype(bf16)
                    launch_all(seg, ring_scatter(seg, 1, k), length // 4)
                else:
                    tot[rows, :] = total.astype(bf16)
                    launch_all(seg, ring_gather_of(seg, 1, k), length)
        elif stage <= 5:
            t = 5 - stage
            length = quarter >> 2 * (t + 1)
            wait_rows(6 * length, sum_recv.at[seg, 3 + t])
            if t:
                for k in range(2):
                    launch_all(seg, ring_gather_of(seg, 0, k), quarter // 4)
            else:
                launch_all(seg, [core_doubling(seg)], half)
        else:
            wait_rows(half, sum_recv.at[seg, 9])

    def advance(seg, stage):
        if not CUBE[seg]:
            return ring_advance(seg, stage)
        at, count = SEGMENTS[seg]
        half, quarter = count // 2, count // 8
        if stage == 0:
            launch_all(seg, [core_halving(seg)], half)
        elif stage == 1:
            wait_rows(half, sum_recv.at[seg, 0])
            for k in range(4):
                rows = rows_at(at + pipe * half + k * quarter, quarter)
                came = pl.ds(in_at[seg, "core"] + k * quarter, quarter)
                pay[rows, :] = pay[rows, :] + sum_in[came, :]
                launch_all(seg, [halving(seg, 0, k)], quarter // 2)
        elif stage <= 5:
            s = stage - 2
            length = quarter >> (s + 1)
            wait_rows(4 * length, sum_recv.at[seg, 1 + s])
            for k in range(4):
                rows = rows_at(*part_of(seg, k, s + 1))
                total = pay[rows, :] + sum_in[pl.ds(in_at[seg, s, k], length), :]
                if s < 3:
                    pay[rows, :] = total
                    launch_all(seg, [halving(seg, s + 1, k)], length // 2)
                else:
                    tot[rows, :] = total
                    launch_all(seg, [doubling(seg, 3, k)], length)
        elif stage <= 9:
            t = 9 - stage
            length = quarter >> (t + 1)
            wait_rows(4 * length, sum_recv.at[seg, 5 + t])
            if t:
                for k in range(4):
                    launch_all(seg, [doubling(seg, t - 1, k)], 2 * length)
            else:
                launch_all(seg, [core_doubling(seg)], half)
        else:
            wait_rows(half, sum_recv.at[seg, 9])

    def point(name):
        for seg, stage in POINTS[name]:
            advance(seg, stage)

    def remote(src, dst, send, recv, j):
        return pltpu.make_async_remote_copy(
            src_ref=src, dst_ref=dst, send_sem=send, recv_sem=recv,
            device_id={"tensor": lax.rem(y + j, RING)}, device_id_type=MESH,
        )

    def rows_of(j):
        return pl.ds(pl.multiple_of(lax.rem(y + j, RING) * OWN, OWN), OWN)

    def scatter(phase):
        for j in (2, 1, 3):
            remote(part.at[phase, rows_of(j)], rs_in.at[phase, j - 1], y_send.at[0], rs_recv.at[phase], j).start()

    def scattered(phase):
        total = wide(part[phase, own_rows, :])
        wait_for(rs_in.at[phase], rs_recv.at[phase])
        for j in range(3):
            total = total + wide(rs_in[phase, j])
        return total

    def gather(phase, full):
        for j in (2, 1, 3):
            remote(full.at[own_rows], full.at[own_rows], y_send.at[1], ag_recv.at[phase], j).start()

    def gathered(phase):
        wait_for(part.at[phase, pl.ds(0, 3 * OWN)], ag_recv.at[phase])

    def exchange(i, put, got):
        for j in (2, 1, 3):
            remote(put.at[lax.rem(y + j, RING)], got.at[j - 1], y_send.at[2 + i], end_recv.at[i], j).start()

    def weight_step(i, step):
        whole = (all_wo, all_out)[i]
        recv = weight_recv.at[4 * i + step]
        send = weight_send.at[i]

        def block(owner, row, count, col, width):
            rows = pl.ds(pl.multiple_of(owner * COLS + row, 16), count)
            return whole.at[rows, pl.ds(pl.multiple_of(col, 256), width)]

        others = [lax.rem(y + j, RING) for j in (2, 1, 3)]
        if step == 3:
            for owner in others:
                ref = block(owner, 0, COLS, 512 * pipe, 512)
                to_partner(ref, ref, send, recv, "core").start()
            return
        for h, (first_dim, then) in enumerate(ring_orders):
            col = 512 * pipe + 256 * h
            first_at, then_at = rings[first_dim][0], rings[then][0]
            if step == 0:
                ref = block(y, 16 * (4 * then_at + first_at), 16, col, 256)
                for j in (2, 1, 3):
                    remote(ref, ref, send, recv, j).start()
                continue
            position, device = rings[(first_dim, then)[step - 1]]
            for owner in others:
                if step == 1:
                    ref = block(owner, 16 * (4 * then_at + first_at), 16, col, 256)
                else:
                    ref = block(owner, 64 * then_at, 64, col, 256)
                for j in (2, 1, 3):
                    pltpu.make_async_remote_copy(
                        src_ref=ref, dst_ref=ref, send_sem=send, recv_sem=recv,
                        device_id=device(lax.rem(position + j, RING)), device_id_type=MESH,
                    ).start()

    def weight_wait(i, step):
        wait_rows((96, 288, 1152, 1536)[step], weight_recv.at[4 * i + step])

    def rows_exchange(put, into, i):
        for j in (2, 1, 3):
            remote(put.at[lax.rem(y + j, RING)], into.at[own_rows], y_send.at[2 + i], end_recv.at[i], j).start()
        into[own_rows, :] = put[y]

    for c in range(2):
        at = AT_LAST + c * HALF_LAST
        pay[at : at + HALF_LAST, :] = jnp.zeros((HALF_LAST, COLS), bf16)

    first, second = lengths[pipe, 0], lengths[pipe, 1]
    both = first + second

    def segment_of(r):
        return (r >= first).astype(jnp.int32) + (r >= both).astype(jnp.int32)

    same_item = segment_of(iota((ROWS, ROWS), 0)) == segment_of(iota((ROWS, ROWS), 1))
    row = iota((ROWS, 128), 0)
    place = row - jnp.where(row >= first, first, 0) - jnp.where(row >= both, second, 0)
    onehot[...] = jnp.where(place == iota((ROWS, 128), 1), 1.0, 0.0).astype(bf16)
    pos[LONGEST:, :] = jnp.zeros((128 - LONGEST, COLS), bf16)

    loads["pw"].wait()
    loads["ve"].wait()
    r, c = iota((4 * HALF, VARS * PATCH), 0), iota((4 * HALF, VARS * PATCH), 1)
    pick = jnp.where((c == PATCH * (r % HALF) + r // HALF) & (r % HALF < VARS), 1.0, 0.0).astype(bf16)
    for v in range(VARS):
        pwf[PATCH * v : PATCH * (v + 1), :] = wide(pw[v])
    terms[: 4 * HALF, :] = mm(pick, pwf[...].astype(bf16)).astype(bf16)
    terms[4 * HALF : 4 * HALF + VARS, :] = ve[...]
    terms[4 * HALF + VARS :, :] = jnp.zeros((TERMS - 4 * HALF - VARS, D), bf16)
    r, c = iota((VARS * PATCH, 4 * HALF), 1), iota((VARS * PATCH, 4 * HALF), 0)
    pick_back = jnp.where((c == PATCH * (r % HALF) + r // HALF) & (r % HALF < VARS), 1.0, 0.0).astype(bf16)
    loads["patches"].wait()
    x3[:, : 4 * HALF] = mm_tn(patches[...], pick_back)
    lane = iota((ROWS, 128), 1)
    x3[:, 4 * HALF :] = jnp.where(lane < VARS, 1.0, 0.0)

    loads["wq"].wait()
    loads["aq"].wait()
    aq_row = as_row(aq_in)
    query = mm(jnp.broadcast_to(aq_row, (8, D)).astype(bf16), wq[...])[0:1, :].astype(bf16)
    query_row[...] = jnp.broadcast_to(wide(query), (8, COLS))
    head_of = iota((8, COLS), 1) // HEAD_DIM
    block = jnp.where(
        head_of == iota((8, COLS), 0) % HEADS, jnp.broadcast_to(wide(query), (8, COLS)), 0.0
    ).astype(bf16)
    loads["wk"].wait()
    key_dir = mm_nt(block, wk[...]) * score_scale
    split = in_two(key_dir[:HEADS, :])
    kdir[...] = jnp.concatenate([wide(split), jnp.zeros((120, D), f32)], axis=0).astype(bf16)
    key_parts = mm_nt(split, terms[...])
    kterms[...] = key_parts + pltpu.roll(key_parts, HEADS, 0)
    loads["wv"].wait()
    vterms[...] = mm(terms[...], wv[...]).astype(bf16)

    def fold(v):
        folded = v[:, :128] + v[:, 128:256] + v[:, 256:]
        return folded + pltpu.roll(folded, HALF, 1)

    def thrice(v):
        return jnp.concatenate([v, v, v], axis=1)

    for h in range(HEADS):
        scores = fold(x3[...] * kterms[h : h + 1, :])
        scores = jnp.where(lane % HALF < VARS, scores, -1e30)
        raised = jnp.exp(scores - jnp.max(scores, axis=-1, keepdims=True))
        weights = raised / (0.5 * jnp.sum(raised, axis=-1, keepdims=True))
        soft[h] = weights
        shares[h * ROWS : (h + 1) * ROWS, :] = (x3[...] * thrice(weights)).astype(bf16)

    col_head = iota((ROWS, COLS), 1) // HEAD_DIM

    def pick_heads(stacked):
        total = jnp.zeros((ROWS, COLS), f32)
        for h in range(HEADS):
            total = jnp.where(col_head == h, stacked[h * ROWS : (h + 1) * ROWS, :], total)
        return total

    def spread_heads(value):
        for h in range(HEADS):
            masked[h * ROWS : (h + 1) * ROWS, :] = jnp.where(col_head == h, value, 0.0).astype(bf16)

    mixed[...] = pick_heads(mm(shares[...], vterms[...])).astype(bf16)
    loads["wo"].wait()
    loads["pos"].wait()
    loads["aggbias"].wait()
    aggbias_row = as_row(aggbias_in)
    for j in range(RING):
        cols = slice(j * COLS, (j + 1) * COLS)
        part[0, :, cols] = mm(mixed[...], all_wo[own_block, cols]).astype(bf16)
    extra = mm(mixed[...], all_wo[own_block, own_cols]) + mm(onehot[...], pos[...]) + aggbias_row
    part[0, :, own_cols] = extra.astype(bf16)
    pl.semaphore_wait(barrier, len(neighbours))
    scatter(0)
    for name in ("gain1", "shift1", "abias", "gain2", "shift2", "dbias", "ubias"):
        loads[name].wait()
    gain1_row, shift1_row = as_row(gain1_in), as_row(shift1_in)
    abias_row, gain2_row, shift2_row = as_row(abias_in), as_row(gain2_in), as_row(shift2_in)
    dbias_row, ubias_row = as_row(dbias_in), as_row(ubias_in)
    loads["wout"].wait()
    weight_step(1, 0)
    weight_step(0, 0)
    dbias_rows[...] = jnp.broadcast_to(dbias_row, (8, D))
    for i in (1, 0):
        weight_wait(i, 0)
        weight_step(i, 1)
    stream[own_rows, :] = scattered(0).astype(bf16)
    gather(0, stream)
    loads["wqkv"].wait()
    weight_wait(1, 1)
    weight_step(1, 2)
    gathered(0)
    xhat, _ = norm_parts(wide(stream[...]))
    normed[...] = (xhat * gain1_row + shift1_row).astype(bf16)

    for j in range(3):
        qkv[j] = mm(normed[...], wqkv[j]).astype(bf16)
    spread_heads(qkv[0])
    raw = mm_nt(masked[...], qkv[1]) * score_scale
    for h in range(HEADS):
        rows = slice(h * ROWS, (h + 1) * ROWS)
        score = jnp.where(same_item, raw[rows, :], -1e30)
        raised = jnp.exp(score - jnp.max(score, axis=-1, keepdims=True))
        probs[rows, :] = raised / jnp.sum(raised, axis=-1, keepdims=True)
    attended = pick_heads(mm(probs[...].astype(bf16), qkv[2])).astype(bf16)
    att_all[y] = attended
    for j in (2, 1, 3):
        remote(att_all.at[y], att_all.at[y], y_send.at[1], ag_recv.at[1], j).start()
    weight_wait(1, 2)
    weight_step(1, 3)
    weight_wait(0, 1)
    weight_step(0, 2)
    loads["wup"].wait()
    loads["wdown"].wait()
    loads["dy"].wait()
    weight_wait(1, 3)
    gathered(1)
    for j in range(RING):
        cols = slice(j * COLS, (j + 1) * COLS)
        total = wide(stream[:, cols]) + abias_row[:, cols]
        for i in range(RING):
            total = total + mm(att_all[i], all_out[i * COLS : (i + 1) * COLS, cols])
        resid[:, cols] = total
    xhat, _ = norm_parts(resid[...])
    normed2[...] = (xhat * gain2_row + shift2_row).astype(bf16)

    for j in range(RING):
        cols = slice(j * COLS, (j + 1) * COLS)
        pre = mm(normed2[...], wup[:, cols]) + ubias_row[:, cols]
        half_cdf = 0.5 * (1.0 + lax.erf(pre * root_half))
        active[:, cols] = (pre * half_cdf).astype(bf16)
        slope = half_cdf + pre * jnp.exp(-0.5 * pre * pre) * inv_root_tau
        grad = (mm_nt(dy[...], wdown[cols, :]) * slope).astype(bf16)
        g_pre[:, cols] = grad
        small[8 + j : 9 + j, :] = col_sum(wide(grad))
    for j in range(RING):
        rows = slice(j * COLS, (j + 1) * COLS)
        part[3, :, rows] = mm_nt(g_pre[...], wup[rows, :]).astype(bf16)
    scatter(3)
    for j in range(RING):
        cols = slice(j * COLS, (j + 1) * COLS)
        part[2, :, cols] = mm(active[...], wdown[:, cols]).astype(bf16)
    for j in (2, 1, 3):
        cols = pl.ds(pl.multiple_of(lax.rem(y + j, RING) * COLS, COLS), COLS)
        remote(part.at[2, :, cols], block_in.at[j - 1], y_send.at[2], end_recv.at[0], j).start()
    weight_wait(0, 2)
    weight_step(0, 3)
    for j in range(RING):
        cols = slice(j * COLS, (j + 1) * COLS)
        pay[AT_DOWN + j * D : AT_DOWN + (j + 1) * D, :] = mm_tn(active[...], dy[:, cols]).astype(bf16)
    advance(0, 0)
    for j in range(RING):
        cols = slice(j * COLS, (j + 1) * COLS)
        pay[AT_UP + j * D : AT_UP + (j + 1) * D, :] = mm_tn(normed2[...], g_pre[:, cols]).astype(bf16)
    advance(1, 0)
    point("up")
    e2 = scattered(3)
    xhat2, inv2 = norm_parts(resid[own_rows, :])
    g_resid_own = (wide(dy[own_rows, :]) + norm_back(e2, xhat2, inv2, gain2_row)).astype(bf16)
    g_resid[own_rows, :] = g_resid_own
    for j in range(RING):
        put_rows[0, j] = mm_nt(g_resid_own, all_out[j * COLS : (j + 1) * COLS, :]).astype(bf16)
    rows_exchange(put_rows.at[0], g_att, 5)
    gather(2, g_resid)
    point("e2")
    gain2, shift2 = col_sum(e2 * xhat2), col_sum(e2)
    wait_for(block_in, end_recv.at[0])
    result = resid[:, own_cols] + wide(part[2, :, own_cols]) + dbias_rows[0:1, own_cols]
    got_block[...] = (result + wide(block_in[0]) + wide(block_in[1]) + wide(block_in[2])).astype(bf16)
    point("block")
    wait_rows(3 * OWN, end_recv.at[5])

    spread_heads(g_att[...])
    g_probs = mm_nt(masked[...], qkv[2])
    g_v = mm_tn(probs[...].astype(bf16), masked[...]).astype(bf16)
    p = probs[...]
    g_scores = (p * (g_probs - jnp.sum(p * g_probs, axis=-1, keepdims=True))).astype(bf16)
    g_q = (pick_heads(mm(g_scores, qkv[1])) * score_scale).astype(bf16)
    spread_heads(qkv[0])
    g_k = (mm_tn(g_scores, masked[...]) * score_scale).astype(bf16)
    for j in range(RING):
        rows = slice(j * COLS, (j + 1) * COLS)
        total = mm_nt(g_q, wqkv[0, rows, :]) + mm_nt(g_k, wqkv[1, rows, :])
        part[4, :, rows] = (total + mm_nt(g_v, wqkv[2, rows, :])).astype(bf16)
    scatter(4)
    for j, g in enumerate((g_q, g_k, g_v)):
        pay[AT_QKV + j * D : AT_QKV + (j + 1) * D, :] = mm_tn(normed[...], g).astype(bf16)
    gathered(2)
    attended_own = att_all[y]
    for j in range(RING):
        cols = slice(j * COLS, (j + 1) * COLS)
        pay[AT_OUT + j * COLS : AT_OUT + (j + 1) * COLS, :] = mm_tn(
            attended_own, g_resid[:, cols]
        ).astype(bf16)
    advance(2, 0)
    point("out")
    e1 = scattered(4)
    xhat1, inv1 = norm_parts(wide(stream[own_rows, :]))
    g_stream_own = (
        wide(g_resid[own_rows, :]) + norm_back(e1, xhat1, inv1, gain1_row)
    ).astype(bf16)
    g_stream[own_rows, :] = g_stream_own
    weight_wait(0, 3)
    for j in range(RING):
        put_rows[1, j] = mm_nt(g_stream_own, all_wo[j * COLS : (j + 1) * COLS, :]).astype(bf16)
    rows_exchange(put_rows.at[1], g_mixed, 6)
    gather(3, g_stream)
    gain1, shift1 = col_sum(e1 * xhat1), col_sum(e1)
    for j in range(RING):
        cols = slice(j * COLS, (j + 1) * COLS)
        for i, v in enumerate((gain1, shift1, gain2, shift2)):
            put_gain[j, i : i + 1, :] = v[:, cols]
        put_gain[j, 4:8, :] = jnp.zeros((4, COLS), f32)
    exchange(1, put_gain, got_gain)
    point("e1")
    wait_rows(3 * OWN, end_recv.at[6])

    spread_heads(g_mixed[...])
    by_term = mm_nt(masked[...], vterms[...])
    grad_patch = jnp.zeros((ROWS, 4 * HALF), f32)
    for h in range(HEADS):
        mine = by_term[h * ROWS : (h + 1) * ROWS, :]
        weights = soft[h]
        g_weights = fold(x3[...] * mine)
        g_sc = weights * (
            g_weights - 0.5 * jnp.sum(weights * g_weights, axis=-1, keepdims=True)
        )
        g_sc2 = jnp.concatenate([g_sc, g_sc], axis=1)
        w2 = jnp.concatenate([weights, weights], axis=1)
        grad_patch = grad_patch + g_sc2 * kterms[h : h + 1, : 4 * HALF] + w2 * mine[:, : 4 * HALF]
        sums = col_sum(x3[...] * thrice(g_sc))
        score_sum[h : h + 1, :] = sums
    value_sum = mm_tn(shares[...], masked[...]).astype(bf16)
    pay[AT_LAST : AT_LAST + 256, :] = value_sum[:256, :]
    pay[AT_LAST + HALF_LAST : AT_LAST + HALF_LAST + 128, :] = value_sum[256:, :]
    head_cols = iota((HEADS, COLS), 1)
    spot = jnp.where((head_cols % HEADS == iota((HEADS, COLS), 0)) & (head_cols < 8), 1.0, 0.0).astype(bf16)
    across = mm_tn(score_sum[...].astype(bf16), spot).astype(bf16)
    for n in range(TERMS // 16):
        at = score_place(n)
        pay[at : at + 16, :] = across[16 * n : 16 * (n + 1), :]
    gathered(3)
    g_own = g_stream[:, own_cols]
    pay[AT_POS : AT_POS + LONGEST, :] = mm_tn(onehot[...], g_own)[:LONGEST, :].astype(bf16)
    advance(4, 0)
    point("last")
    for j in range(RING):
        cols = slice(j * COLS, (j + 1) * COLS)
        pay[AT_WO + j * COLS : AT_WO + (j + 1) * COLS, :] = mm_tn(
            mixed[...], g_stream[:, cols]
        ).astype(bf16)
    advance(3, 0)
    point("wo")
    along = mm(in_two(score_sum[...]), terms[...])
    along = in_two(along[:HEADS] + along[HEADS:])
    head_of = iota((8, COLS), 1) // HEAD_DIM
    g_query = col_sum(jnp.where(head_of == iota((8, COLS), 0) % HEADS, mm(along, wk[...]), 0.0)) * score_scale
    both_parts = mm_nt(in_two(jnp.broadcast_to(g_query, (HEADS, COLS))), wq[...])
    g_aq = both_parts[0:1, :] + both_parts[HEADS : HEADS + 1, :]
    for j in range(RING):
        put_aq[j] = jnp.broadcast_to(g_aq[:, j * COLS : (j + 1) * COLS], (8, COLS))
    exchange(3, put_aq, got_aq)
    low_patch = grad_patch.astype(bf16)
    width = VARS * PATCH // RING
    r, c = iota((width, 4 * HALF), 1), iota((width, 4 * HALF), 0)
    for j in range(RING):
        pick_own = jnp.where(
            (c + width * j == PATCH * (r % HALF) + r // HALF) & (r % HALF < VARS), 1.0, 0.0
        ).astype(bf16)
        put_patch[j] = mm_nt(pick_own, low_patch).astype(bf16)
    exchange(2, put_patch, got_patch)
    small[0:1, :] = col_sum(wide(g_own))
    small[5:6, :] = col_sum(wide(g_resid[:, own_cols]))
    small[6:7, :] = col_sum(wide(dy[:, own_cols]))
    small[12:32, :] = jnp.zeros((20, COLS), f32)
    wait_for(got_gain, end_recv.at[1])
    small[1:5, :] = (put_gain[y] + got_gain[0] + got_gain[1] + got_gain[2])[0:4, :]

    def vector_step(i):
        if i == 0:
            wait_for(got_aq, end_recv.at[3])
            small[7:8, :] = (put_aq[y] + got_aq[0] + got_aq[1] + got_aq[2])[0:1, :]
            rd_out[0] = small[...]
            to_partner(rd_out.at[0], rd_in.at[0], other_send.at[0], rd_recv.at[0], "core").start()
            return
        at, n = (0, 1) if i == 1 else (3 * i - 5, 3)
        wait_for(rd_in.at[pl.ds(at, n)], rd_recv.at[i - 1])
        value = rd_out[i - 1]
        for j in range(n):
            value = value + rd_in[at + j]
        if i == 3:
            total_small[...] = value
            return
        rd_out[i] = value
        position, device = rings["xz"[i - 1]]
        for j in (2, 1, 3):
            pltpu.make_async_remote_copy(
                src_ref=rd_out.at[i], dst_ref=rd_in.at[3 * i - 3 + j], send_sem=other_send.at[0],
                recv_sem=rd_recv.at[i], device_id=device(lax.rem(position + j, RING)), device_id_type=MESH,
            ).start()

    terms_base = AT_TERMS + pipe * 256

    def terms_gather(t):
        dim = ring_orders[0][t]
        for copy in ring_gather(
            share(terms_base, 256, ring_orders[0], t + 1), dim, (other_send.at[1], extra_recv.at[t])
        ):
            copy.start()

    def terms_step(i):
        if i == 0:
            value_rows = tot[rows_at(*share_of(4, 0, 2)), :]
            score_rows = tot[rows_at(*share_of(4, 1, 2)), :]
            total = mm_nt(value_rows, wv[...]) + mm(score_rows[:, :128], kdir[...])
            for j in range(RING):
                put_terms[j] = total[:, j * COLS : (j + 1) * COLS].astype(bf16)
            exchange(4, put_terms, got_terms)
        elif i == 1:
            wait_for(got_terms, end_recv.at[4])
            total = wide(put_terms[y]) + wide(got_terms[0]) + wide(got_terms[1]) + wide(got_terms[2])
            tot[rows_at(*share(terms_base, 256, ring_orders[0], 2)), :] = total.astype(bf16)
            terms_gather(1)
        elif i == 2:
            wait_rows(48, extra_recv.at[1])
            terms_gather(0)
        elif i == 3:
            wait_rows(192, extra_recv.at[0])
            rows = rows_at(terms_base, 256)
            to_partner(tot.at[rows], tot.at[rows], other_send.at[1], extra_recv.at[2], "core").start()
        else:
            wait_rows(256, extra_recv.at[2])

    next_of = {"t": 0, "v": 0}
    for step in TAIL:
        if step == "t":
            terms_step(next_of["t"])
            next_of["t"] += 1
        elif step == "v":
            vector_step(next_of["v"])
            next_of["v"] += 1
        else:
            advance(*step)
    assert next_of == {"t": 5, "v": 4}
    wait_for(got_patch, end_recv.at[2])
    patch_sum[...] = (
        wide(put_patch[y]) + wide(got_patch[0]) + wide(got_patch[1]) + wide(got_patch[2])
    )
    for seg in range(len(SEGMENTS)):
        wait_rows(sent_rows[seg], sum_send.at[seg])
    wait_for(rs_in.at[pl.ds(0, 3)], y_send.at[0])
    wait_for(terms, y_send.at[1])
    wait_for(block_in, y_send.at[2])
    for i in (5, 6):
        wait_rows(3 * OWN, y_send.at[2 + i])
    for i in range(2):
        wait_rows(96 + 288 + 1152 + 1536, weight_send.at[i])
    for i, got in ((1, got_gain), (2, got_patch), (3, got_aq), (4, got_terms)):
        wait_for(got, y_send.at[2 + i])
    wait_for(rd_in, other_send.at[0])
    wait_rows(3 * 16 + 3 * 64 + 256, other_send.at[1])


MAIN_VMEM = 50 * 1024 * 1024
FINISH_VMEM = 50 * 1024 * 1024


def run_chain(lengths, *args):
    hbm = pl.BlockSpec(memory_space=pl.ANY)
    V = pltpu.VMEM
    low = lambda *s: V(s, bf16)
    full = lambda *s: V(s, f32)
    kept = [w for name, w in zip(WEIGHTS, args) if name not in ("wo", "wout")]
    scratch = [low(*w.shape) if w.shape[0] != LONGEST else low(128, COLS) for w in kept]
    scratch += [low(D, D), low(D, D)]
    scratch += [
        full(VARS * PATCH, D), low(HEADS * ROWS, TERMS), low(TERMS, COLS), full(8, TERMS),
        low(128, D), full(HEADS, ROWS, 128), full(ROWS, TERMS), low(ROWS, 128),
        low(5, ROWS, D), low(5, 3, OWN, D), low(ROWS, D), low(ROWS, D), full(ROWS, D),
        low(ROWS, D), low(ROWS, D), low(ROWS, D), full(8, D), low(3, ROWS, COLS),
        low(2, RING, OWN, COLS), low(ROWS, COLS), low(ROWS, COLS),
        low(ROWS, COLS), low(3, ROWS, COLS), full(HEADS * ROWS, ROWS), low(RING, ROWS, COLS),
        low(ROWS, D), low(ROWS, D), low(HEADS * ROWS, COLS),
        low(3, 48, ROWS), low(RING, 48, ROWS),
        full(3, 8, COLS), full(RING, 8, COLS), full(SMALL, COLS), full(HEADS, TERMS),
        full(3, 8, COLS), full(RING, 8, COLS), low(3, 16, COLS), low(RING, 16, COLS),
        full(3, SMALL, COLS), full(7, SMALL, COLS),
        low(PAY, COLS), low(PAY * 31 // 32, COLS),
    ]
    dma = pltpu.SemaphoreType.DMA
    scratch += [
        dma((len(args),)), dma((9,)), dma((5,)), dma((4,)), dma((7,)), dma((5,)), dma((5, 10)), dma((3,)),
        dma((3,)), dma((2,)), dma((8,)), dma((2,)),
    ]
    return pl.pallas_call(
        chain,
        out_shape=(
            low(ROWS, COLS), full(48, ROWS), low(ALL, COLS), low(TERMS, D), full(SMALL, COLS), full(8, COLS),
        ),
        in_specs=[pl.BlockSpec(memory_space=pltpu.SMEM)] + [hbm] * len(args),
        out_specs=[pl.BlockSpec(memory_space=pltpu.VMEM)] * 6,
        scratch_shapes=scratch,
        compiler_params=pltpu.CompilerParams(
            collective_id=0, has_side_effects=True, vmem_limit_bytes=MAIN_VMEM
        ),
    )(lengths, *[pltpu.with_memory_space_constraint(a, pltpu.HBM) for a in args])


VECTORS = (0, 7, 1, 2, 5, 3, 4, 6)


def finish(
    tot, block_in, patch_in, terms, small, query, aq_from, hk,
    o_block, o_patch, o_down, o_up, o_out, o_qkv, o_wo, o_wv, o_wk, o_wq,
    o_pw, o_ve, o_pos, *rest,
):
    o_vectors, o_upbias = rest[:8], rest[8]
    wk, aq_in, down, up, out, qkv, wo, gv, gk, gq, load_sem, save_sem = rest[9:]
    loads = [
        pltpu.make_async_copy(hk, wk, load_sem.at[0]), pltpu.make_async_copy(aq_from, aq_in, load_sem.at[1])
    ]
    for copy in loads:
        copy.start()
    saves = []

    def store(i, src, dst):
        copy = pltpu.make_async_copy(src, dst, save_sem.at[i])
        copy.start()
        saves.append(copy)

    for j in range(RING):
        down[:, j * COLS : (j + 1) * COLS] = wide(tot[AT_DOWN + j * D : AT_DOWN + (j + 1) * D, :])
    store(4, down, o_down)
    for j in range(RING):
        up[:, j * COLS : (j + 1) * COLS] = wide(tot[AT_UP + j * D : AT_UP + (j + 1) * D, :])
    store(5, up, o_up)
    for j in range(3):
        qkv[j] = wide(tot[AT_QKV + j * D : AT_QKV + (j + 1) * D, :])
    store(6, qkv, o_qkv)
    for j in range(RING):
        out[:, j * COLS : (j + 1) * COLS] = wide(tot[AT_OUT + j * COLS : AT_OUT + (j + 1) * COLS, :])
    store(7, out, o_out)
    for j in range(RING):
        wo[:, j * COLS : (j + 1) * COLS] = wide(tot[AT_WO + j * COLS : AT_WO + (j + 1) * COLS, :])
    store(1, wo, o_wo)
    store(8, block_in, o_block)
    store(9, patch_in, o_patch)
    for copy in loads:
        copy.wait()
    value_sum = jnp.concatenate(
        [tot[AT_LAST : AT_LAST + 256, :], tot[AT_LAST + HALF_LAST : AT_LAST + HALF_LAST + 128, :]], axis=0
    )
    gv[...] = mm_tn(terms[...], value_sum)
    store(0, gv, o_wv)
    across = jnp.concatenate(
        [tot[score_place(n) : score_place(n) + 16, :128] for n in range(TERMS // 16)], axis=0
    )
    along = in_two(mm_tn(across, terms[...])[:HEADS, :])
    head_of = iota((8, COLS), 1) // HEAD_DIM
    mine = head_of == iota((8, COLS), 0) % HEADS
    block = jnp.where(mine, query[...], 0.0).astype(bf16)
    gk[...] = mm_tn(along, block) * score_scale
    store(2, gk, o_wk)
    g_query = col_sum(jnp.where(mine, mm(along, wk[...]), 0.0)) * score_scale
    row = iota((8, D), 0)
    aq = jnp.where(row < 2, jnp.broadcast_to(as_row(aq_in), (8, D)), 0.0).astype(bf16)
    high = wide(g_query.astype(bf16))
    both = jnp.where(
        iota((8, COLS), 0) == 0,
        jnp.broadcast_to(high, (8, COLS)), jnp.broadcast_to(g_query - high, (8, COLS)),
    ).astype(bf16)
    gq[...] = mm_tn(aq, both)
    store(3, gq, o_wq)
    o_pos[...] = wide(tot[AT_POS : AT_POS + LONGEST, :])
    for p in range(PATCH):
        o_pw[:, p, :] = wide(tot[AT_TERMS + HALF * p : AT_TERMS + HALF * p + VARS, :])
    o_ve[...] = wide(tot[AT_TERMS + 4 * HALF : AT_TERMS + 4 * HALF + VARS, :])
    for ref, i in zip(o_vectors, VECTORS):
        ref[0:1, :] = small[i : i + 1, :128]
        ref[1:2, :] = small[i : i + 1, 128:]
    for j in range(RING):
        o_upbias[2 * j : 2 * j + 1, :] = small[8 + j : 9 + j, :128]
        o_upbias[2 * j + 1 : 2 * j + 2, :] = small[8 + j : 9 + j, 128:]
    for copy in saves:
        copy.wait()


def run_finish(*args):
    vmem = pl.BlockSpec(memory_space=pltpu.VMEM)
    hbm = pl.BlockSpec(memory_space=pl.ANY)
    full = lambda *s: pltpu.VMEM(s, f32)
    shape = lambda *s: jax.ShapeDtypeStruct(s, f32)
    big = [(D, D), (D, D), (COLS, D), (3, D, COLS), (COLS, D), (D, COLS), (D, COLS), (D, COLS)]
    return pl.pallas_call(
        finish,
        out_shape=[jax.ShapeDtypeStruct((ROWS, COLS), bf16), shape(48, ROWS)]
        + [shape(*s) for s in big]
        + [shape(VARS, PATCH, COLS), shape(VARS, COLS), shape(LONGEST, COLS)]
        + [shape(2, 128)] * 8 + [shape(8, 128)],
        in_specs=[vmem] * 6 + [hbm] * 2,
        out_specs=[hbm] * 10 + [vmem] * 12,
        scratch_shapes=[
            pltpu.VMEM((D, COLS), bf16), pltpu.VMEM((8, 128), bf16),
            full(D, D), full(D, D), full(COLS, D), full(3, D, COLS), full(COLS, D),
            full(D, COLS), full(D, COLS), full(D, COLS),
            pltpu.SemaphoreType.DMA((2,)), pltpu.SemaphoreType.DMA((10,)),
        ],
        compiler_params=pltpu.CompilerParams(vmem_limit_bytes=FINISH_VMEM),
    )(*[pltpu.with_memory_space_constraint(a, pltpu.VMEM if i < 6 else pltpu.HBM) for i, a in enumerate(args)])


def shards(
    patches, item_lengths, cotangent, patch_weight, var_embed, agg_query, agg_wq, agg_wk, agg_wv,
    agg_wo, agg_bias, pos_table, first_gain, first_shift, attn_qkv, attn_out, attn_bias,
    second_gain, second_shift, mlp_up, up_bias, mlp_down, down_bias,
):
    tiled = lambda v: v.reshape(v.shape[0] // 128, 128)
    block, patch, summed, terms, small, query = run_chain(
        item_lengths, patches.T, patch_weight, var_embed, tiled(agg_query), tiled(first_gain),
        tiled(first_shift), tiled(attn_bias), tiled(second_gain), tiled(second_shift),
        tiled(down_bias), tiled(up_bias), tiled(agg_bias),
        agg_wq, agg_wk, agg_wv, agg_wo, pos_table, attn_qkv.transpose(1, 0, 2), attn_out,
        mlp_up, mlp_down, cotangent,
    )
    (
        block, patch, g_down, g_up, g_out, g_qkv, g_wo, g_wv, g_wk, g_wq, g_pw, g_ve, g_pos,
        g_agg_bias, g_aq, g_gain1, g_shift1, g_attn_bias, g_gain2, g_shift2, g_down_bias, g_up_bias,
    ) = run_finish(summed, block, patch, terms, small, query, tiled(agg_query), agg_wk)
    flat = lambda v: v.reshape(-1)
    return (
        block, patch.T, g_pw, g_ve, flat(g_aq), g_wq, g_wk, g_wv, g_wo, flat(g_agg_bias), g_pos,
        flat(g_gain1), flat(g_shift1), g_qkv.transpose(1, 0, 2), g_out, flat(g_attn_bias),
        flat(g_gain2), flat(g_shift2), g_up, flat(g_up_bias), g_down, flat(g_down_bias),
    )


def solution(mesh):
    rows = P(("dp", "pipe"), None)
    cols = P(None, "tensor")
    split = P("tensor", None)
    part = P("tensor")
    both = P(("dp", "pipe"), "tensor")
    last = P(None, None, "tensor")
    return jax.shard_map(
        shards,
        mesh=mesh,
        in_specs=(
            rows, P("dp", None), rows, P(), P(), P(), cols, cols, cols, split, part, cols, P(), P(),
            last, split, P(), P(), P(), cols, part, split, P(),
        ),
        out_specs=(
            both, both, last, cols, part, cols, cols, cols, split, part, cols, part, part, last,
            split, part, part, part, cols, part, split, part,
        ),
        check_vma=False,
    )
```

```python
import jax
import jax.numpy as jnp
from jax import lax
from jax.experimental import pallas as pl
from jax.experimental.pallas import tpu as pltpu
from jax.sharding import PartitionSpec as P

D = 1024
HEAD_DIM = 64
VARS = 48
PATCH = 4
LONGEST = 96
RING = 4
ROWS = 128
OWN = ROWS // RING
COLS = D // RING
HEADS = COLS // HEAD_DIM
HALF = 64
TERMS = 6 * HALF

AT_DOWN = 0
AT_UP = 4096
AT_OUT = 8192
AT_QKV = 9216
AT_WO = 12288
AT_LAST = 13312
PAY = 14336
AT_TERMS = PAY
ALL = PAY + 512
SEGMENTS = ((AT_DOWN, 4096), (AT_UP, 4096), (AT_OUT, 4096), (AT_WO, 1024), (AT_LAST, 1024))
CUBE = (True, True, True, False, False)
HALF_LAST = 512
AT_POS = AT_LAST + HALF_LAST + 128
SMALL = 32

norm_eps = 1e-05
root_half = 0.7071067811865476
inv_root_tau = 0.3989422804014327
score_scale = HEAD_DIM ** (-0.5)
highest = lax.Precision.HIGHEST
f32 = jnp.float32
bf16 = jnp.bfloat16
MESH = pl.DeviceIdType.MESH


def wide(v):
    return v.astype(f32)


def dot(left, right, dims, precision=None):
    return lax.dot_general(left, right, (dims, ((), ())), precision=precision, preferred_element_type=f32)


def mm(a, b, **kw):
    return dot(a, b, ((1,), (0,)), **kw)


def mm_nt(a, b, **kw):
    return dot(a, b, ((1,), (1,)), **kw)


def mm_tn(a, b, **kw):
    return dot(a, b, ((0,), (0,)), **kw)


def iota(shape, axis):
    return lax.broadcasted_iota(jnp.int32, shape, axis)


def norm_parts(x):
    centred = x - jnp.mean(x, axis=-1, keepdims=True)
    inverse = lax.rsqrt(jnp.mean(centred * centred, axis=-1, keepdims=True) + norm_eps)
    return centred * inverse, inverse


def norm_back(grad, xhat, inverse, gain):
    scaled = grad * gain
    return inverse * (
        scaled
        - jnp.mean(scaled, axis=-1, keepdims=True)
        - xhat * jnp.mean(scaled * xhat, axis=-1, keepdims=True)
    )


def col_sum(a):
    return jnp.sum(a, axis=0, keepdims=True)


WEIGHTS = (
    "patches", "pw", "ve", "aq", "gain1", "shift1", "abias", "gain2", "shift2", "dbias", "ubias", "aggbias",
    "wq", "wk", "wv", "wo", "pos", "wqkv", "wout", "wup", "wdown", "dy",
)
EARLY = ("aq", "wq", "pw", "ve", "wk", "wv", "wout", "patches", "wo", "pos", "aggbias")


def as_row(ref):
    value = wide(ref[...])
    return jnp.concatenate([value[i : i + 1, :] for i in range(value.shape[0])], axis=1)


def in_two(value):
    high = wide(value.astype(bf16))
    return jnp.concatenate([high, value - high], axis=0).astype(bf16)


def score_place(n):
    c, j = n // 16, n % 16
    return AT_LAST + c * HALF_LAST + 256 + 16 * (4 * (j % 4) + j // 4)


POINTS = {
    "up": ((0, 1), (1, 1)),
    "e2": (),
    "block": ((0, 2),),
    "attn": ((1, 2),),
    "out": ((0, 3), (2, 1), (1, 3)),
    "e1": ((0, 4),),
    "last": ((2, 2), (1, 4)),
    "wo": ((0, 5),),
}
TAIL = (
    (4, 1), (3, 1), (2, 3), (1, 5), "v", (0, 6), "v", (4, 2), (3, 2), (2, 4), (1, 6), (0, 7), "v", (4, 3), "t",
    (0, 8), (3, 3), (2, 5), (1, 7), "v", "t", (4, 4), (3, 4), (2, 6), (1, 8), "t", (4, 5), (3, 5), (4, 6),
    (3, 6), (2, 7), "t", (2, 8), "t",
)


def chain(
    lengths, hpatches, hpw, hve, haq, hgain1, hshift1, habias, hgain2, hshift2, hdbias,
    hubias, haggbias,
    hq, hk, hv, ho, hpos, hqkv, hout, hup, hdown, hdy,
    got_block, patch_sum, tot, terms, total_small, query_row,
    patches, pw, ve, aq_in, gain1_in, shift1_in, abias_in, gain2_in, shift2_in, dbias_in,
    ubias_in, aggbias_in,
    wq, wk, wv, pos, wqkv, wup, wdown, dy, all_wo, all_out,
    pwf, shares, vterms, kterms, kdir, soft, x3, onehot,
    part, rs_in, stream, normed, resid, normed2, g_resid, g_stream, dbias_rows, block_in,
    put_rows, g_att, g_mixed,
    mixed, qkv, probs, att_all, active, g_pre, masked,
    got_patch, put_patch, got_gain, put_gain, small, score_sum,
    got_aq, put_aq, got_terms, put_terms, rd_out, rd_in,
    pay, sum_in,
    load_sem, y_send, rs_recv, ag_recv, end_recv, sum_send, sum_recv, extra_recv, rd_recv, other_send, weight_recv, weight_send,
):
    y = lax.axis_index("tensor")
    pipe = lax.axis_index("pipe")
    dp = lax.axis_index("dp")
    x, z = lax.rem(dp, 4), dp // 4
    own_rows = pl.ds(pl.multiple_of(y * OWN, OWN), OWN)
    own_cols = pl.ds(pl.multiple_of(y * COLS, COLS), COLS)
    own_block = own_cols
    barrier = pltpu.get_barrier_semaphore()
    rings = {"x": (x, lambda q: {"dp": 4 * z + q}), "z": (z, lambda q: {"dp": 4 * q + x})}
    neighbours = [{"pipe": 1 - pipe}]
    for j in (1, 2, 3):
        neighbours.append({"tensor": lax.rem(y + j, RING)})
        neighbours += [at(lax.rem(p + j, RING)) for p, at in rings.values()]
    for device in neighbours:
        pl.semaphore_signal(barrier, inc=1, device_id=device, device_id_type=MESH)
    dims = {
        "core": (pipe, {"pipe": 1 - pipe}),
        "xa": (lax.rem((x + 1) // 2, 2), {"dp": dp + 1 - 2 * lax.rem(x, 2)}),
        "xb": (x // 2, {"dp": 4 * z + 3 - x}),
        "za": (lax.rem((z + 1) // 2, 2), {"dp": dp + 4 - 8 * lax.rem(z, 2)}),
        "zb": (z // 2, {"dp": 4 * (3 - z) + x}),
    }
    orders = (("xa", "xb", "z"), ("za", "zb", "x"), ("xb", "xa", "z"), ("zb", "za", "x"))
    ring_orders = (("x", "z"), ("z", "x"))
    loads = {
        name: pltpu.make_async_copy(src, dst, load_sem.at[i])
        for i, (name, src, dst) in enumerate(zip(
            WEIGHTS,
            (hpatches, hpw, hve, haq, hgain1, hshift1, habias, hgain2, hshift2, hdbias, hubias, haggbias,
             hq, hk, hv, ho, hpos, hqkv, hout, hup, hdown, hdy),
            (patches, pw, ve, aq_in, gain1_in, shift1_in, abias_in, gain2_in, shift2_in, dbias_in,
             ubias_in, aggbias_in,
             wq, wk, wv, all_wo.at[own_block], pos.at[pl.ds(0, LONGEST)], wqkv, all_out.at[own_block],
             wup, wdown, dy),
        ))
    }
    for name in EARLY + tuple(name for name in WEIGHTS if name not in EARLY):
        loads[name].start()

    def wait_for(like, sem):
        pltpu.make_async_copy(like, like, sem).wait()

    def wait_rows(count, sem):
        wait_for(tot.at[pl.ds(0, count)], sem)

    sent_rows = [0] * len(SEGMENTS)

    def to_partner(src, dst, send, recv, dim):
        return pltpu.make_async_remote_copy(
            src_ref=src, dst_ref=dst, send_sem=send, recv_sem=recv,
            device_id=dims[dim][1], device_id_type=MESH,
        )

    def rows_at(start, length):
        return pl.ds(pl.multiple_of(start, 16), length)

    def region(base, length, order, steps):
        for dim in order[:steps]:
            pair = dim in dims
            length //= 2 if pair else RING
            base = base + (dims[dim] if pair else rings[dim])[0] * length
        return base, length

    def part_of(seg, k, steps):
        at, count = SEGMENTS[seg]
        return region(at + pipe * (count // 2) + k * (count // 8), count // 8, orders[k], steps)

    in_at = {}
    place_in = 0
    for seg, (_, count) in enumerate(SEGMENTS):
        in_at[seg, "core"] = place_in
        place_in += count // 2
        for s in range(3):
            for k in range(4):
                if CUBE[seg]:
                    in_at[seg, s, k] = place_in
                    place_in += count // 16 >> s if s < 2 else 3 * (count // 128)
        for s in range(2):
            for k in range(2):
                if not CUBE[seg]:
                    in_at[seg, s, k] = place_in
                    place_in += 3 * (count // 16 >> 2 * s)
    assert place_in <= sum_in.shape[0]

    def core_halving(seg):
        at, count = SEGMENTS[seg]
        half = count // 2
        return to_partner(
            pay.at[rows_at(at + (1 - pipe) * half, half)], sum_in.at[pl.ds(in_at[seg, "core"], half)],
            sum_send.at[seg], sum_recv.at[seg, 0], "core",
        )

    def halving(seg, s, k):
        base, length = part_of(seg, k, s)
        dim = orders[k][s]
        length //= 2
        return to_partner(
            pay.at[rows_at(base + (1 - dims[dim][0]) * length, length)],
            sum_in.at[pl.ds(in_at[seg, s, k], length)], sum_send.at[seg], sum_recv.at[seg, 1 + s], dim,
        )

    def doubling(seg, t, k):
        rows = rows_at(*part_of(seg, k, t + 1))
        return to_partner(
            tot.at[rows], tot.at[rows], sum_send.at[seg], sum_recv.at[seg, 5 + t], orders[k][t]
        )

    def last_scatter(seg, k):
        base, length = part_of(seg, k, 2)
        length //= RING
        dim = orders[k][2]
        sems = (sum_send.at[seg], sum_recv.at[seg, 3])
        return [
            ring_copy(
                rows_at(base + lax.rem(rings[dim][0] + j, RING) * length, length), pay,
                sum_in.at[pl.ds(in_at[seg, 2, k] + (j - 1) * length, length)], sems, dim, j,
            )
            for j in (2, 1, 3)
        ]

    def first_gather(seg, k):
        return ring_gather(part_of(seg, k, 3), orders[k][2], (sum_send.at[seg], sum_recv.at[seg, 7]))

    def core_doubling(seg):
        at, count = SEGMENTS[seg]
        rows = rows_at(at + pipe * (count // 2), count // 2)
        return to_partner(tot.at[rows], tot.at[rows], sum_send.at[seg], sum_recv.at[seg, 9], "core")

    def ring_copy(src_rows, src, dst, sems, dim, j):
        position, device = rings[dim]
        return pltpu.make_async_remote_copy(
            src_ref=src.at[src_rows], dst_ref=dst, send_sem=sems[0], recv_sem=sems[1],
            device_id=device(lax.rem(position + j, RING)), device_id_type=MESH,
        )

    def share(base, length, order, steps):
        for dim in order[:steps]:
            length //= RING
            base = base + rings[dim][0] * length
        return base, length

    def share_of(seg, k, steps):
        at, count = SEGMENTS[seg]
        return share(at + pipe * (count // 2) + k * (count // 4), count // 4, ring_orders[k], steps)

    def ring_scatter(seg, s, k):
        base, length = share_of(seg, k, s)
        length //= RING
        dim = ring_orders[k][s]
        position = rings[dim][0]
        sems = (sum_send.at[seg], sum_recv.at[seg, 1 + s])
        return [
            ring_copy(
                rows_at(base + lax.rem(position + j, RING) * length, length), pay,
                sum_in.at[pl.ds(in_at[seg, s, k] + (j - 1) * length, length)],
                sems, dim, j,
            )
            for j in (2, 1, 3)
        ]

    def ring_gather(base_length, dim, sems):
        rows = rows_at(*base_length)
        return [ring_copy(rows, tot, tot.at[rows], sems, dim, j) for j in (2, 1, 3)]

    def ring_gather_of(seg, t, k):
        sems = (sum_send.at[seg], sum_recv.at[seg, 3 + t])
        return ring_gather(share_of(seg, k, t + 1), ring_orders[k][t], sems)

    def launch_all(seg, copies, rows):
        for copy in copies:
            copy.start()
        sent_rows[seg] += len(copies) * rows

    def ring_advance(seg, stage):
        at, count = SEGMENTS[seg]
        half, quarter = count // 2, count // 4
        if stage == 0:
            launch_all(seg, [core_halving(seg)], half)
        elif stage == 1:
            wait_rows(half, sum_recv.at[seg, 0])
            for k in range(2):
                rows = rows_at(at + pipe * half + k * quarter, quarter)
                came = pl.ds(in_at[seg, "core"] + k * quarter, quarter)
                pay[rows, :] = pay[rows, :] + sum_in[came, :]
                launch_all(seg, ring_scatter(seg, 0, k), quarter // 4)
        elif stage <= 3:
            s = stage - 2
            length = quarter >> 2 * (s + 1)
            wait_rows(6 * length, sum_recv.at[seg, 1 + s])
            for k in range(2):
                rows = rows_at(*share_of(seg, k, s + 1))
                total = wide(pay[rows, :])
                for j in range(3):
                    total = total + wide(sum_in[pl.ds(in_at[seg, s, k] + j * length, length), :])
                if s == 0:
                    pay[rows, :] = total.astype(bf16)
                    launch_all(seg, ring_scatter(seg, 1, k), length // 4)
                else:
                    tot[rows, :] = total.astype(bf16)
                    launch_all(seg, ring_gather_of(seg, 1, k), length)
        elif stage <= 5:
            t = 5 - stage
            length = quarter >> 2 * (t + 1)
            wait_rows(6 * length, sum_recv.at[seg, 3 + t])
            if t:
                for k in range(2):
                    launch_all(seg, ring_gather_of(seg, 0, k), quarter // 4)
            else:
                launch_all(seg, [core_doubling(seg)], half)
        else:
            wait_rows(half, sum_recv.at[seg, 9])

    def advance(seg, stage):
        if not CUBE[seg]:
            return ring_advance(seg, stage)
        at, count = SEGMENTS[seg]
        half, quarter = count // 2, count // 8
        if stage == 0:
            launch_all(seg, [core_halving(seg)], half)
        elif stage == 1:
            wait_rows(half, sum_recv.at[seg, 0])
            for k in range(4):
                rows = rows_at(at + pipe * half + k * quarter, quarter)
                came = pl.ds(in_at[seg, "core"] + k * quarter, quarter)
                pay[rows, :] = pay[rows, :] + sum_in[came, :]
                launch_all(seg, [halving(seg, 0, k)], quarter // 2)
        elif stage <= 3:
            s = stage - 2
            length = quarter >> (s + 1)
            wait_rows(4 * length, sum_recv.at[seg, 1 + s])
            for k in range(4):
                rows = rows_at(*part_of(seg, k, s + 1))
                pay[rows, :] = pay[rows, :] + sum_in[pl.ds(in_at[seg, s, k], length), :]
                if s == 0:
                    launch_all(seg, [halving(seg, 1, k)], length // 2)
                else:
                    launch_all(seg, last_scatter(seg, k), length // RING)
        elif stage == 4:
            length = quarter // 16
            wait_rows(12 * length, sum_recv.at[seg, 3])
            for k in range(4):
                rows = rows_at(*part_of(seg, k, 3))
                total = wide(pay[rows, :])
                for j in range(3):
                    total = total + wide(sum_in[pl.ds(in_at[seg, 2, k] + j * length, length), :])
                tot[rows, :] = total.astype(bf16)
                launch_all(seg, first_gather(seg, k), length)
        elif stage == 5:
            wait_rows(12 * (quarter // 16), sum_recv.at[seg, 7])
            for k in range(4):
                launch_all(seg, [doubling(seg, 1, k)], quarter // 4)
        elif stage == 6:
            wait_rows(quarter, sum_recv.at[seg, 6])
            for k in range(4):
                launch_all(seg, [doubling(seg, 0, k)], quarter // 2)
        elif stage == 7:
            wait_rows(2 * quarter, sum_recv.at[seg, 5])
            launch_all(seg, [core_doubling(seg)], half)
        else:
            wait_rows(half, sum_recv.at[seg, 9])

    def point(name):
        for seg, stage in POINTS[name]:
            advance(seg, stage)

    def remote(src, dst, send, recv, j):
        return pltpu.make_async_remote_copy(
            src_ref=src, dst_ref=dst, send_sem=send, recv_sem=recv,
            device_id={"tensor": lax.rem(y + j, RING)}, device_id_type=MESH,
        )

    def rows_of(j):
        return pl.ds(pl.multiple_of(lax.rem(y + j, RING) * OWN, OWN), OWN)

    def scatter(phase):
        for j in (2, 1, 3):
            remote(part.at[phase, rows_of(j)], rs_in.at[phase, j - 1], y_send.at[0], rs_recv.at[phase], j).start()

    def scattered(phase):
        total = wide(part[phase, own_rows, :])
        wait_for(rs_in.at[phase], rs_recv.at[phase])
        for j in range(3):
            total = total + wide(rs_in[phase, j])
        return total

    def gather(phase, full):
        for j in (2, 1, 3):
            remote(full.at[own_rows], full.at[own_rows], y_send.at[1], ag_recv.at[phase], j).start()

    def gathered(phase):
        wait_for(part.at[phase, pl.ds(0, 3 * OWN)], ag_recv.at[phase])

    def exchange(i, put, got):
        for j in (2, 1, 3):
            remote(put.at[lax.rem(y + j, RING)], got.at[j - 1], y_send.at[2 + i], end_recv.at[i], j).start()

    def weight_step(i, step):
        whole = (all_wo, all_out)[i]
        recv = weight_recv.at[4 * i + step]
        send = weight_send.at[i]

        def block(owner, row, count, col, width):
            rows = pl.ds(pl.multiple_of(owner * COLS + row, 16), count)
            return whole.at[rows, pl.ds(pl.multiple_of(col, 256), width)]

        others = [lax.rem(y + j, RING) for j in (2, 1, 3)]
        if step == 3:
            for owner in others:
                ref = block(owner, 0, COLS, 512 * pipe, 512)
                to_partner(ref, ref, send, recv, "core").start()
            return
        for h, (first_dim, then) in enumerate(ring_orders):
            col = 512 * pipe + 256 * h
            first_at, then_at = rings[first_dim][0], rings[then][0]
            if step == 0:
                ref = block(y, 16 * (4 * then_at + first_at), 16, col, 256)
                for j in (2, 1, 3):
                    remote(ref, ref, send, recv, j).start()
                continue
            position, device = rings[(first_dim, then)[step - 1]]
            for owner in others:
                if step == 1:
                    ref = block(owner, 16 * (4 * then_at + first_at), 16, col, 256)
                else:
                    ref = block(owner, 64 * then_at, 64, col, 256)
                for j in (2, 1, 3):
                    pltpu.make_async_remote_copy(
                        src_ref=ref, dst_ref=ref, send_sem=send, recv_sem=recv,
                        device_id=device(lax.rem(position + j, RING)), device_id_type=MESH,
                    ).start()

    def weight_wait(i, step):
        wait_rows((96, 288, 1152, 1536)[step], weight_recv.at[4 * i + step])

    def rows_exchange(put, into, i):
        for j in (2, 1, 3):
            remote(put.at[lax.rem(y + j, RING)], into.at[own_rows], y_send.at[2 + i], end_recv.at[i], j).start()
        into[own_rows, :] = put[y]

    for c in range(2):
        at = AT_LAST + c * HALF_LAST
        pay[at : at + HALF_LAST, :] = jnp.zeros((HALF_LAST, COLS), bf16)

    first, second = lengths[pipe, 0], lengths[pipe, 1]
    both = first + second

    def segment_of(r):
        return (r >= first).astype(jnp.int32) + (r >= both).astype(jnp.int32)

    same_item = segment_of(iota((ROWS, ROWS), 0)) == segment_of(iota((ROWS, ROWS), 1))
    row = iota((ROWS, 128), 0)
    place = row - jnp.where(row >= first, first, 0) - jnp.where(row >= both, second, 0)
    onehot[...] = jnp.where(place == iota((ROWS, 128), 1), 1.0, 0.0).astype(bf16)
    pos[LONGEST:, :] = jnp.zeros((128 - LONGEST, COLS), bf16)

    loads["pw"].wait()
    loads["ve"].wait()
    r, c = iota((4 * HALF, VARS * PATCH), 0), iota((4 * HALF, VARS * PATCH), 1)
    pick = jnp.where((c == PATCH * (r % HALF) + r // HALF) & (r % HALF < VARS), 1.0, 0.0).astype(bf16)
    for v in range(VARS):
        pwf[PATCH * v : PATCH * (v + 1), :] = wide(pw[v])
    terms[: 4 * HALF, :] = mm(pick, pwf[...].astype(bf16)).astype(bf16)
    terms[4 * HALF : 4 * HALF + VARS, :] = ve[...]
    terms[4 * HALF + VARS :, :] = jnp.zeros((TERMS - 4 * HALF - VARS, D), bf16)
    r, c = iota((VARS * PATCH, 4 * HALF), 1), iota((VARS * PATCH, 4 * HALF), 0)
    pick_back = jnp.where((c == PATCH * (r % HALF) + r // HALF) & (r % HALF < VARS), 1.0, 0.0).astype(bf16)
    loads["patches"].wait()
    x3[:, : 4 * HALF] = mm_tn(patches[...], pick_back)
    lane = iota((ROWS, 128), 1)
    x3[:, 4 * HALF :] = jnp.where(lane < VARS, 1.0, 0.0)

    loads["wq"].wait()
    loads["aq"].wait()
    aq_row = as_row(aq_in)
    query = mm(jnp.broadcast_to(aq_row, (8, D)).astype(bf16), wq[...])[0:1, :].astype(bf16)
    query_row[...] = jnp.broadcast_to(wide(query), (8, COLS))
    head_of = iota((8, COLS), 1) // HEAD_DIM
    block = jnp.where(
        head_of == iota((8, COLS), 0) % HEADS, jnp.broadcast_to(wide(query), (8, COLS)), 0.0
    ).astype(bf16)
    loads["wk"].wait()
    key_dir = mm_nt(block, wk[...]) * score_scale
    split = in_two(key_dir[:HEADS, :])
    kdir[...] = jnp.concatenate([wide(split), jnp.zeros((120, D), f32)], axis=0).astype(bf16)
    key_parts = mm_nt(split, terms[...])
    kterms[...] = key_parts + pltpu.roll(key_parts, HEADS, 0)
    loads["wv"].wait()
    vterms[...] = mm(terms[...], wv[...]).astype(bf16)
    pl.semaphore_wait(barrier, len(neighbours))
    loads["wout"].wait()
    weight_step(1, 0)

    def fold(v):
        folded = v[:, :128] + v[:, 128:256] + v[:, 256:]
        return folded + pltpu.roll(folded, HALF, 1)

    def thrice(v):
        return jnp.concatenate([v, v, v], axis=1)

    for h in range(HEADS):
        scores = fold(x3[...] * kterms[h : h + 1, :])
        scores = jnp.where(lane % HALF < VARS, scores, -1e30)
        raised = jnp.exp(scores - jnp.max(scores, axis=-1, keepdims=True))
        weights = raised / (0.5 * jnp.sum(raised, axis=-1, keepdims=True))
        soft[h] = weights
        shares[h * ROWS : (h + 1) * ROWS, :] = (x3[...] * thrice(weights)).astype(bf16)

    col_head = iota((ROWS, COLS), 1) // HEAD_DIM

    def pick_heads(stacked):
        total = jnp.zeros((ROWS, COLS), f32)
        for h in range(HEADS):
            total = jnp.where(col_head == h, stacked[h * ROWS : (h + 1) * ROWS, :], total)
        return total

    def spread_heads(value):
        for h in range(HEADS):
            masked[h * ROWS : (h + 1) * ROWS, :] = jnp.where(col_head == h, value, 0.0).astype(bf16)

    mixed[...] = pick_heads(mm(shares[...], vterms[...])).astype(bf16)
    loads["wo"].wait()
    loads["pos"].wait()
    loads["aggbias"].wait()
    aggbias_row = as_row(aggbias_in)
    for j in range(RING):
        cols = slice(j * COLS, (j + 1) * COLS)
        part[0, :, cols] = mm(mixed[...], all_wo[own_block, cols]).astype(bf16)
    extra = mm(mixed[...], all_wo[own_block, own_cols]) + mm(onehot[...], pos[...]) + aggbias_row
    part[0, :, own_cols] = extra.astype(bf16)
    scatter(0)
    for name in ("gain1", "shift1", "abias", "gain2", "shift2", "dbias", "ubias"):
        loads[name].wait()
    gain1_row, shift1_row = as_row(gain1_in), as_row(shift1_in)
    abias_row, gain2_row, shift2_row = as_row(abias_in), as_row(gain2_in), as_row(shift2_in)
    dbias_row, ubias_row = as_row(dbias_in), as_row(ubias_in)
    dbias_rows[...] = jnp.broadcast_to(dbias_row, (8, D))
    weight_wait(1, 0)
    weight_step(1, 1)
    stream[own_rows, :] = scattered(0).astype(bf16)
    gather(0, stream)
    loads["wqkv"].wait()
    weight_wait(1, 1)
    weight_step(1, 2)
    weight_step(0, 0)
    gathered(0)
    xhat, _ = norm_parts(wide(stream[...]))
    normed[...] = (xhat * gain1_row + shift1_row).astype(bf16)

    for j in range(3):
        qkv[j] = mm(normed[...], wqkv[j]).astype(bf16)
    spread_heads(qkv[0])
    raw = mm_nt(masked[...], qkv[1]) * score_scale
    for h in range(HEADS):
        rows = slice(h * ROWS, (h + 1) * ROWS)
        score = jnp.where(same_item, raw[rows, :], -1e30)
        raised = jnp.exp(score - jnp.max(score, axis=-1, keepdims=True))
        probs[rows, :] = raised / jnp.sum(raised, axis=-1, keepdims=True)
    attended = pick_heads(mm(probs[...].astype(bf16), qkv[2])).astype(bf16)
    att_all[y] = attended
    for j in (2, 1, 3):
        remote(att_all.at[y], att_all.at[y], y_send.at[1], ag_recv.at[1], j).start()
    weight_wait(0, 0)
    weight_step(0, 1)
    weight_wait(1, 2)
    weight_step(1, 3)
    loads["wup"].wait()
    loads["wdown"].wait()
    loads["dy"].wait()
    weight_wait(1, 3)
    gathered(1)
    weight_wait(0, 1)
    weight_step(0, 2)
    for j in range(RING):
        cols = slice(j * COLS, (j + 1) * COLS)
        total = wide(stream[:, cols]) + abias_row[:, cols]
        for i in range(RING):
            total = total + mm(att_all[i], all_out[i * COLS : (i + 1) * COLS, cols])
        resid[:, cols] = total
    xhat, _ = norm_parts(resid[...])
    normed2[...] = (xhat * gain2_row + shift2_row).astype(bf16)

    for j in range(RING):
        cols = slice(j * COLS, (j + 1) * COLS)
        pre = mm(normed2[...], wup[:, cols]) + ubias_row[:, cols]
        half_cdf = 0.5 * (1.0 + lax.erf(pre * root_half))
        active[:, cols] = (pre * half_cdf).astype(bf16)
        slope = half_cdf + pre * jnp.exp(-0.5 * pre * pre) * inv_root_tau
        grad = (mm_nt(dy[...], wdown[cols, :]) * slope).astype(bf16)
        g_pre[:, cols] = grad
        small[8 + j : 9 + j, :] = col_sum(wide(grad))
    for j in range(RING):
        rows = slice(j * COLS, (j + 1) * COLS)
        part[3, :, rows] = mm_nt(g_pre[...], wup[rows, :]).astype(bf16)
    scatter(3)
    for j in range(RING):
        cols = slice(j * COLS, (j + 1) * COLS)
        part[2, :, cols] = mm(active[...], wdown[:, cols]).astype(bf16)
    for j in (2, 1, 3):
        cols = pl.ds(pl.multiple_of(lax.rem(y + j, RING) * COLS, COLS), COLS)
        remote(part.at[2, :, cols], block_in.at[j - 1], y_send.at[2], end_recv.at[0], j).start()
    for j in range(RING):
        cols = slice(j * COLS, (j + 1) * COLS)
        pay[AT_DOWN + j * D : AT_DOWN + (j + 1) * D, :] = mm_tn(active[...], dy[:, cols]).astype(bf16)
    advance(0, 0)
    for j in range(RING):
        cols = slice(j * COLS, (j + 1) * COLS)
        pay[AT_UP + j * D : AT_UP + (j + 1) * D, :] = mm_tn(normed2[...], g_pre[:, cols]).astype(bf16)
    advance(1, 0)
    weight_wait(0, 2)
    weight_step(0, 3)
    point("up")
    e2 = scattered(3)
    xhat2, inv2 = norm_parts(resid[own_rows, :])
    g_resid_own = (wide(dy[own_rows, :]) + norm_back(e2, xhat2, inv2, gain2_row)).astype(bf16)
    g_resid[own_rows, :] = g_resid_own
    for j in range(RING):
        put_rows[0, j] = mm_nt(g_resid_own, all_out[j * COLS : (j + 1) * COLS, :]).astype(bf16)
    rows_exchange(put_rows.at[0], g_att, 5)
    gather(2, g_resid)
    point("e2")
    gain2, shift2 = col_sum(e2 * xhat2), col_sum(e2)
    wait_for(block_in, end_recv.at[0])
    result = resid[:, own_cols] + wide(part[2, :, own_cols]) + dbias_rows[0:1, own_cols]
    got_block[...] = (result + wide(block_in[0]) + wide(block_in[1]) + wide(block_in[2])).astype(bf16)
    point("block")
    wait_rows(3 * OWN, end_recv.at[5])

    spread_heads(g_att[...])
    g_probs = mm_nt(masked[...], qkv[2])
    g_v = mm_tn(probs[...].astype(bf16), masked[...]).astype(bf16)
    p = probs[...]
    g_scores = (p * (g_probs - jnp.sum(p * g_probs, axis=-1, keepdims=True))).astype(bf16)
    g_q = (pick_heads(mm(g_scores, qkv[1])) * score_scale).astype(bf16)
    spread_heads(qkv[0])
    g_k = (mm_tn(g_scores, masked[...]) * score_scale).astype(bf16)
    for j in range(RING):
        rows = slice(j * COLS, (j + 1) * COLS)
        total = mm_nt(g_q, wqkv[0, rows, :]) + mm_nt(g_k, wqkv[1, rows, :])
        part[4, :, rows] = (total + mm_nt(g_v, wqkv[2, rows, :])).astype(bf16)
    scatter(4)
    point("attn")
    for j, g in enumerate((g_q, g_k, g_v)):
        pay[AT_QKV + j * D : AT_QKV + (j + 1) * D, :] = mm_tn(normed[...], g).astype(bf16)
    gathered(2)
    attended_own = att_all[y]
    for j in range(RING):
        cols = slice(j * COLS, (j + 1) * COLS)
        pay[AT_OUT + j * COLS : AT_OUT + (j + 1) * COLS, :] = mm_tn(
            attended_own, g_resid[:, cols]
        ).astype(bf16)
    advance(2, 0)
    point("out")
    e1 = scattered(4)
    xhat1, inv1 = norm_parts(wide(stream[own_rows, :]))
    g_stream_own = (
        wide(g_resid[own_rows, :]) + norm_back(e1, xhat1, inv1, gain1_row)
    ).astype(bf16)
    g_stream[own_rows, :] = g_stream_own
    weight_wait(0, 3)
    for j in range(RING):
        put_rows[1, j] = mm_nt(g_stream_own, all_wo[j * COLS : (j + 1) * COLS, :]).astype(bf16)
    rows_exchange(put_rows.at[1], g_mixed, 6)
    gather(3, g_stream)
    gain1, shift1 = col_sum(e1 * xhat1), col_sum(e1)
    for j in range(RING):
        cols = slice(j * COLS, (j + 1) * COLS)
        for i, v in enumerate((gain1, shift1, gain2, shift2)):
            put_gain[j, i : i + 1, :] = v[:, cols]
        put_gain[j, 4:8, :] = jnp.zeros((4, COLS), f32)
    exchange(1, put_gain, got_gain)
    point("e1")
    wait_rows(3 * OWN, end_recv.at[6])

    spread_heads(g_mixed[...])
    by_term = mm_nt(masked[...], vterms[...])
    grad_patch = jnp.zeros((ROWS, 4 * HALF), f32)
    for h in range(HEADS):
        mine = by_term[h * ROWS : (h + 1) * ROWS, :]
        weights = soft[h]
        g_weights = fold(x3[...] * mine)
        g_sc = weights * (
            g_weights - 0.5 * jnp.sum(weights * g_weights, axis=-1, keepdims=True)
        )
        g_sc2 = jnp.concatenate([g_sc, g_sc], axis=1)
        w2 = jnp.concatenate([weights, weights], axis=1)
        grad_patch = grad_patch + g_sc2 * kterms[h : h + 1, : 4 * HALF] + w2 * mine[:, : 4 * HALF]
        sums = col_sum(x3[...] * thrice(g_sc))
        score_sum[h : h + 1, :] = sums
    value_sum = mm_tn(shares[...], masked[...]).astype(bf16)
    pay[AT_LAST : AT_LAST + 256, :] = value_sum[:256, :]
    pay[AT_LAST + HALF_LAST : AT_LAST + HALF_LAST + 128, :] = value_sum[256:, :]
    head_cols = iota((HEADS, COLS), 1)
    spot = jnp.where((head_cols % HEADS == iota((HEADS, COLS), 0)) & (head_cols < 8), 1.0, 0.0).astype(bf16)
    across = mm_tn(score_sum[...].astype(bf16), spot).astype(bf16)
    for n in range(TERMS // 16):
        at = score_place(n)
        pay[at : at + 16, :] = across[16 * n : 16 * (n + 1), :]
    gathered(3)
    g_own = g_stream[:, own_cols]
    pay[AT_POS : AT_POS + LONGEST, :] = mm_tn(onehot[...], g_own)[:LONGEST, :].astype(bf16)
    advance(4, 0)
    point("last")
    for j in range(RING):
        cols = slice(j * COLS, (j + 1) * COLS)
        pay[AT_WO + j * COLS : AT_WO + (j + 1) * COLS, :] = mm_tn(
            mixed[...], g_stream[:, cols]
        ).astype(bf16)
    advance(3, 0)
    point("wo")
    along = mm(in_two(score_sum[...]), terms[...])
    along = in_two(along[:HEADS] + along[HEADS:])
    head_of = iota((8, COLS), 1) // HEAD_DIM
    g_query = col_sum(jnp.where(head_of == iota((8, COLS), 0) % HEADS, mm(along, wk[...]), 0.0)) * score_scale
    both_parts = mm_nt(in_two(jnp.broadcast_to(g_query, (HEADS, COLS))), wq[...])
    g_aq = both_parts[0:1, :] + both_parts[HEADS : HEADS + 1, :]
    for j in range(RING):
        put_aq[j] = jnp.broadcast_to(g_aq[:, j * COLS : (j + 1) * COLS], (8, COLS))
    exchange(3, put_aq, got_aq)
    low_patch = grad_patch.astype(bf16)
    width = VARS * PATCH // RING
    r, c = iota((width, 4 * HALF), 1), iota((width, 4 * HALF), 0)
    for j in range(RING):
        pick_own = jnp.where(
            (c + width * j == PATCH * (r % HALF) + r // HALF) & (r % HALF < VARS), 1.0, 0.0
        ).astype(bf16)
        put_patch[j] = mm_nt(pick_own, low_patch).astype(bf16)
    exchange(2, put_patch, got_patch)
    small[0:1, :] = col_sum(wide(g_own))
    small[5:6, :] = col_sum(wide(g_resid[:, own_cols]))
    small[6:7, :] = col_sum(wide(dy[:, own_cols]))
    small[12:32, :] = jnp.zeros((20, COLS), f32)
    wait_for(got_gain, end_recv.at[1])
    small[1:5, :] = (put_gain[y] + got_gain[0] + got_gain[1] + got_gain[2])[0:4, :]

    def vector_step(i):
        if i == 0:
            wait_for(got_aq, end_recv.at[3])
            small[7:8, :] = (put_aq[y] + got_aq[0] + got_aq[1] + got_aq[2])[0:1, :]
            rd_out[0] = small[...]
            to_partner(rd_out.at[0], rd_in.at[0], other_send.at[0], rd_recv.at[0], "core").start()
            return
        at, n = (0, 1) if i == 1 else (3 * i - 5, 3)
        wait_for(rd_in.at[pl.ds(at, n)], rd_recv.at[i - 1])
        value = rd_out[i - 1]
        for j in range(n):
            value = value + rd_in[at + j]
        if i == 3:
            total_small[...] = value
            return
        rd_out[i] = value
        position, device = rings["xz"[i - 1]]
        for j in (2, 1, 3):
            pltpu.make_async_remote_copy(
                src_ref=rd_out.at[i], dst_ref=rd_in.at[3 * i - 3 + j], send_sem=other_send.at[0],
                recv_sem=rd_recv.at[i], device_id=device(lax.rem(position + j, RING)), device_id_type=MESH,
            ).start()

    terms_base = AT_TERMS + pipe * 256

    def terms_gather(t):
        dim = ring_orders[0][t]
        for copy in ring_gather(
            share(terms_base, 256, ring_orders[0], t + 1), dim, (other_send.at[1], extra_recv.at[t])
        ):
            copy.start()

    def terms_step(i):
        if i == 0:
            value_rows = tot[rows_at(*share_of(4, 0, 2)), :]
            score_rows = tot[rows_at(*share_of(4, 1, 2)), :]
            total = mm_nt(value_rows, wv[...]) + mm(score_rows[:, :128], kdir[...])
            for j in range(RING):
                put_terms[j] = total[:, j * COLS : (j + 1) * COLS].astype(bf16)
            exchange(4, put_terms, got_terms)
        elif i == 1:
            wait_for(got_terms, end_recv.at[4])
            total = wide(put_terms[y]) + wide(got_terms[0]) + wide(got_terms[1]) + wide(got_terms[2])
            tot[rows_at(*share(terms_base, 256, ring_orders[0], 2)), :] = total.astype(bf16)
            terms_gather(1)
        elif i == 2:
            wait_rows(48, extra_recv.at[1])
            terms_gather(0)
        elif i == 3:
            wait_rows(192, extra_recv.at[0])
            rows = rows_at(terms_base, 256)
            to_partner(tot.at[rows], tot.at[rows], other_send.at[1], extra_recv.at[2], "core").start()
        else:
            wait_rows(256, extra_recv.at[2])

    next_of = {"t": 0, "v": 0}
    for step in TAIL:
        if step == "t":
            terms_step(next_of["t"])
            next_of["t"] += 1
        elif step == "v":
            vector_step(next_of["v"])
            next_of["v"] += 1
        else:
            advance(*step)
    assert next_of == {"t": 5, "v": 4}
    wait_for(got_patch, end_recv.at[2])
    patch_sum[...] = (
        wide(put_patch[y]) + wide(got_patch[0]) + wide(got_patch[1]) + wide(got_patch[2])
    )
    for seg in range(len(SEGMENTS)):
        wait_rows(sent_rows[seg], sum_send.at[seg])
    wait_for(rs_in.at[pl.ds(0, 3)], y_send.at[0])
    wait_for(terms, y_send.at[1])
    wait_for(block_in, y_send.at[2])
    for i in (5, 6):
        wait_rows(3 * OWN, y_send.at[2 + i])
    for i in range(2):
        wait_rows(96 + 288 + 1152 + 1536, weight_send.at[i])
    for i, got in ((1, got_gain), (2, got_patch), (3, got_aq), (4, got_terms)):
        wait_for(got, y_send.at[2 + i])
    wait_for(rd_in, other_send.at[0])
    wait_rows(3 * 16 + 3 * 64 + 256, other_send.at[1])


MAIN_VMEM = 50 * 1024 * 1024
FINISH_VMEM = 50 * 1024 * 1024


def run_chain(lengths, *args):
    hbm = pl.BlockSpec(memory_space=pl.ANY)
    V = pltpu.VMEM
    low = lambda *s: V(s, bf16)
    full = lambda *s: V(s, f32)
    kept = [w for name, w in zip(WEIGHTS, args) if name not in ("wo", "wout")]
    scratch = [low(*w.shape) if w.shape[0] != LONGEST else low(128, COLS) for w in kept]
    scratch += [low(D, D), low(D, D)]
    scratch += [
        full(VARS * PATCH, D), low(HEADS * ROWS, TERMS), low(TERMS, COLS), full(8, TERMS),
        low(128, D), full(HEADS, ROWS, 128), full(ROWS, TERMS), low(ROWS, 128),
        low(5, ROWS, D), low(5, 3, OWN, D), low(ROWS, D), low(ROWS, D), full(ROWS, D),
        low(ROWS, D), low(ROWS, D), low(ROWS, D), full(8, D), low(3, ROWS, COLS),
        low(2, RING, OWN, COLS), low(ROWS, COLS), low(ROWS, COLS),
        low(ROWS, COLS), low(3, ROWS, COLS), full(HEADS * ROWS, ROWS), low(RING, ROWS, COLS),
        low(ROWS, D), low(ROWS, D), low(HEADS * ROWS, COLS),
        low(3, 48, ROWS), low(RING, 48, ROWS),
        full(3, 8, COLS), full(RING, 8, COLS), full(SMALL, COLS), full(HEADS, TERMS),
        full(3, 8, COLS), full(RING, 8, COLS), low(3, 16, COLS), low(RING, 16, COLS),
        full(3, SMALL, COLS), full(7, SMALL, COLS),
        low(PAY, COLS), low(PAY * 31 // 32, COLS),
    ]
    dma = pltpu.SemaphoreType.DMA
    scratch += [
        dma((len(args),)), dma((9,)), dma((5,)), dma((4,)), dma((7,)), dma((5,)), dma((5, 10)), dma((3,)),
        dma((3,)), dma((2,)), dma((8,)), dma((2,)),
    ]
    return pl.pallas_call(
        chain,
        out_shape=(
            low(ROWS, COLS), full(48, ROWS), low(ALL, COLS), low(TERMS, D), full(SMALL, COLS), full(8, COLS),
        ),
        in_specs=[pl.BlockSpec(memory_space=pltpu.SMEM)] + [hbm] * len(args),
        out_specs=[pl.BlockSpec(memory_space=pltpu.VMEM)] * 6,
        scratch_shapes=scratch,
        compiler_params=pltpu.CompilerParams(
            collective_id=0, has_side_effects=True, vmem_limit_bytes=MAIN_VMEM
        ),
    )(lengths, *[pltpu.with_memory_space_constraint(a, pltpu.HBM) for a in args])


VECTORS = (0, 7, 1, 2, 5, 3, 4, 6)


def finish(
    tot, block_in, patch_in, terms, small, query, aq_from, hk,
    o_block, o_patch, o_down, o_up, o_out, o_qkv, o_wo, o_wv, o_wk, o_wq,
    o_pw, o_ve, o_pos, *rest,
):
    o_vectors, o_upbias = rest[:8], rest[8]
    wk, aq_in, down, up, out, qkv, wo, gv, gk, gq, load_sem, save_sem = rest[9:]
    loads = [
        pltpu.make_async_copy(hk, wk, load_sem.at[0]), pltpu.make_async_copy(aq_from, aq_in, load_sem.at[1])
    ]
    for copy in loads:
        copy.start()
    saves = []

    def store(i, src, dst):
        copy = pltpu.make_async_copy(src, dst, save_sem.at[i])
        copy.start()
        saves.append(copy)

    for j in range(RING):
        down[:, j * COLS : (j + 1) * COLS] = wide(tot[AT_DOWN + j * D : AT_DOWN + (j + 1) * D, :])
    store(4, down, o_down)
    for j in range(RING):
        up[:, j * COLS : (j + 1) * COLS] = wide(tot[AT_UP + j * D : AT_UP + (j + 1) * D, :])
    store(5, up, o_up)
    for j in range(3):
        qkv[j] = wide(tot[AT_QKV + j * D : AT_QKV + (j + 1) * D, :])
    store(6, qkv, o_qkv)
    for j in range(RING):
        out[:, j * COLS : (j + 1) * COLS] = wide(tot[AT_OUT + j * COLS : AT_OUT + (j + 1) * COLS, :])
    store(7, out, o_out)
    for j in range(RING):
        wo[:, j * COLS : (j + 1) * COLS] = wide(tot[AT_WO + j * COLS : AT_WO + (j + 1) * COLS, :])
    store(1, wo, o_wo)
    store(8, block_in, o_block)
    store(9, patch_in, o_patch)
    for copy in loads:
        copy.wait()
    value_sum = jnp.concatenate(
        [tot[AT_LAST : AT_LAST + 256, :], tot[AT_LAST + HALF_LAST : AT_LAST + HALF_LAST + 128, :]], axis=0
    )
    gv[...] = mm_tn(terms[...], value_sum)
    store(0, gv, o_wv)
    across = jnp.concatenate(
        [tot[score_place(n) : score_place(n) + 16, :128] for n in range(TERMS // 16)], axis=0
    )
    along = in_two(mm_tn(across, terms[...])[:HEADS, :])
    head_of = iota((8, COLS), 1) // HEAD_DIM
    mine = head_of == iota((8, COLS), 0) % HEADS
    block = jnp.where(mine, query[...], 0.0).astype(bf16)
    gk[...] = mm_tn(along, block) * score_scale
    store(2, gk, o_wk)
    g_query = col_sum(jnp.where(mine, mm(along, wk[...]), 0.0)) * score_scale
    row = iota((8, D), 0)
    aq = jnp.where(row < 2, jnp.broadcast_to(as_row(aq_in), (8, D)), 0.0).astype(bf16)
    high = wide(g_query.astype(bf16))
    both = jnp.where(
        iota((8, COLS), 0) == 0,
        jnp.broadcast_to(high, (8, COLS)), jnp.broadcast_to(g_query - high, (8, COLS)),
    ).astype(bf16)
    gq[...] = mm_tn(aq, both)
    store(3, gq, o_wq)
    o_pos[...] = wide(tot[AT_POS : AT_POS + LONGEST, :])
    for p in range(PATCH):
        o_pw[:, p, :] = wide(tot[AT_TERMS + HALF * p : AT_TERMS + HALF * p + VARS, :])
    o_ve[...] = wide(tot[AT_TERMS + 4 * HALF : AT_TERMS + 4 * HALF + VARS, :])
    for ref, i in zip(o_vectors, VECTORS):
        ref[0:1, :] = small[i : i + 1, :128]
        ref[1:2, :] = small[i : i + 1, 128:]
    for j in range(RING):
        o_upbias[2 * j : 2 * j + 1, :] = small[8 + j : 9 + j, :128]
        o_upbias[2 * j + 1 : 2 * j + 2, :] = small[8 + j : 9 + j, 128:]
    for copy in saves:
        copy.wait()


def run_finish(*args):
    vmem = pl.BlockSpec(memory_space=pltpu.VMEM)
    hbm = pl.BlockSpec(memory_space=pl.ANY)
    full = lambda *s: pltpu.VMEM(s, f32)
    shape = lambda *s: jax.ShapeDtypeStruct(s, f32)
    big = [(D, D), (D, D), (COLS, D), (3, D, COLS), (COLS, D), (D, COLS), (D, COLS), (D, COLS)]
    return pl.pallas_call(
        finish,
        out_shape=[jax.ShapeDtypeStruct((ROWS, COLS), bf16), shape(48, ROWS)]
        + [shape(*s) for s in big]
        + [shape(VARS, PATCH, COLS), shape(VARS, COLS), shape(LONGEST, COLS)]
        + [shape(2, 128)] * 8 + [shape(8, 128)],
        in_specs=[vmem] * 6 + [hbm] * 2,
        out_specs=[hbm] * 10 + [vmem] * 12,
        scratch_shapes=[
            pltpu.VMEM((D, COLS), bf16), pltpu.VMEM((8, 128), bf16),
            full(D, D), full(D, D), full(COLS, D), full(3, D, COLS), full(COLS, D),
            full(D, COLS), full(D, COLS), full(D, COLS),
            pltpu.SemaphoreType.DMA((2,)), pltpu.SemaphoreType.DMA((10,)),
        ],
        compiler_params=pltpu.CompilerParams(vmem_limit_bytes=FINISH_VMEM),
    )(*[pltpu.with_memory_space_constraint(a, pltpu.VMEM if i < 6 else pltpu.HBM) for i, a in enumerate(args)])


def shards(
    patches, item_lengths, cotangent, patch_weight, var_embed, agg_query, agg_wq, agg_wk, agg_wv,
    agg_wo, agg_bias, pos_table, first_gain, first_shift, attn_qkv, attn_out, attn_bias,
    second_gain, second_shift, mlp_up, up_bias, mlp_down, down_bias,
):
    tiled = lambda v: v.reshape(v.shape[0] // 128, 128)
    block, patch, summed, terms, small, query = run_chain(
        item_lengths, patches.T, patch_weight, var_embed, tiled(agg_query), tiled(first_gain),
        tiled(first_shift), tiled(attn_bias), tiled(second_gain), tiled(second_shift),
        tiled(down_bias), tiled(up_bias), tiled(agg_bias),
        agg_wq, agg_wk, agg_wv, agg_wo, pos_table, attn_qkv.transpose(1, 0, 2), attn_out,
        mlp_up, mlp_down, cotangent,
    )
    (
        block, patch, g_down, g_up, g_out, g_qkv, g_wo, g_wv, g_wk, g_wq, g_pw, g_ve, g_pos,
        g_agg_bias, g_aq, g_gain1, g_shift1, g_attn_bias, g_gain2, g_shift2, g_down_bias, g_up_bias,
    ) = run_finish(summed, block, patch, terms, small, query, tiled(agg_query), agg_wk)
    flat = lambda v: v.reshape(-1)
    return (
        block, patch.T, g_pw, g_ve, flat(g_aq), g_wq, g_wk, g_wv, g_wo, flat(g_agg_bias), g_pos,
        flat(g_gain1), flat(g_shift1), g_qkv.transpose(1, 0, 2), g_out, flat(g_attn_bias),
        flat(g_gain2), flat(g_shift2), g_up, flat(g_up_bias), g_down, flat(g_down_bias),
    )


def solution(mesh):
    rows = P(("dp", "pipe"), None)
    cols = P(None, "tensor")
    split = P("tensor", None)
    part = P("tensor")
    both = P(("dp", "pipe"), "tensor")
    last = P(None, None, "tensor")
    return jax.shard_map(
        shards,
        mesh=mesh,
        in_specs=(
            rows, P("dp", None), rows, P(), P(), P(), cols, cols, cols, split, part, cols, P(), P(),
            last, split, P(), P(), P(), cols, part, split, P(),
        ),
        out_specs=(
            both, both, last, cols, part, cols, cols, cols, split, part, cols, part, part, last,
            split, part, part, part, cols, part, split, part,
        ),
        check_vma=False,
    )
```

```python
import jax
import jax.numpy as jnp
from jax import lax
from jax.experimental import pallas as pl
from jax.experimental.pallas import tpu as pltpu
from jax.sharding import PartitionSpec as P

D = 1024
HEAD_DIM = 64
VARS = 48
PATCH = 4
LONGEST = 96
RING = 4
ROWS = 128
OWN = ROWS // RING
COLS = D // RING
HEADS = COLS // HEAD_DIM
HALF = 64
TERMS = 6 * HALF

AT_DOWN = 0
AT_UP = 4096
AT_OUT = 8192
AT_QKV = 9216
AT_WO = 12288
AT_LAST = 13312
PAY = 14336
AT_TERMS = PAY
ALL = PAY + 512
SEGMENTS = ((AT_DOWN, 4096), (AT_UP, 4096), (AT_OUT, 4096), (AT_WO, 1024), (AT_LAST, 1024))
CUBE = (True, True, True, False, False)
LAST = 4
HALF_LAST = 512
AT_POS = AT_LAST + HALF_LAST + 128
SMALL = 16

norm_eps = 1e-05
root_half = 0.7071067811865476
inv_root_tau = 0.3989422804014327
score_scale = HEAD_DIM ** (-0.5)
highest = lax.Precision.HIGHEST
f32 = jnp.float32
bf16 = jnp.bfloat16
MESH = pl.DeviceIdType.MESH


def wide(v):
    return v.astype(f32)


def dot(left, right, dims, precision=None):
    return lax.dot_general(left, right, (dims, ((), ())), precision=precision, preferred_element_type=f32)


def mm(a, b, **kw):
    return dot(a, b, ((1,), (0,)), **kw)


def mm_nt(a, b, **kw):
    return dot(a, b, ((1,), (1,)), **kw)


def mm_tn(a, b, **kw):
    return dot(a, b, ((0,), (0,)), **kw)


def iota(shape, axis):
    return lax.broadcasted_iota(jnp.int32, shape, axis)


def norm_parts(x):
    centred = x - jnp.mean(x, axis=-1, keepdims=True)
    inverse = lax.rsqrt(jnp.mean(centred * centred, axis=-1, keepdims=True) + norm_eps)
    return centred * inverse, inverse


def norm_back(grad, xhat, inverse, gain):
    scaled = grad * gain
    return inverse * (
        scaled
        - jnp.mean(scaled, axis=-1, keepdims=True)
        - xhat * jnp.mean(scaled * xhat, axis=-1, keepdims=True)
    )


def col_sum(a):
    return jnp.sum(a, axis=0, keepdims=True)


WEIGHTS = (
    "patches", "pw", "ve", "aq", "gain1", "shift1", "abias", "gain2", "shift2", "dbias", "ubias", "aggbias",
    "wq", "wk", "wv", "wo", "pos", "wqkv", "wout", "wup", "wdown", "dy",
)
EARLY = ("aq", "wq", "pw", "ve", "wk", "wv", "wout", "patches", "wo", "pos", "aggbias")


def as_row(ref):
    value = wide(ref[...])
    return jnp.concatenate([value[i : i + 1, :] for i in range(value.shape[0])], axis=1)


def in_two(value):
    high = wide(value.astype(bf16))
    return jnp.concatenate([high, value - high], axis=0).astype(bf16)


def score_place(n):
    c, j = n // 16, n % 16
    return AT_LAST + c * HALF_LAST + 256 + 16 * (4 * (j % 4) + j // 4)


POINTS = {
    "up": ((0, 1), (1, 1)),
    "e2": (),
    "block": ((0, 2),),
    "attn": ((1, 2),),
    "out": ((0, 3), (2, 1), (1, 3)),
    "e1": ((0, 4),),
    "last": ((2, 2), (1, 4)),
    "wo": ((0, 5),),
}
TAIL = (
    (4, 1), (3, 1), (2, 3), (1, 5), "v", (0, 6), "v", (4, 2), (3, 2), (2, 4), (1, 6), (0, 7), "v", (4, 3), "t",
    (0, 8), (3, 3), (2, 5), (1, 7), "v", "t", (4, 4), (3, 4), (2, 6), (1, 8), "t", (4, 5), (3, 5), (4, 6),
    (3, 6), (2, 7), "t", (2, 8), "t",
)


def chain(
    lengths, hpatches, hpw, hve, haq, hgain1, hshift1, habias, hgain2, hshift2, hdbias,
    hubias, haggbias,
    hq, hk, hv, ho, hpos, hqkv, hout, hup, hdown, hdy,
    got_block, patch_sum, tot, terms, total_small, query_row,
    patches, pw, ve, aq_in, gain1_in, shift1_in, abias_in, gain2_in, shift2_in, dbias_in,
    ubias_in, aggbias_in,
    wq, wk, wv, pos, wqkv, wup, wdown, dy, all_wo, all_out,
    pwf, shares, vterms, kterms, kdir, soft, x3, onehot,
    part, rs_in, stream, normed, resid, normed2, g_resid, g_stream, dbias_rows, block_in,
    put_rows, g_att, g_mixed,
    mixed, qkv, probs, att_all, active, g_pre, masked,
    got_patch, put_patch, got_gain, put_gain, small, score_sum,
    got_aq, put_aq, got_terms, put_terms, rd_out, rd_in,
    pay, sum_in,
    load_sem, y_send, rs_recv, ag_recv, end_recv, sum_send, sum_recv, extra_recv, rd_recv, other_send, weight_recv, weight_send,
):
    y = lax.axis_index("tensor")
    pipe = lax.axis_index("pipe")
    dp = lax.axis_index("dp")
    x, z = lax.rem(dp, 4), dp // 4
    own_rows = pl.ds(pl.multiple_of(y * OWN, OWN), OWN)
    own_cols = pl.ds(pl.multiple_of(y * COLS, COLS), COLS)
    own_block = own_cols
    barrier = pltpu.get_barrier_semaphore()
    rings = {"x": (x, lambda q: {"dp": 4 * z + q}), "z": (z, lambda q: {"dp": 4 * q + x})}
    neighbours = [{"pipe": 1 - pipe}]
    for j in (1, 2, 3):
        neighbours.append({"tensor": lax.rem(y + j, RING)})
        neighbours += [at(lax.rem(p + j, RING)) for p, at in rings.values()]
    for device in neighbours:
        pl.semaphore_signal(barrier, inc=1, device_id=device, device_id_type=MESH)
    dims = {
        "core": (pipe, {"pipe": 1 - pipe}),
        "xa": (lax.rem((x + 1) // 2, 2), {"dp": dp + 1 - 2 * lax.rem(x, 2)}),
        "xb": (x // 2, {"dp": 4 * z + 3 - x}),
        "za": (lax.rem((z + 1) // 2, 2), {"dp": dp + 4 - 8 * lax.rem(z, 2)}),
        "zb": (z // 2, {"dp": 4 * (3 - z) + x}),
    }
    orders = (("xa", "xb", "z"), ("za", "zb", "x"), ("xb", "xa", "z"), ("zb", "za", "x"))
    ring_orders = (("x", "z"), ("z", "x"))
    loads = {
        name: pltpu.make_async_copy(src, dst, load_sem.at[i])
        for i, (name, src, dst) in enumerate(zip(
            WEIGHTS,
            (hpatches, hpw, hve, haq, hgain1, hshift1, habias, hgain2, hshift2, hdbias, hubias, haggbias,
             hq, hk, hv, ho, hpos, hqkv, hout, hup, hdown, hdy),
            (patches, pw, ve, aq_in, gain1_in, shift1_in, abias_in, gain2_in, shift2_in, dbias_in,
             ubias_in, aggbias_in,
             wq, wk, wv, all_wo.at[own_block], pos.at[pl.ds(0, LONGEST)], wqkv, all_out.at[own_block],
             wup, wdown, dy),
        ))
    }
    for name in EARLY + tuple(name for name in WEIGHTS if name not in EARLY):
        loads[name].start()

    def wait_for(like, sem):
        pltpu.make_async_copy(like, like, sem).wait()

    def wait_rows(count, sem):
        wait_for(tot.at[pl.ds(0, count)], sem)

    sent_rows = [0] * len(SEGMENTS)

    def to_partner(src, dst, send, recv, dim):
        return pltpu.make_async_remote_copy(
            src_ref=src, dst_ref=dst, send_sem=send, recv_sem=recv,
            device_id=dims[dim][1], device_id_type=MESH,
        )

    def rows_at(start, length):
        return pl.ds(pl.multiple_of(start, 16), length)

    def region(base, length, order, steps):
        for dim in order[:steps]:
            pair = dim in dims
            length //= 2 if pair else RING
            base = base + (dims[dim] if pair else rings[dim])[0] * length
        return base, length

    def part_of(seg, k, steps):
        at, count = SEGMENTS[seg]
        return region(at + pipe * (count // 2) + k * (count // 8), count // 8, orders[k], steps)

    in_at = {}
    place_in = 0
    for seg, (_, count) in enumerate(SEGMENTS):
        in_at[seg, "core"] = place_in
        place_in += count // 2
        for s in range(3):
            for k in range(4):
                if CUBE[seg]:
                    in_at[seg, s, k] = place_in
                    place_in += count // 16 >> s if s < 2 else 3 * (count // 128)
        for s in range(2):
            for k in range(2):
                if not CUBE[seg]:
                    in_at[seg, s, k] = place_in
                    place_in += 3 * (count // 16 >> 2 * s)
    assert place_in <= sum_in.shape[0]

    def core_halving(seg):
        at, count = SEGMENTS[seg]
        half = count // 2
        return to_partner(
            pay.at[rows_at(at + (1 - pipe) * half, half)], sum_in.at[pl.ds(in_at[seg, "core"], half)],
            sum_send.at[seg], sum_recv.at[seg, 0], "core",
        )

    def halving(seg, s, k):
        base, length = part_of(seg, k, s)
        dim = orders[k][s]
        length //= 2
        return to_partner(
            pay.at[rows_at(base + (1 - dims[dim][0]) * length, length)],
            sum_in.at[pl.ds(in_at[seg, s, k], length)], sum_send.at[seg], sum_recv.at[seg, 1 + s], dim,
        )

    def doubling(seg, t, k):
        rows = rows_at(*part_of(seg, k, t + 1))
        return to_partner(
            tot.at[rows], tot.at[rows], sum_send.at[seg], sum_recv.at[seg, 5 + t], orders[k][t]
        )

    def last_scatter(seg, k):
        base, length = part_of(seg, k, 2)
        length //= RING
        dim = orders[k][2]
        sems = (sum_send.at[seg], sum_recv.at[seg, 3])
        return [
            ring_copy(
                rows_at(base + lax.rem(rings[dim][0] + j, RING) * length, length), pay,
                sum_in.at[pl.ds(in_at[seg, 2, k] + (j - 1) * length, length)], sems, dim, j,
            )
            for j in (2, 1, 3)
        ]

    def first_gather(seg, k):
        return ring_gather(part_of(seg, k, 3), orders[k][2], (sum_send.at[seg], sum_recv.at[seg, 7]))

    def part_to_core(seg, k, other):
        base, length = part_of(seg, k, 0)
        bit = dims[orders[k][0]][0]
        rows = rows_at(base + (1 - bit if other else bit) * (length // 2), length // 2)
        return to_partner(tot.at[rows], tot.at[rows], sum_send.at[seg], sum_recv.at[seg, 9], "core")

    def core_doubling(seg):
        at, count = SEGMENTS[seg]
        rows = rows_at(at + pipe * (count // 2), count // 2)
        return to_partner(tot.at[rows], tot.at[rows], sum_send.at[seg], sum_recv.at[seg, 9], "core")

    def width_of(seg, k):
        return pl.ds(0, 128 if (seg, k) == (LAST, 1) else COLS)

    def wait_parts(seg, rows, sem):
        units = 3 if seg == LAST else 4
        wait_for(tot.at[pl.ds(0, units * rows), pl.ds(0, 128)], sem)

    def ring_copy(src_rows, src, dst, sems, dim, j):
        position, device = rings[dim]
        return pltpu.make_async_remote_copy(
            src_ref=src.at[src_rows], dst_ref=dst, send_sem=sems[0], recv_sem=sems[1],
            device_id=device(lax.rem(position + j, RING)), device_id_type=MESH,
        )

    def share(base, length, order, steps):
        for dim in order[:steps]:
            length //= RING
            base = base + rings[dim][0] * length
        return base, length

    def share_of(seg, k, steps):
        at, count = SEGMENTS[seg]
        return share(at + pipe * (count // 2) + k * (count // 4), count // 4, ring_orders[k], steps)

    def ring_scatter(seg, s, k):
        base, length = share_of(seg, k, s)
        length //= RING
        dim = ring_orders[k][s]
        position = rings[dim][0]
        sems = (sum_send.at[seg], sum_recv.at[seg, 1 + s])
        cols = width_of(seg, k)
        return [
            ring_copy(
                (rows_at(base + lax.rem(position + j, RING) * length, length), cols), pay,
                sum_in.at[pl.ds(in_at[seg, s, k] + (j - 1) * length, length), cols],
                sems, dim, j,
            )
            for j in (2, 1, 3)
        ]

    def ring_gather(base_length, dim, sems, cols=pl.ds(0, COLS)):
        place = (rows_at(*base_length), cols)
        return [ring_copy(place, tot, tot.at[place], sems, dim, j) for j in (2, 1, 3)]

    def ring_gather_of(seg, t, k):
        sems = (sum_send.at[seg], sum_recv.at[seg, 3 + t])
        return ring_gather(share_of(seg, k, t + 1), ring_orders[k][t], sems, width_of(seg, k))

    def launch_all(seg, copies, rows, narrow=False):
        for copy in copies:
            copy.start()
        sent_rows[seg] += len(copies) * rows * (2 - narrow)

    def ring_advance(seg, stage):
        at, count = SEGMENTS[seg]
        half, quarter = count // 2, count // 4
        if stage == 0:
            launch_all(seg, [core_halving(seg)], half)
        elif stage == 1:
            wait_rows(half, sum_recv.at[seg, 0])
            for k in range(2):
                rows = rows_at(at + pipe * half + k * quarter, quarter)
                came = pl.ds(in_at[seg, "core"] + k * quarter, quarter)
                pay[rows, :] = pay[rows, :] + sum_in[came, :]
                launch_all(seg, ring_scatter(seg, 0, k), quarter // 4, (seg, k) == (LAST, 1))
        elif stage <= 3:
            s = stage - 2
            length = quarter >> 2 * (s + 1)
            wait_parts(seg, 3 * length, sum_recv.at[seg, 1 + s])
            for k in range(2):
                rows = rows_at(*share_of(seg, k, s + 1))
                cols = width_of(seg, k)
                narrow = (seg, k) == (LAST, 1)
                total = wide(pay[rows, cols])
                for j in range(3):
                    total = total + wide(sum_in[pl.ds(in_at[seg, s, k] + j * length, length), cols])
                if s == 0:
                    pay[rows, cols] = total.astype(bf16)
                    launch_all(seg, ring_scatter(seg, 1, k), length // 4, narrow)
                else:
                    tot[rows, cols] = total.astype(bf16)
                    launch_all(seg, ring_gather_of(seg, 1, k), length, narrow)
        elif stage <= 5:
            t = 5 - stage
            length = quarter >> 2 * (t + 1)
            wait_parts(seg, 3 * length, sum_recv.at[seg, 3 + t])
            if t:
                for k in range(2):
                    launch_all(seg, ring_gather_of(seg, 0, k), quarter // 4, (seg, k) == (LAST, 1))
            else:
                launch_all(seg, [core_doubling(seg)], half)
        else:
            wait_rows(half, sum_recv.at[seg, 9])

    def advance(seg, stage):
        if not CUBE[seg]:
            return ring_advance(seg, stage)
        at, count = SEGMENTS[seg]
        half, quarter = count // 2, count // 8
        if stage == 0:
            launch_all(seg, [core_halving(seg)], half)
        elif stage == 1:
            wait_rows(half, sum_recv.at[seg, 0])
            for k in range(4):
                rows = rows_at(at + pipe * half + k * quarter, quarter)
                came = pl.ds(in_at[seg, "core"] + k * quarter, quarter)
                pay[rows, :] = pay[rows, :] + sum_in[came, :]
                launch_all(seg, [halving(seg, 0, k)], quarter // 2)
        elif stage <= 3:
            s = stage - 2
            length = quarter >> (s + 1)
            wait_rows(4 * length, sum_recv.at[seg, 1 + s])
            for k in range(4):
                rows = rows_at(*part_of(seg, k, s + 1))
                pay[rows, :] = pay[rows, :] + sum_in[pl.ds(in_at[seg, s, k], length), :]
                if s == 0:
                    launch_all(seg, [halving(seg, 1, k)], length // 2)
                else:
                    launch_all(seg, last_scatter(seg, k), length // RING)
        elif stage == 4:
            length = quarter // 16
            wait_rows(12 * length, sum_recv.at[seg, 3])
            for k in range(4):
                rows = rows_at(*part_of(seg, k, 3))
                total = wide(pay[rows, :])
                for j in range(3):
                    total = total + wide(sum_in[pl.ds(in_at[seg, 2, k] + j * length, length), :])
                tot[rows, :] = total.astype(bf16)
                launch_all(seg, first_gather(seg, k), length)
        elif stage == 5:
            wait_rows(12 * (quarter // 16), sum_recv.at[seg, 7])
            for k in range(4):
                launch_all(seg, [doubling(seg, 1, k)], quarter // 4)
        elif stage == 6:
            wait_rows(quarter, sum_recv.at[seg, 6])
            for k in range(4):
                launch_all(seg, [doubling(seg, 0, k)], quarter // 2)
            for k in range(4):
                launch_all(seg, [part_to_core(seg, k, 0)], quarter // 2)
        elif stage == 7:
            wait_rows(2 * quarter, sum_recv.at[seg, 5])
            for k in range(4):
                launch_all(seg, [part_to_core(seg, k, 1)], quarter // 2)
        else:
            wait_rows(half, sum_recv.at[seg, 9])

    def point(name):
        for seg, stage in POINTS[name]:
            advance(seg, stage)

    def remote(src, dst, send, recv, j):
        return pltpu.make_async_remote_copy(
            src_ref=src, dst_ref=dst, send_sem=send, recv_sem=recv,
            device_id={"tensor": lax.rem(y + j, RING)}, device_id_type=MESH,
        )

    def rows_of(j):
        return pl.ds(pl.multiple_of(lax.rem(y + j, RING) * OWN, OWN), OWN)

    def scatter(phase):
        for j in (2, 1, 3):
            remote(part.at[phase, rows_of(j)], rs_in.at[phase, j - 1], y_send.at[0], rs_recv.at[phase], j).start()

    def scattered(phase):
        total = wide(part[phase, own_rows, :])
        wait_for(rs_in.at[phase], rs_recv.at[phase])
        for j in range(3):
            total = total + wide(rs_in[phase, j])
        return total

    def gather(phase, full):
        for j in (2, 1, 3):
            remote(full.at[own_rows], full.at[own_rows], y_send.at[1], ag_recv.at[phase], j).start()

    def gathered(phase):
        wait_for(part.at[phase, pl.ds(0, 3 * OWN)], ag_recv.at[phase])

    def exchange(i, put, got):
        for j in (2, 1, 3):
            remote(put.at[lax.rem(y + j, RING)], got.at[j - 1], y_send.at[2 + i], end_recv.at[i], j).start()

    def weight_step(i, step):
        whole = (all_wo, all_out)[i]
        recv = weight_recv.at[4 * i + step]
        send = weight_send.at[i]

        def block(owner, row, count, col, width):
            rows = pl.ds(pl.multiple_of(owner * COLS + row, 16), count)
            return whole.at[rows, pl.ds(pl.multiple_of(col, 256), width)]

        others = [lax.rem(y + j, RING) for j in (2, 1, 3)]
        if step == 3:
            for owner in others:
                ref = block(owner, 0, COLS, 512 * pipe, 512)
                to_partner(ref, ref, send, recv, "core").start()
            return
        for h, (first_dim, then) in enumerate(ring_orders):
            col = 512 * pipe + 256 * h
            first_at, then_at = rings[first_dim][0], rings[then][0]
            if step == 0:
                ref = block(y, 16 * (4 * then_at + first_at), 16, col, 256)
                for j in (2, 1, 3):
                    remote(ref, ref, send, recv, j).start()
                continue
            position, device = rings[(first_dim, then)[step - 1]]
            for owner in others:
                if step == 1:
                    ref = block(owner, 16 * (4 * then_at + first_at), 16, col, 256)
                else:
                    ref = block(owner, 64 * then_at, 64, col, 256)
                for j in (2, 1, 3):
                    pltpu.make_async_remote_copy(
                        src_ref=ref, dst_ref=ref, send_sem=send, recv_sem=recv,
                        device_id=device(lax.rem(position + j, RING)), device_id_type=MESH,
                    ).start()

    def weight_wait(i, step):
        wait_rows((96, 288, 1152, 1536)[step], weight_recv.at[4 * i + step])

    def rows_exchange(put, into, i):
        for j in (2, 1, 3):
            remote(put.at[lax.rem(y + j, RING)], into.at[own_rows], y_send.at[2 + i], end_recv.at[i], j).start()
        into[own_rows, :] = put[y]

    for c in range(2):
        at = AT_LAST + c * HALF_LAST
        pay[at : at + HALF_LAST, :] = jnp.zeros((HALF_LAST, COLS), bf16)

    first, second = lengths[pipe, 0], lengths[pipe, 1]
    both = first + second

    def segment_of(r):
        return (r >= first).astype(jnp.int32) + (r >= both).astype(jnp.int32)

    same_item = segment_of(iota((ROWS, ROWS), 0)) == segment_of(iota((ROWS, ROWS), 1))
    row = iota((ROWS, 128), 0)
    place = row - jnp.where(row >= first, first, 0) - jnp.where(row >= both, second, 0)
    onehot[...] = jnp.where(place == iota((ROWS, 128), 1), 1.0, 0.0).astype(bf16)
    pos[LONGEST:, :] = jnp.zeros((128 - LONGEST, COLS), bf16)

    loads["pw"].wait()
    loads["ve"].wait()
    r, c = iota((4 * HALF, VARS * PATCH), 0), iota((4 * HALF, VARS * PATCH), 1)
    pick = jnp.where((c == PATCH * (r % HALF) + r // HALF) & (r % HALF < VARS), 1.0, 0.0).astype(bf16)
    for v in range(VARS):
        pwf[PATCH * v : PATCH * (v + 1), :] = wide(pw[v])
    terms[: 4 * HALF, :] = mm(pick, pwf[...].astype(bf16)).astype(bf16)
    terms[4 * HALF : 4 * HALF + VARS, :] = ve[...]
    terms[4 * HALF + VARS :, :] = jnp.zeros((TERMS - 4 * HALF - VARS, D), bf16)
    r, c = iota((VARS * PATCH, 4 * HALF), 1), iota((VARS * PATCH, 4 * HALF), 0)
    pick_back = jnp.where((c == PATCH * (r % HALF) + r // HALF) & (r % HALF < VARS), 1.0, 0.0).astype(bf16)
    loads["patches"].wait()
    x3[:, : 4 * HALF] = mm_tn(patches[...], pick_back)
    lane = iota((ROWS, 128), 1)
    x3[:, 4 * HALF :] = jnp.where(lane < VARS, 1.0, 0.0)

    loads["wq"].wait()
    loads["aq"].wait()
    aq_row = as_row(aq_in)
    query = mm(jnp.broadcast_to(aq_row, (8, D)).astype(bf16), wq[...])[0:1, :].astype(bf16)
    query_row[...] = jnp.broadcast_to(wide(query), (8, COLS))
    head_of = iota((8, COLS), 1) // HEAD_DIM
    block = jnp.where(
        head_of == iota((8, COLS), 0) % HEADS, jnp.broadcast_to(wide(query), (8, COLS)), 0.0
    ).astype(bf16)
    loads["wk"].wait()
    key_dir = mm_nt(block, wk[...]) * score_scale
    split = in_two(key_dir[:HEADS, :])
    kdir[...] = jnp.concatenate([wide(split), jnp.zeros((120, D), f32)], axis=0).astype(bf16)
    key_parts = mm_nt(split, terms[...])
    kterms[...] = key_parts + pltpu.roll(key_parts, HEADS, 0)
    loads["wv"].wait()
    vterms[...] = mm(terms[...], wv[...]).astype(bf16)
    pl.semaphore_wait(barrier, len(neighbours))
    loads["wout"].wait()
    weight_step(1, 0)

    def fold(v):
        folded = v[:, :128] + v[:, 128:256] + v[:, 256:]
        return folded + pltpu.roll(folded, HALF, 1)

    def thrice(v):
        return jnp.concatenate([v, v, v], axis=1)

    for h in range(HEADS):
        scores = fold(x3[...] * kterms[h : h + 1, :])
        scores = jnp.where(lane % HALF < VARS, scores, -1e30)
        raised = jnp.exp(scores - jnp.max(scores, axis=-1, keepdims=True))
        weights = raised / (0.5 * jnp.sum(raised, axis=-1, keepdims=True))
        soft[h] = weights
        shares[h * ROWS : (h + 1) * ROWS, :] = (x3[...] * thrice(weights)).astype(bf16)

    col_head = iota((ROWS, COLS), 1) // HEAD_DIM

    def pick_heads(stacked):
        total = jnp.zeros((ROWS, COLS), f32)
        for h in range(HEADS):
            total = jnp.where(col_head == h, stacked[h * ROWS : (h + 1) * ROWS, :], total)
        return total

    def spread_heads(value):
        for h in range(HEADS):
            masked[h * ROWS : (h + 1) * ROWS, :] = jnp.where(col_head == h, value, 0.0).astype(bf16)

    mixed[...] = pick_heads(mm(shares[...], vterms[...])).astype(bf16)
    loads["wo"].wait()
    loads["pos"].wait()
    loads["aggbias"].wait()
    aggbias_row = as_row(aggbias_in)
    for j in range(RING):
        cols = slice(j * COLS, (j + 1) * COLS)
        part[0, :, cols] = mm(mixed[...], all_wo[own_block, cols]).astype(bf16)
    extra = mm(mixed[...], all_wo[own_block, own_cols]) + mm(onehot[...], pos[...]) + aggbias_row
    part[0, :, own_cols] = extra.astype(bf16)
    scatter(0)
    for name in ("gain1", "shift1", "abias", "gain2", "shift2", "dbias", "ubias"):
        loads[name].wait()
    gain1_row, shift1_row = as_row(gain1_in), as_row(shift1_in)
    abias_row, gain2_row, shift2_row = as_row(abias_in), as_row(gain2_in), as_row(shift2_in)
    dbias_row, ubias_row = as_row(dbias_in), as_row(ubias_in)
    dbias_rows[...] = jnp.broadcast_to(dbias_row, (8, D))
    weight_wait(1, 0)
    weight_step(1, 1)
    stream[own_rows, :] = scattered(0).astype(bf16)
    gather(0, stream)
    loads["wqkv"].wait()
    weight_wait(1, 1)
    weight_step(1, 2)
    weight_step(0, 0)
    gathered(0)
    xhat, _ = norm_parts(wide(stream[...]))
    normed[...] = (xhat * gain1_row + shift1_row).astype(bf16)

    for j in range(3):
        qkv[j] = mm(normed[...], wqkv[j]).astype(bf16)
    spread_heads(qkv[0])
    raw = mm_nt(masked[...], qkv[1]) * score_scale
    for h in range(HEADS):
        rows = slice(h * ROWS, (h + 1) * ROWS)
        score = jnp.where(same_item, raw[rows, :], -1e30)
        raised = jnp.exp(score - jnp.max(score, axis=-1, keepdims=True))
        probs[rows, :] = raised / jnp.sum(raised, axis=-1, keepdims=True)
    attended = pick_heads(mm(probs[...].astype(bf16), qkv[2])).astype(bf16)
    att_all[y] = attended
    for j in (2, 1, 3):
        remote(att_all.at[y], att_all.at[y], y_send.at[1], ag_recv.at[1], j).start()
    weight_wait(0, 0)
    weight_step(0, 1)
    weight_wait(1, 2)
    weight_step(1, 3)
    loads["wup"].wait()
    loads["wdown"].wait()
    loads["dy"].wait()
    weight_wait(1, 3)
    gathered(1)
    weight_wait(0, 1)
    weight_step(0, 2)
    for j in range(RING):
        cols = slice(j * COLS, (j + 1) * COLS)
        total = wide(stream[:, cols]) + abias_row[:, cols]
        for i in range(RING):
            total = total + mm(att_all[i], all_out[i * COLS : (i + 1) * COLS, cols])
        resid[:, cols] = total
    xhat, _ = norm_parts(resid[...])
    normed2[...] = (xhat * gain2_row + shift2_row).astype(bf16)

    for j in range(RING):
        cols = slice(j * COLS, (j + 1) * COLS)
        pre = mm(normed2[...], wup[:, cols]) + ubias_row[:, cols]
        half_cdf = 0.5 * (1.0 + lax.erf(pre * root_half))
        active[:, cols] = (pre * half_cdf).astype(bf16)
        slope = half_cdf + pre * jnp.exp(-0.5 * pre * pre) * inv_root_tau
        grad = (mm_nt(dy[...], wdown[cols, :]) * slope).astype(bf16)
        g_pre[:, cols] = grad
        small[8 + j : 9 + j, :] = col_sum(wide(grad))
    for j in range(RING):
        rows = slice(j * COLS, (j + 1) * COLS)
        part[3, :, rows] = mm_nt(g_pre[...], wup[rows, :]).astype(bf16)
    scatter(3)
    for j in range(RING):
        cols = slice(j * COLS, (j + 1) * COLS)
        part[2, :, cols] = mm(active[...], wdown[:, cols]).astype(bf16)
    for j in (2, 1, 3):
        cols = pl.ds(pl.multiple_of(lax.rem(y + j, RING) * COLS, COLS), COLS)
        remote(part.at[2, :, cols], block_in.at[j - 1], y_send.at[2], end_recv.at[0], j).start()
    for j in range(RING):
        cols = slice(j * COLS, (j + 1) * COLS)
        pay[AT_DOWN + j * D : AT_DOWN + (j + 1) * D, :] = mm_tn(active[...], dy[:, cols]).astype(bf16)
    advance(0, 0)
    for j in range(RING):
        cols = slice(j * COLS, (j + 1) * COLS)
        pay[AT_UP + j * D : AT_UP + (j + 1) * D, :] = mm_tn(normed2[...], g_pre[:, cols]).astype(bf16)
    advance(1, 0)
    weight_wait(0, 2)
    weight_step(0, 3)
    point("up")
    e2 = scattered(3)
    xhat2, inv2 = norm_parts(resid[own_rows, :])
    g_resid_own = (wide(dy[own_rows, :]) + norm_back(e2, xhat2, inv2, gain2_row)).astype(bf16)
    g_resid[own_rows, :] = g_resid_own
    for j in range(RING):
        put_rows[0, j] = mm_nt(g_resid_own, all_out[j * COLS : (j + 1) * COLS, :]).astype(bf16)
    rows_exchange(put_rows.at[0], g_att, 5)
    gather(2, g_resid)
    point("e2")
    gain2, shift2 = col_sum(e2 * xhat2), col_sum(e2)
    wait_for(block_in, end_recv.at[0])
    result = resid[:, own_cols] + wide(part[2, :, own_cols]) + dbias_rows[0:1, own_cols]
    got_block[...] = (result + wide(block_in[0]) + wide(block_in[1]) + wide(block_in[2])).astype(bf16)
    point("block")
    wait_rows(3 * OWN, end_recv.at[5])

    spread_heads(g_att[...])
    g_probs = mm_nt(masked[...], qkv[2])
    g_v = mm_tn(probs[...].astype(bf16), masked[...]).astype(bf16)
    p = probs[...]
    g_scores = (p * (g_probs - jnp.sum(p * g_probs, axis=-1, keepdims=True))).astype(bf16)
    g_q = (pick_heads(mm(g_scores, qkv[1])) * score_scale).astype(bf16)
    spread_heads(qkv[0])
    g_k = (mm_tn(g_scores, masked[...]) * score_scale).astype(bf16)
    for j in range(RING):
        rows = slice(j * COLS, (j + 1) * COLS)
        total = mm_nt(g_q, wqkv[0, rows, :]) + mm_nt(g_k, wqkv[1, rows, :])
        part[4, :, rows] = (total + mm_nt(g_v, wqkv[2, rows, :])).astype(bf16)
    scatter(4)
    point("attn")
    for j, g in enumerate((g_q, g_k, g_v)):
        pay[AT_QKV + j * D : AT_QKV + (j + 1) * D, :] = mm_tn(normed[...], g).astype(bf16)
    gathered(2)
    attended_own = att_all[y]
    for j in range(RING):
        cols = slice(j * COLS, (j + 1) * COLS)
        pay[AT_OUT + j * COLS : AT_OUT + (j + 1) * COLS, :] = mm_tn(
            attended_own, g_resid[:, cols]
        ).astype(bf16)
    advance(2, 0)
    point("out")
    e1 = scattered(4)
    xhat1, inv1 = norm_parts(wide(stream[own_rows, :]))
    g_stream_own = (
        wide(g_resid[own_rows, :]) + norm_back(e1, xhat1, inv1, gain1_row)
    ).astype(bf16)
    g_stream[own_rows, :] = g_stream_own
    weight_wait(0, 3)
    for j in range(RING):
        put_rows[1, j] = mm_nt(g_stream_own, all_wo[j * COLS : (j + 1) * COLS, :]).astype(bf16)
    rows_exchange(put_rows.at[1], g_mixed, 6)
    gather(3, g_stream)
    gain1, shift1 = col_sum(e1 * xhat1), col_sum(e1)
    for j in range(RING):
        cols = slice(j * COLS, (j + 1) * COLS)
        for i, v in enumerate((gain1, shift1, gain2, shift2)):
            put_gain[j, i : i + 1, :] = v[:, cols]
        put_gain[j, 4:8, :] = jnp.zeros((4, COLS), f32)
    exchange(1, put_gain, got_gain)
    point("e1")
    wait_rows(3 * OWN, end_recv.at[6])

    spread_heads(g_mixed[...])
    by_term = mm_nt(masked[...], vterms[...])
    grad_patch = jnp.zeros((ROWS, 4 * HALF), f32)
    for h in range(HEADS):
        mine = by_term[h * ROWS : (h + 1) * ROWS, :]
        weights = soft[h]
        g_weights = fold(x3[...] * mine)
        g_sc = weights * (
            g_weights - 0.5 * jnp.sum(weights * g_weights, axis=-1, keepdims=True)
        )
        g_sc2 = jnp.concatenate([g_sc, g_sc], axis=1)
        w2 = jnp.concatenate([weights, weights], axis=1)
        grad_patch = grad_patch + g_sc2 * kterms[h : h + 1, : 4 * HALF] + w2 * mine[:, : 4 * HALF]
        sums = col_sum(x3[...] * thrice(g_sc))
        score_sum[h : h + 1, :] = sums
    value_sum = mm_tn(shares[...], masked[...]).astype(bf16)
    pay[AT_LAST : AT_LAST + 256, :] = value_sum[:256, :]
    pay[AT_LAST + HALF_LAST : AT_LAST + HALF_LAST + 128, :] = value_sum[256:, :]
    head_cols = iota((HEADS, COLS), 1)
    spot = jnp.where((head_cols % HEADS == iota((HEADS, COLS), 0)) & (head_cols < 8), 1.0, 0.0).astype(bf16)
    across = mm_tn(score_sum[...].astype(bf16), spot).astype(bf16)
    for n in range(TERMS // 16):
        at = score_place(n)
        pay[at : at + 16, :] = across[16 * n : 16 * (n + 1), :]
    gathered(3)
    g_own = g_stream[:, own_cols]
    pay[AT_POS : AT_POS + LONGEST, :] = mm_tn(onehot[...], g_own)[:LONGEST, :].astype(bf16)
    advance(4, 0)
    point("last")
    for j in range(RING):
        cols = slice(j * COLS, (j + 1) * COLS)
        pay[AT_WO + j * COLS : AT_WO + (j + 1) * COLS, :] = mm_tn(
            mixed[...], g_stream[:, cols]
        ).astype(bf16)
    advance(3, 0)
    point("wo")
    along = mm(in_two(score_sum[...]), terms[...])
    along = in_two(along[:HEADS] + along[HEADS:])
    head_of = iota((8, COLS), 1) // HEAD_DIM
    g_query = col_sum(jnp.where(head_of == iota((8, COLS), 0) % HEADS, mm(along, wk[...]), 0.0)) * score_scale
    both_parts = mm_nt(in_two(jnp.broadcast_to(g_query, (HEADS, COLS))), wq[...])
    g_aq = both_parts[0:1, :] + both_parts[HEADS : HEADS + 1, :]
    for j in range(RING):
        put_aq[j] = jnp.broadcast_to(g_aq[:, j * COLS : (j + 1) * COLS], (8, COLS))
    exchange(3, put_aq, got_aq)
    low_patch = grad_patch.astype(bf16)
    width = VARS * PATCH // RING
    r, c = iota((width, 4 * HALF), 1), iota((width, 4 * HALF), 0)
    for j in range(RING):
        pick_own = jnp.where(
            (c + width * j == PATCH * (r % HALF) + r // HALF) & (r % HALF < VARS), 1.0, 0.0
        ).astype(bf16)
        put_patch[j] = mm_nt(pick_own, low_patch).astype(bf16)
    exchange(2, put_patch, got_patch)
    small[0:1, :] = col_sum(wide(g_own))
    small[5:6, :] = col_sum(wide(g_resid[:, own_cols]))
    small[6:7, :] = col_sum(wide(dy[:, own_cols]))
    small[12:16, :] = jnp.zeros((4, COLS), f32)
    wait_for(got_gain, end_recv.at[1])
    small[1:5, :] = (put_gain[y] + got_gain[0] + got_gain[1] + got_gain[2])[0:4, :]

    def vector_step(i):
        if i == 0:
            wait_for(got_aq, end_recv.at[3])
            small[7:8, :] = (put_aq[y] + got_aq[0] + got_aq[1] + got_aq[2])[0:1, :]
            rd_out[0] = small[...]
            to_partner(rd_out.at[0], rd_in.at[0], other_send.at[0], rd_recv.at[0], "core").start()
            return
        at, n = (0, 1) if i == 1 else (3 * i - 5, 3)
        wait_for(rd_in.at[pl.ds(at, n)], rd_recv.at[i - 1])
        value = rd_out[i - 1]
        for j in range(n):
            value = value + rd_in[at + j]
        if i == 3:
            total_small[...] = value
            return
        rd_out[i] = value
        position, device = rings["xz"[i - 1]]
        for j in (2, 1, 3):
            pltpu.make_async_remote_copy(
                src_ref=rd_out.at[i], dst_ref=rd_in.at[3 * i - 3 + j], send_sem=other_send.at[0],
                recv_sem=rd_recv.at[i], device_id=device(lax.rem(position + j, RING)), device_id_type=MESH,
            ).start()

    terms_base = AT_TERMS + pipe * 256

    def terms_gather(t):
        dim = ring_orders[0][t]
        for copy in ring_gather(
            share(terms_base, 256, ring_orders[0], t + 1), dim, (other_send.at[1], extra_recv.at[t])
        ):
            copy.start()

    def terms_step(i):
        if i == 0:
            value_rows = tot[rows_at(*share_of(LAST, 0, 2)), :]
            score_rows = tot[rows_at(*share_of(LAST, 1, 2)), pl.ds(0, 128)]
            total = mm_nt(value_rows, wv[...]) + mm(score_rows, kdir[...])
            for j in range(RING):
                put_terms[j] = total[:, j * COLS : (j + 1) * COLS].astype(bf16)
            exchange(4, put_terms, got_terms)
        elif i == 1:
            wait_for(got_terms, end_recv.at[4])
            total = wide(put_terms[y]) + wide(got_terms[0]) + wide(got_terms[1]) + wide(got_terms[2])
            tot[rows_at(*share(terms_base, 256, ring_orders[0], 2)), :] = total.astype(bf16)
            terms_gather(1)
        elif i == 2:
            wait_rows(48, extra_recv.at[1])
            terms_gather(0)
        elif i == 3:
            wait_rows(192, extra_recv.at[0])
            rows = rows_at(terms_base, 256)
            to_partner(tot.at[rows], tot.at[rows], other_send.at[1], extra_recv.at[2], "core").start()
        else:
            wait_rows(256, extra_recv.at[2])

    next_of = {"t": 0, "v": 0}
    for step in TAIL:
        if step == "t":
            terms_step(next_of["t"])
            next_of["t"] += 1
        elif step == "v":
            vector_step(next_of["v"])
            next_of["v"] += 1
        else:
            advance(*step)
    assert next_of == {"t": 5, "v": 4}
    wait_for(got_patch, end_recv.at[2])
    patch_sum[...] = (
        wide(put_patch[y]) + wide(got_patch[0]) + wide(got_patch[1]) + wide(got_patch[2])
    )
    for seg in range(len(SEGMENTS)):
        if seg == LAST:
            wait_for(tot.at[pl.ds(0, sent_rows[seg]), pl.ds(0, 128)], sum_send.at[seg])
        else:
            wait_rows(sent_rows[seg] // 2, sum_send.at[seg])
    wait_for(rs_in.at[pl.ds(0, 3)], y_send.at[0])
    wait_for(terms, y_send.at[1])
    wait_for(block_in, y_send.at[2])
    for i in (5, 6):
        wait_rows(3 * OWN, y_send.at[2 + i])
    for i in range(2):
        wait_rows(96 + 288 + 1152 + 1536, weight_send.at[i])
    for i, got in ((1, got_gain), (2, got_patch), (3, got_aq), (4, got_terms)):
        wait_for(got, y_send.at[2 + i])
    wait_for(rd_in, other_send.at[0])
    wait_rows(3 * 16 + 3 * 64 + 256, other_send.at[1])


MAIN_VMEM = 50 * 1024 * 1024
FINISH_VMEM = 50 * 1024 * 1024


def run_chain(lengths, *args):
    hbm = pl.BlockSpec(memory_space=pl.ANY)
    V = pltpu.VMEM
    low = lambda *s: V(s, bf16)
    full = lambda *s: V(s, f32)
    kept = [w for name, w in zip(WEIGHTS, args) if name not in ("wo", "wout")]
    scratch = [low(*w.shape) if w.shape[0] != LONGEST else low(128, COLS) for w in kept]
    scratch += [low(D, D), low(D, D)]
    scratch += [
        full(VARS * PATCH, D), low(HEADS * ROWS, TERMS), low(TERMS, COLS), full(8, TERMS),
        low(128, D), full(HEADS, ROWS, 128), full(ROWS, TERMS), low(ROWS, 128),
        low(5, ROWS, D), low(5, 3, OWN, D), low(ROWS, D), low(ROWS, D), full(ROWS, D),
        low(ROWS, D), low(ROWS, D), low(ROWS, D), full(8, D), low(3, ROWS, COLS),
        low(2, RING, OWN, COLS), low(ROWS, COLS), low(ROWS, COLS),
        low(ROWS, COLS), low(3, ROWS, COLS), full(HEADS * ROWS, ROWS), low(RING, ROWS, COLS),
        low(ROWS, D), low(ROWS, D), low(HEADS * ROWS, COLS),
        low(3, 48, ROWS), low(RING, 48, ROWS),
        full(3, 8, COLS), full(RING, 8, COLS), full(SMALL, COLS), full(HEADS, TERMS),
        full(3, 8, COLS), full(RING, 8, COLS), low(3, 16, COLS), low(RING, 16, COLS),
        full(3, SMALL, COLS), full(7, SMALL, COLS),
        low(PAY, COLS), low(PAY * 31 // 32, COLS),
    ]
    dma = pltpu.SemaphoreType.DMA
    scratch += [
        dma((len(args),)), dma((9,)), dma((5,)), dma((4,)), dma((7,)), dma((5,)), dma((5, 10)), dma((3,)),
        dma((3,)), dma((2,)), dma((8,)), dma((2,)),
    ]
    return pl.pallas_call(
        chain,
        out_shape=(
            low(ROWS, COLS), full(48, ROWS), low(ALL, COLS), low(TERMS, D), full(SMALL, COLS), full(8, COLS),
        ),
        in_specs=[pl.BlockSpec(memory_space=pltpu.SMEM)] + [hbm] * len(args),
        out_specs=[pl.BlockSpec(memory_space=pltpu.VMEM)] * 6,
        scratch_shapes=scratch,
        compiler_params=pltpu.CompilerParams(
            collective_id=0, has_side_effects=True, vmem_limit_bytes=MAIN_VMEM
        ),
    )(lengths, *[pltpu.with_memory_space_constraint(a, pltpu.HBM) for a in args])


VECTORS = (0, 7, 1, 2, 5, 3, 4, 6)


def finish(
    tot, block_in, patch_in, terms, small, query, aq_from, hk,
    o_block, o_patch, o_down, o_up, o_out, o_qkv, o_wo, o_wv, o_wk, o_wq,
    o_pw, o_ve, o_pos, *rest,
):
    o_vectors, o_upbias = rest[:8], rest[8]
    (
        wk, aq_in, down, up, out, qkv, wo, gv, gk, gq, gpw, gve, gpos, vectors, gub, load_sem, save_sem,
    ) = rest[9:]
    loads = [
        pltpu.make_async_copy(hk, wk, load_sem.at[0]), pltpu.make_async_copy(aq_from, aq_in, load_sem.at[1])
    ]
    for copy in loads:
        copy.start()
    saves = []

    def store(src, dst):
        copy = pltpu.make_async_copy(src, dst, save_sem.at[len(saves)])
        copy.start()
        saves.append(copy)

    def blocks(dst, at, count, first, rows):
        for j in range(RING):
            start = at + j * count + first
            dst[first : first + rows, j * COLS : (j + 1) * COLS] = wide(tot[start : start + rows, :])

    for first in (0, D // 2):
        blocks(down, AT_DOWN, D, first, D // 2)
        half = pl.ds(first, D // 2)
        store(down.at[half], o_down.at[half])
    blocks(up, AT_UP, D, 0, D)
    store(up, o_up)
    for j in range(3):
        qkv[j] = wide(tot[AT_QKV + j * D : AT_QKV + (j + 1) * D, :])
    store(qkv, o_qkv)
    value_sum = jnp.concatenate(
        [tot[AT_LAST : AT_LAST + 256, :], tot[AT_LAST + HALF_LAST : AT_LAST + HALF_LAST + 128, :]], axis=0
    )
    gv[...] = mm_tn(terms[...], value_sum)
    store(gv, o_wv)
    across = jnp.concatenate(
        [tot[score_place(n) : score_place(n) + 16, :128] for n in range(TERMS // 16)], axis=0
    )
    along = in_two(mm_tn(across, terms[...])[:HEADS, :])
    head_of = iota((8, COLS), 1) // HEAD_DIM
    mine = head_of == iota((8, COLS), 0) % HEADS
    block = jnp.where(mine, query[...], 0.0).astype(bf16)
    gk[...] = mm_tn(along, block) * score_scale
    store(gk, o_wk)
    for copy in loads:
        copy.wait()
    g_query = col_sum(jnp.where(mine, mm(along, wk[...]), 0.0)) * score_scale
    row = iota((8, D), 0)
    aq = jnp.where(row < 2, jnp.broadcast_to(as_row(aq_in), (8, D)), 0.0).astype(bf16)
    high = wide(g_query.astype(bf16))
    both = jnp.where(
        iota((8, COLS), 0) == 0,
        jnp.broadcast_to(high, (8, COLS)), jnp.broadcast_to(g_query - high, (8, COLS)),
    ).astype(bf16)
    gq[...] = mm_tn(aq, both)
    store(gq, o_wq)
    for p in range(PATCH):
        gpw[:, p, :] = wide(tot[AT_TERMS + HALF * p : AT_TERMS + HALF * p + VARS, :])
    store(gpw, o_pw)
    gve[...] = wide(tot[AT_TERMS + 4 * HALF : AT_TERMS + 4 * HALF + VARS, :])
    store(gve, o_ve)
    gpos[...] = wide(tot[AT_POS : AT_POS + LONGEST, :])
    store(gpos, o_pos)
    for n, (ref, i) in enumerate(zip(o_vectors, VECTORS)):
        vectors[n, 0:1, :] = small[i : i + 1, :128]
        vectors[n, 1:2, :] = small[i : i + 1, 128:]
        store(vectors.at[n], ref)
    for j in range(RING):
        gub[2 * j : 2 * j + 1, :] = small[8 + j : 9 + j, :128]
        gub[2 * j + 1 : 2 * j + 2, :] = small[8 + j : 9 + j, 128:]
    store(gub, o_upbias)
    store(block_in, o_block)
    store(patch_in, o_patch)
    blocks(out, AT_OUT, COLS, 0, COLS)
    store(out, o_out)
    blocks(wo, AT_WO, COLS, 0, COLS)
    store(wo, o_wo)
    for copy in saves:
        copy.wait()


def run_finish(*args):
    vmem = pl.BlockSpec(memory_space=pltpu.VMEM)
    hbm = pl.BlockSpec(memory_space=pl.ANY)
    full = lambda *s: pltpu.VMEM(s, f32)
    shape = lambda *s: jax.ShapeDtypeStruct(s, f32)
    big = [(D, D), (D, D), (COLS, D), (3, D, COLS), (COLS, D), (D, COLS), (D, COLS), (D, COLS)]
    return pl.pallas_call(
        finish,
        out_shape=[jax.ShapeDtypeStruct((ROWS, COLS), bf16), shape(48, ROWS)]
        + [shape(*s) for s in big]
        + [shape(VARS, PATCH, COLS), shape(VARS, COLS), shape(LONGEST, COLS)]
        + [shape(2, 128)] * 8 + [shape(8, 128)],
        in_specs=[vmem] * 6 + [hbm] * 2,
        out_specs=[hbm] * 22,
        scratch_shapes=[
            pltpu.VMEM((D, COLS), bf16), pltpu.VMEM((8, 128), bf16),
            full(D, D), full(D, D), full(COLS, D), full(3, D, COLS), full(COLS, D),
            full(D, COLS), full(D, COLS), full(D, COLS),
            full(VARS, PATCH, COLS), full(VARS, COLS), full(LONGEST, COLS), full(8, 2, 128), full(8, 128),
            pltpu.SemaphoreType.DMA((2,)), pltpu.SemaphoreType.DMA((23,)),
        ],
        compiler_params=pltpu.CompilerParams(vmem_limit_bytes=FINISH_VMEM),
    )(*[pltpu.with_memory_space_constraint(a, pltpu.VMEM if i < 6 else pltpu.HBM) for i, a in enumerate(args)])


def shards(
    patches, item_lengths, cotangent, patch_weight, var_embed, agg_query, agg_wq, agg_wk, agg_wv,
    agg_wo, agg_bias, pos_table, first_gain, first_shift, attn_qkv, attn_out, attn_bias,
    second_gain, second_shift, mlp_up, up_bias, mlp_down, down_bias,
):
    tiled = lambda v: v.reshape(v.shape[0] // 128, 128)
    block, patch, summed, terms, small, query = run_chain(
        item_lengths, patches.T, patch_weight, var_embed, tiled(agg_query), tiled(first_gain),
        tiled(first_shift), tiled(attn_bias), tiled(second_gain), tiled(second_shift),
        tiled(down_bias), tiled(up_bias), tiled(agg_bias),
        agg_wq, agg_wk, agg_wv, agg_wo, pos_table, attn_qkv.transpose(1, 0, 2), attn_out,
        mlp_up, mlp_down, cotangent,
    )
    (
        block, patch, g_down, g_up, g_out, g_qkv, g_wo, g_wv, g_wk, g_wq, g_pw, g_ve, g_pos,
        g_agg_bias, g_aq, g_gain1, g_shift1, g_attn_bias, g_gain2, g_shift2, g_down_bias, g_up_bias,
    ) = run_finish(summed, block, patch, terms, small, query, tiled(agg_query), agg_wk)
    flat = lambda v: v.reshape(-1)
    return (
        block, patch.T, g_pw, g_ve, flat(g_aq), g_wq, g_wk, g_wv, g_wo, flat(g_agg_bias), g_pos,
        flat(g_gain1), flat(g_shift1), g_qkv.transpose(1, 0, 2), g_out, flat(g_attn_bias),
        flat(g_gain2), flat(g_shift2), g_up, flat(g_up_bias), g_down, flat(g_down_bias),
    )


def solution(mesh):
    rows = P(("dp", "pipe"), None)
    cols = P(None, "tensor")
    split = P("tensor", None)
    part = P("tensor")
    both = P(("dp", "pipe"), "tensor")
    last = P(None, None, "tensor")
    return jax.shard_map(
        shards,
        mesh=mesh,
        in_specs=(
            rows, P("dp", None), rows, P(), P(), P(), cols, cols, cols, split, part, cols, P(), P(),
            last, split, P(), P(), P(), cols, part, split, P(),
        ),
        out_specs=(
            both, both, last, cols, part, cols, cols, cols, split, part, cols, part, part, last,
            split, part, part, part, cols, part, split, part,
        ),
        check_vma=False,
    )
```
